32 devices in a mesh: seq: 4 (over x, core), shard: 8 (over z, y).
Axes of the slice: x: 2, y: 2, z: 4, core: 2. Of those that a mesh axis runs over, the one named last changes fastest.
Arguments:
- tokens: bfloat16 [8, 1536, 768], P('shard', 'seq'), may hold values from -8 to 8
- route_residual: float32 [8, 1536, 8], P('shard', 'seq'), may hold values from -3 to 3
- doc_lengths: int32 [8, 8], P('shard'), may hold values from 1 to 1153, 1536 in all within a row
- routes: int32 [8, 1536, 2], P('shard', 'seq'), may hold values from 0 to 7, all different within a row
- priority: int32 [8, 1536], P('shard', 'seq'), may hold values from 0 to 1535, each once within a row
- grad_out: bfloat16 [8, 1536, 768], P('shard', 'seq'), may hold values from -6 to 6
- attend_in: float32 [3, 768, 768], P(None, 'shard'), may hold values from -0.21875 to 0.21875
- attend_in_first: float32 [3, 768, 768], P(None, 'shard'), may hold values from -640 to 640
- attend_in_second: float32 [3, 768, 768], P(None, 'shard'), may hold values from 12288 to 49152
- attend_out: float32 [768, 768], P('shard'), may hold values from -0.75 to 0.75
- attend_out_first: float32 [768, 768], P('shard'), may hold values from -128 to 128
- attend_out_second: float32 [768, 768], P('shard'), may hold values from 491.52 to 1966.08
- expert_up: float32 [4, 768, 4096], P(None, 'shard'), may hold values from -0.21875 to 0.21875
- expert_up_first: float32 [4, 768, 4096], P(None, 'shard'), may hold values from -64 to 64
- expert_up_second: float32 [4, 768, 4096], P(None, 'shard'), may hold values from 122.88 to 491.52
- expert_down: float32 [4, 2048, 768], P(None, 'shard'), may hold values from -0.125 to 0.125
- expert_down_first: float32 [4, 2048, 768], P(None, 'shard'), may hold values from -96 to 96
- expert_down_second: float32 [4, 2048, 768], P(None, 'shard'), may hold values from 276.48 to 1105.92
- router_mix: float32 [768, 12], P('shard'), may hold values from -0.109375 to 0.109375
- router_mix_first: float32 [768, 12], P('shard'), may hold values from -2048 to 2048
- router_mix_second: float32 [768, 12], P('shard'), may hold values from 110592 to 442368
- vectors: float32 [4, 768], P(None, 'shard'), may hold values from 0.5 to 1.5
- vectors_first: float32 [4, 768], P(None, 'shard'), may hold values from -640 to 640
- vectors_second: float32 [4, 768], P(None, 'shard'), may hold values from 12288 to 49152
Outputs:
- layer_out: bfloat16 [8, 1536, 768], P('shard', 'seq')
- grad_tokens: float32 [8, 1536, 768], P('shard', 'seq')
- grad_route_residual: float32 [8, 1536, 8], P('shard', 'seq')
- attend_in_new: float32 [3, 768, 768], P(None, 'shard')
- attend_in_first_new: float32 [3, 768, 768], P(None, 'shard')
- attend_in_second_new: float32 [3, 768, 768], P(None, 'shard')
- attend_out_new: float32 [768, 768], P('shard')
- attend_out_first_new: float32 [768, 768], P('shard')
- attend_out_second_new: float32 [768, 768], P('shard')
- expert_up_new: float32 [4, 768, 4096], P(None, 'shard')
- expert_up_first_new: float32 [4, 768, 4096], P(None, 'shard')
- expert_up_second_new: float32 [4, 768, 4096], P(None, 'shard')
- expert_down_new: float32 [4, 2048, 768], P(None, 'shard')
- expert_down_first_new: float32 [4, 2048, 768], P(None, 'shard')
- expert_down_second_new: float32 [4, 2048, 768], P(None, 'shard')
- router_mix_new: float32 [768, 12], P('shard')
- router_mix_first_new: float32 [768, 12], P('shard')
- router_mix_second_new: float32 [768, 12], P('shard')
- vectors_new: float32 [4, 768], P(None, 'shard')
- vectors_first_new: float32 [4, 768], P(None, 'shard')
- vectors_second_new: float32 [4, 768], P(None, 'shard')
The draws below stay inside these ranges and needn't reach their ends.
Inputs may be any that keep to these rules, and one draw needn't show every extreme that they name: `doc_lengths`: each stream's lengths sum to 1536; the longest is exactly 1153. `routes`: a token's two experts differ. `priority`: each stream's row is a permutation.
All inputs are finite; a program needn't handle non-finite values.
Results may differ from the reference program's by a relative error of at most 0.012.
Values may be sent and summed in bfloat16 or wider, within the bound.
A program may use at most 192 MiB of HBM per device.

```python
import math
from functools import partial
import jax
import jax.numpy as jnp
import numpy as np
from jax import lax

D = 768
HEADS = 12
HEAD_DIM = 64
FF = 2048
NFFN = 4
NEXP = 8
TOPK = 2
NDOC = 8
STEP = 5
TOK_DEV = 384
SEQ_LEN = 1536
GROUPS = 8
TOKENS = 12288
CAP = 96


def raised(values, stream_key, source, target, parts, factor):
    def block_of(axis_at):
        return (jnp.arange(values.shape[axis_at]) // (values.shape[axis_at] // parts)).reshape((-1,) + (1,) * (values.ndim - 1 - axis_at))

    one_side = jax.random.permutation(stream_key, parts)[block_of(target)]
    far = (block_of(target) + parts // 2) % parts
    return jnp.where((block_of(source) == one_side) | (block_of(source) == far), factor * values, values)


def block_levels(own_key, shape, pieces, smallest, top_value):
    def one(axis_at, blocks):
        draws = jax.random.uniform(jax.random.fold_in(jax.random.fold_in(own_key, 6), axis_at), (blocks,), jnp.float32, smallest / len(pieces), top_value / len(pieces))
        return jnp.repeat(jnp.exp(draws), shape[axis_at] // blocks).reshape((-1,) + (1,) * (len(shape) - axis_at - 1))

    gain = one(*pieces[0])
    for cut in pieces[1:]:
        gain = gain * one(*cut)
    return gain


def distinct(stream_key, rows, amount, top, lift):
    order = jax.random.permutation(jax.random.fold_in(stream_key, 1), amount)
    boost = order
    for power in range(3):
        boost = boost * boost // amount
    boost = boost * lift // amount
    tickets = jax.random.randint(jax.random.fold_in(stream_key, 2), (rows, amount), 0, 4096) + boost
    fixed_rows = jax.random.permutation(jax.random.fold_in(stream_key, 3), rows)[jnp.arange(amount) % rows]
    tickets = jnp.where(jnp.arange(rows)[:, None] == fixed_rows[None, :], 1 << 14, tickets)
    merit = tickets * amount + jnp.arange(amount)
    return lax.top_k(merit.astype(jnp.int32), top)[1].astype(jnp.int32)


def length_profile(amount, total, most, lean):
    loads = [(1 << 20) // math.isqrt(grade ** lean) + 1 for grade in range(2, amount + 1)]
    rest, holding = total - most - (amount - 1), [1] * (amount - 1)
    while rest > 0:
        candidates = [i for i in range(amount - 1) if holding[i] < most]
        whole, left = sum([loads[i] for i in candidates]), rest
        for i in candidates:
            addition = min(most - holding[i], max(1, left * loads[i] // whole), rest)
            holding[i] = holding[i] + addition
            rest = rest - addition
    return np.array([most] + holding)


def ragged_sizes(stream_key, count, total, limit, slope):
    if count == 2:
        one = jax.random.randint(stream_key, (), max(1, total - limit), min(limit, total - 1) + 1)
        return jnp.stack([one, total - one])
    sizes = jnp.asarray(length_profile(count, total, limit, slope), jnp.int32)
    twos = (count - 1) // 2
    donor, taker = sizes[1:1 + 2 * twos:2], sizes[2:2 + 2 * twos:2]
    slack = jnp.minimum(donor - 1, limit - taker)
    shifted = jax.random.randint(jax.random.fold_in(stream_key, 1), (twos,), 0, 1 << 20) % (slack + 1)
    sizes = sizes.at[1:1 + 2 * twos:2].set(donor - shifted).at[2:2 + 2 * twos:2].set(taker + shifted)
    return sizes[jax.random.permutation(jax.random.fold_in(stream_key, 2), count)]


def gaussian(rng, shape, spread, most, split=(), held_as=jnp.bfloat16):
    array = spread * jax.random.normal(rng, shape, jnp.float32)
    if split:
        array = array * block_levels(rng, shape, split, -0.22, 0.18)
    return jnp.clip(array, -most, most).astype(held_as)


def gaussian_with(stream_key, shape, deviation, limit, pieces, heavy, kind=jnp.bfloat16):
    entries = deviation * jax.random.normal(stream_key, shape, jnp.float32)
    if pieces:
        entries = entries * block_levels(stream_key, shape, pieces, -0.22, 0.18)
    return jnp.clip(raised(entries, jax.random.fold_in(stream_key, 3), *heavy), -limit, limit).astype(kind)


def setup_inputs(seed: int = 0) -> dict:
    arg_keys = jax.random.split(jax.random.key(seed), 25)
    tokens = gaussian_with(arg_keys[0], (GROUPS, SEQ_LEN, D), 1.0, 8.0, ((0, 8), (1, 4)), (0, 2, 8, 2.0))
    route_residual = gaussian(arg_keys[1], (GROUPS, SEQ_LEN, NEXP), 0.5, 3.0, ((0, 8), (1, 4)), jnp.float32)
    doc_lengths = jax.vmap(lambda own: ragged_sizes(own, NDOC, SEQ_LEN, 3 * TOK_DEV + 1, 2))(jax.random.split(arg_keys[2], GROUPS)).reshape((GROUPS, NDOC)).astype(jnp.int32)
    routes = distinct(arg_keys[3], GROUPS * SEQ_LEN, NEXP, TOPK, 2048).reshape((GROUPS, SEQ_LEN, TOPK))
    priority = jax.vmap(lambda own: jax.random.permutation(own, SEQ_LEN))(jax.random.split(arg_keys[4], GROUPS)).reshape((GROUPS, SEQ_LEN)).astype(jnp.int32)
    grad_out = gaussian(arg_keys[5], (GROUPS, SEQ_LEN, D), 1.0, 6.0, ((0, 8), (1, 4)))
    attend_in = gaussian(arg_keys[6], (3, D, D), D ** -0.5, 0.21875, ((1, 8),), jnp.float32)
    attend_in_first = gaussian(arg_keys[7], (3, D, D), (TOKENS ** 0.5), 640.0, ((1, 8),), jnp.float32)
    attend_in_second = jnp.clip(jnp.exp(math.log(49152.0) - 1.3862944 * jax.random.uniform(arg_keys[8], (3, D, D), jnp.float32) ** block_levels(arg_keys[8], (3, D, D), ((1, 8),), -0.2, 0.2)), 12288.0, 49152.0)
    attend_out = gaussian(arg_keys[9], (D, D), HEAD_DIM ** -0.5, 0.75, ((0, 8),), jnp.float32)
    attend_out_first = gaussian(arg_keys[10], (D, D), (0.2 * TOKENS ** 0.5), 128.0, ((0, 8),), jnp.float32)
    attend_out_second = jnp.clip(jnp.exp(math.log(1966.08) - 1.3862944 * jax.random.uniform(arg_keys[11], (D, D), jnp.float32) ** block_levels(arg_keys[11], (D, D), ((0, 8),), -0.2, 0.2)), 491.52, 1966.08)
    expert_up = gaussian(arg_keys[12], (NFFN, D, 2 * FF), D ** -0.5, 0.21875, ((1, 8),), jnp.float32)
    expert_up_first = gaussian(arg_keys[13], (NFFN, D, 2 * FF), (0.1 * TOKENS ** 0.5), 64.0, ((1, 8),), jnp.float32)
    expert_up_second = jnp.clip(jnp.exp(math.log(491.52) - 1.3862944 * jax.random.uniform(arg_keys[14], (NFFN, D, 2 * FF), jnp.float32) ** block_levels(arg_keys[14], (NFFN, D, 2 * FF), ((1, 8),), -0.2, 0.2)), 122.88, 491.52)
    expert_down = gaussian(arg_keys[15], (NFFN, FF, D), FF ** -0.5, 0.125, ((1, 8),), jnp.float32)
    expert_down_first = gaussian(arg_keys[16], (NFFN, FF, D), (0.15 * TOKENS ** 0.5), 96.0, ((1, 8),), jnp.float32)
    expert_down_second = jnp.clip(jnp.exp(math.log(1105.92) - 1.3862944 * jax.random.uniform(arg_keys[17], (NFFN, FF, D), jnp.float32) ** block_levels(arg_keys[17], (NFFN, FF, D), ((1, 8),), -0.2, 0.2)), 276.48, 1105.92)
    router_mix = gaussian(arg_keys[18], (D, NEXP + 4), (4 * D) ** -0.5, 0.109375, ((0, 8),), jnp.float32)
    router_mix_first = gaussian(arg_keys[19], (D, NEXP + 4), (3.0 * TOKENS ** 0.5), 2048.0, ((0, 8),), jnp.float32)
    router_mix_second = jnp.clip(jnp.exp(math.log(442368.0) - 1.3862944 * jax.random.uniform(arg_keys[20], (D, NEXP + 4), jnp.float32) ** block_levels(arg_keys[20], (D, NEXP + 4), ((0, 8),), -0.2, 0.2)), 110592.0, 442368.0)
    vectors = jnp.clip(1.0 + 0.1 * jax.random.normal(arg_keys[21], (4, D), jnp.float32), 0.5, 1.5)
    vectors_first = gaussian(arg_keys[22], (4, D), (TOKENS ** 0.5), 640.0, ((1, 8),), jnp.float32)
    vectors_second = jnp.clip(jnp.exp(math.log(49152.0) - 1.3862944 * jax.random.uniform(arg_keys[23], (4, D), jnp.float32) ** block_levels(arg_keys[23], (4, D), ((1, 8),), -0.2, 0.2)), 12288.0, 49152.0)
    return dict(tokens=tokens, route_residual=route_residual, doc_lengths=doc_lengths, routes=routes, priority=priority, grad_out=grad_out, attend_in=attend_in, attend_in_first=attend_in_first, attend_in_second=attend_in_second, attend_out=attend_out, attend_out_first=attend_out_first, attend_out_second=attend_out_second, expert_up=expert_up, expert_up_first=expert_up_first, expert_up_second=expert_up_second, expert_down=expert_down, expert_down_first=expert_down_first, expert_down_second=expert_down_second, router_mix=router_mix, router_mix_first=router_mix_first, router_mix_second=router_mix_second, vectors=vectors, vectors_first=vectors_first, vectors_second=vectors_second)


NORM_EPSILON = 1e-05
ROPE_BASE = 10000.0
NEGATIVE = -1e+30
HIGHEST = lax.Precision.HIGHEST
MOMENT_DECAY = 0.5
ADAM_EPSILON = 1e-08
STEP_RATES = (0.04, 0.1, 0.04, 0.02, 0.02, 0.2)
STEP_DECAYS = (0.1, 0.1, 0.1, 0.1, 0.1, 0.0)

@jax.custom_vjp
def low(v):
    return lax.optimization_barrier(v.astype(jnp.bfloat16)).astype(jnp.float32)

@jax.custom_vjp
def low_back(v):
    return v

def low_keep(v):
    return (low(v), None)

def low_pass(kept, grad):
    return (grad,)

def back_keep(v):
    return (v, None)

def back_low(kept, grad):
    return (low(grad),)
low.defvjp(low_keep, low_pass)
low_back.defvjp(back_keep, back_low)

def rms_norm(values, gain_row):
    scale_rows = lax.rsqrt(lax.optimization_barrier(jnp.mean(values * values, axis=-1, keepdims=True)) + NORM_EPSILON)
    return values * scale_rows * gain_row

def doc_layout(lengths, token_ids):
    starts = jnp.cumsum(lengths) - lengths
    inside = starts[None, :] <= token_ids[:, None]
    segment = lax.optimization_barrier(jnp.sum(inside.astype(jnp.int32), axis=1))
    doc_begin = lax.optimization_barrier(jnp.max(jnp.where(inside, starts[None, :], 0), axis=1))
    return (segment, token_ids - doc_begin)

def rope_tables(positions):
    frequency = ROPE_BASE ** (-(jnp.arange(HEAD_DIM // 2, dtype=jnp.float32) * 2.0 / HEAD_DIM))
    angles = positions.astype(jnp.float32)[:, None] * frequency[None, :]
    return (jnp.cos(angles), jnp.sin(angles))

def rotate(values, cosine, sine_table, direction):
    shaped = values.reshape(values.shape[0], -1, HEAD_DIM)
    front_half = shaped[..., :HEAD_DIM // 2]
    back_half = shaped[..., HEAD_DIM // 2:]
    cos_rows = cosine[:, None, :]
    sin_rows = direction * sine_table[:, None, :]
    turned = jnp.concatenate([front_half * cos_rows - back_half * sin_rows, back_half * cos_rows + front_half * sin_rows], axis=-1)
    return turned.reshape(values.shape)

def attend_block(offset, query_heads, key_heads, value_heads, segment, block_rows):
    query_rows = lax.dynamic_slice_in_dim(query_heads, offset, block_rows, 0)
    scores = jnp.einsum('qhd,khd->hqk', query_rows, key_heads, precision=HIGHEST) * HEAD_DIM ** (-0.5)
    scores = low_back(scores)
    row_ids = offset + jnp.arange(block_rows, dtype=jnp.int32)
    col_ids = jnp.arange(key_heads.shape[0], dtype=jnp.int32)
    row_seg = lax.dynamic_slice_in_dim(segment, offset, block_rows, 0)
    allowed = (row_seg[:, None] == segment[None, :]) & (col_ids[None, :] <= row_ids[:, None])
    scores = jnp.where(allowed[None], scores, NEGATIVE)
    probabilities = low(jax.nn.softmax(scores, axis=-1))
    return jnp.einsum('hqk,khd->qhd', probabilities, value_heads, precision=HIGHEST)

def attend(query, key_rows, value_rows, segment):
    stream_len = query.shape[0]
    block_rows = min(512, stream_len)
    query_heads = query.reshape(stream_len, HEADS, HEAD_DIM)
    key_heads = key_rows.reshape(stream_len, HEADS, HEAD_DIM)
    value_heads = value_rows.reshape(stream_len, HEADS, HEAD_DIM)
    checked = jax.checkpoint(partial(attend_block, block_rows=block_rows))
    offsets = jnp.arange(0, stream_len, block_rows, dtype=jnp.int32)
    outputs = lax.map(lambda offset: checked(offset, query_heads, key_heads, value_heads, segment), offsets)
    return outputs.reshape(stream_len, HEADS * HEAD_DIM)

def expert_block(hidden_rows, route_rows, priority_rows, w_up, w_down):
    local_tokens = hidden_rows.shape[0]
    expert_id = route_rows.T.reshape(-1)
    order_key = (jnp.arange(TOPK, dtype=jnp.int32)[:, None] * SEQ_LEN + priority_rows[None, :]).reshape(-1)
    earlier = (expert_id[:, None] == expert_id[None, :]) & (order_key[None, :] < order_key[:, None])
    slot_rank = lax.optimization_barrier(jnp.sum(earlier.astype(jnp.int32), axis=1))
    kept_pair = (expert_id < NFFN) & (slot_rank < CAP)
    index_rows = jnp.where(kept_pair, expert_id * CAP + slot_rank, NFFN * CAP).astype(jnp.int32)
    pair_rows = jnp.concatenate([hidden_rows] * TOPK, axis=0)
    buffer_rows = jnp.zeros((NFFN * CAP + 1, D), jnp.float32).at[index_rows].add(pair_rows)
    buffer_rows = buffer_rows[:NFFN * CAP].reshape(NFFN, CAP, D)
    up_proj = low_back(jnp.einsum('ecd,edf->ecf', buffer_rows, w_up, precision=HIGHEST))
    activated = low(jax.nn.silu(up_proj[..., :FF]) * up_proj[..., FF:])
    down_proj = low_back(jnp.einsum('ecf,efd->ecd', activated, w_down, precision=HIGHEST))
    padded = jnp.concatenate([down_proj.reshape(NFFN * CAP, D), jnp.zeros((1, D), jnp.float32)], axis=0)
    return padded[index_rows].reshape(TOPK, local_tokens, D)

def pair_values(route_ids, ffn_rows, hidden_val, coefficient, vector_rows):
    const_zero = coefficient[:, 0, 0:1] * hidden_val + coefficient[:, 0, 1:2] * vector_rows[2][None, :]
    const_one = coefficient[:, 1, 0:1] * hidden_val + coefficient[:, 1, 1:2] * vector_rows[3][None, :]
    outputs = []
    for pick_index in range(TOPK):
        expert_col = route_ids[:, pick_index][:, None]
        result = jnp.where(expert_col < NFFN, ffn_rows[pick_index], 0.0)
        result = jnp.where(expert_col == NFFN + 1, hidden_val, result)
        result = jnp.where(expert_col == NFFN + 2, const_zero, result)
        result = jnp.where(expert_col == NFFN + 3, const_one, result)
        outputs.append(result)
    return outputs

def layer(params, residual_in, route_residual, lengths, route_ids, priority_ids):
    w_in, w_out, w_up, w_down, w_router, w_vectors = [low(weight_item) for weight_item in params]
    stream_len = residual_in.shape[0]
    token_ids = jnp.arange(stream_len, dtype=jnp.int32)
    segment, positions = doc_layout(lengths, token_ids)
    cosine, sine_table = rope_tables(positions)
    normed = low(rms_norm(residual_in, w_vectors[0]))
    raw = low_back(jnp.einsum('td,cde->cte', normed, w_in, precision=HIGHEST))
    query = low_back(low(rotate(raw[0], cosine, sine_table, 1.0)))
    key_rows = low_back(low(rotate(raw[1], cosine, sine_table, 1.0)))
    value_rows = low_back(low(raw[2]))
    attended = low_back(low(attend(query, key_rows, value_rows, segment)))
    branch = low_back(jnp.dot(attended, w_out, precision=HIGHEST))
    middle = residual_in + branch
    hidden = low(rms_norm(middle, w_vectors[1]))
    logits = jnp.dot(hidden, w_router, precision=HIGHEST)
    route_logits = logits[:, :NEXP] + route_residual
    picked = jnp.take_along_axis(route_logits, route_ids, axis=1)
    gate_weights = jax.nn.softmax(picked, axis=-1)
    coefficient = jax.nn.softmax(logits[:, NEXP:].reshape(stream_len, 2, 2), axis=-1)
    blocks = stream_len // TOK_DEV
    ffn_blocks = jax.vmap(expert_block, in_axes=(0, 0, 0, None, None))(hidden.reshape(blocks, TOK_DEV, D), route_ids.reshape(blocks, TOK_DEV, TOPK), priority_ids.reshape(blocks, TOK_DEV), w_up, w_down)
    ffn_rows = ffn_blocks.transpose(1, 0, 2, 3).reshape(TOPK, stream_len, D)
    values_list = pair_values(route_ids, ffn_rows, hidden, coefficient, w_vectors)
    mixture = gate_weights[:, 0:1] * values_list[0] + gate_weights[:, 1:2] * values_list[1]
    return middle + mixture

def adam_update(weight, grad, first, second, rate, decay):
    first_new = MOMENT_DECAY * first + (1.0 - MOMENT_DECAY) * grad
    second_new = MOMENT_DECAY * second + (1.0 - MOMENT_DECAY) * grad * grad
    correction = 1.0 - MOMENT_DECAY ** STEP
    update = first_new / correction / (jnp.sqrt(second_new / correction) + ADAM_EPSILON)
    return (weight - rate * (update + decay * weight), first_new, second_new)

def reference(tokens, route_residual, doc_lengths, routes, priority, grad_out, attend_in, attend_in_first, attend_in_second, attend_out, attend_out_first, attend_out_second, expert_up, expert_up_first, expert_up_second, expert_down, expert_down_first, expert_down_second, router_mix, router_mix_first, router_mix_second, vectors, vectors_first, vectors_second):
    params = (attend_in, attend_out, expert_up, expert_down, router_mix, vectors)

    def group_step(totals, inputs):
        token_rows, residual_rows, length_row, route_rows, priority_rows, grad_rows = inputs

        def forward(weight_set, token_vals, residual_vals):
            return layer(weight_set, token_vals, residual_vals, length_row, route_rows, priority_rows)
        result, pullback = jax.vjp(forward, params, token_rows.astype(jnp.float32), residual_rows)
        grad_params, grad_token_rows, grad_residual_rows = pullback(grad_rows.astype(jnp.float32))
        totals = jax.tree.map(jnp.add, totals, grad_params)
        return (totals, (result.astype(jnp.bfloat16), grad_token_rows, grad_residual_rows))
    zero_grads = jax.tree.map(jnp.zeros_like, params)
    totals, (layer_out, grad_tokens, grad_residual) = lax.scan(group_step, zero_grads, (tokens, route_residual, doc_lengths, routes, priority, grad_out))
    firsts = (attend_in_first, attend_out_first, expert_up_first, expert_down_first, router_mix_first, vectors_first)
    seconds = (attend_in_second, attend_out_second, expert_up_second, expert_down_second, router_mix_second, vectors_second)
    results = []
    for kind_index in range(6):
        results.extend(adam_update(params[kind_index], totals[kind_index], firsts[kind_index], seconds[kind_index], STEP_RATES[kind_index], STEP_DECAYS[kind_index]))
    return (layer_out, grad_tokens, grad_residual, results[0], results[1], results[2], results[3], results[4], results[5], results[6], results[7], results[8], results[9], results[10], results[11], results[12], results[13], results[14], results[15], results[16], results[17])
```

```python
import functools

import jax
import jax.numpy as jnp
import numpy as np
from jax import lax
from jax.experimental import pallas as pl
from jax.experimental.pallas import tpu as pltpu
from jax.sharding import PartitionSpec as P

D = 768
HEADS = 12
HEAD_DIM = 64
FF = 2048
NFFN = 4
NEXP = 8
TOPK = 2
STEP = 5
CAP = 96
LINE = 4
OUTER = 8
LOCAL_HEADS = 3

NORM_EPSILON = 1e-05
ROPE_BASE = 10000.0
NEGATIVE = -1e30
MOMENT_DECAY = 0.5
ADAM_EPSILON = 1e-08
STEP_RATES = (0.04, 0.1, 0.04, 0.02, 0.02, 0.2)
STEP_DECAYS = (0.1, 0.1, 0.1, 0.1, 0.1, 0.0)
BF = jnp.bfloat16
F32 = jnp.float32
MESH = pl.DeviceIdType.MESH
VMEM_LIMIT = 48 * 2**20


def mm(left, right):
    return jnp.dot(left, right, preferred_element_type=F32)


def mm_nt(left, right):
    return lax.dot_general(left, right, (((1,), (1,)), ((), ())), preferred_element_type=F32)


def mm_tn(left, right):
    return lax.dot_general(left, right, (((0,), (0,)), ((), ())), preferred_element_type=F32)


class Place:
    def __init__(self, inner):
        q = lax.axis_index("seq")
        shard = lax.axis_index("shard")
        self.inner = inner
        self.rest = lax.rem(shard, inner) if inner > 1 else 0
        outer = lax.div(shard, inner) if inner > 1 else shard
        self.q = q
        self.x = lax.div(q, 2)
        self.c = lax.rem(q, 2)
        self.l = lax.div(outer, 2)
        self.y = lax.rem(outer, 2)
        self.own = outer

    def at(self, x=None, c=None, l=None, y=None):
        x = self.x if x is None else x
        c = self.c if c is None else c
        l = self.l if l is None else l
        y = self.y if y is None else y
        return (2 * x + c, (2 * l + y) * self.inner + self.rest)


def greet(me, devices, line):
    barrier = pltpu.get_barrier_semaphore()
    for device in devices:
        pl.semaphore_signal(barrier, inc=1, device_id=device, device_id_type=MESH)
    if not line:
        pl.semaphore_wait(barrier, len(devices))
        return

    @pl.when(me.l > 0)
    def _():
        pl.semaphore_signal(barrier, inc=1, device_id=me.at(l=me.l - 1), device_id_type=MESH)

    @pl.when(me.l < LINE - 1)
    def _():
        pl.semaphore_signal(barrier, inc=1, device_id=me.at(l=me.l + 1), device_id_type=MESH)

    near = jnp.minimum(me.l, 1) + jnp.minimum(LINE - 1 - me.l, 1)
    pl.semaphore_wait(barrier, len(devices) + near)


def remote(src, dst, send, recv, device):
    return pltpu.make_async_remote_copy(
        src_ref=src, dst_ref=dst, send_sem=send, recv_sem=recv, device_id=device, device_id_type=MESH
    )


def rope_constants(stream_len):
    frequency = ROPE_BASE ** (-(np.arange(HEAD_DIM // 2, dtype=np.float64) * 2.0 / HEAD_DIM))
    angles = np.arange(stream_len, dtype=np.float64)[:, None] * frequency[None, :]
    cosine = np.tile(np.cos(angles), (1, 4)).astype(np.float32)
    sine = np.tile(np.sin(angles), (1, 4)).astype(np.float32)
    turn = np.zeros((128, 128), np.float32)
    for j in range(128):
        if j % 64 < 32:
            turn[j + 32, j] = -1.0
        else:
            turn[j - 32, j] = 1.0
    return cosine, sine, turn


A_ROWS = 5 * 96
O_ROWS = 144
S_ROWS = 96
PACK = A_ROWS + O_ROWS + S_ROWS
TOK = 384
STREAM = 1536
ATT = 576


def forward_kernel(
    inner,
    tok, pack, up, dn, cos, sin, begin, turn,
    stream, packs, wo_all, wup, wdn, normed, qs, ks, vs, ohead, lse, attended, branch, wo,
    wq, wr, pk, got, ss, rs, ls,
):
    me = Place(inner)
    x, c, l, y, q, own = me.x, me.c, me.l, me.y, me.q, me.own
    nx, nc, ny = 1 - x, 1 - c, 1 - y

    S_TOK, S_PACK, S_WO, S_EX, S_ATT = 0, 3, 15, 18, 52
    R_TOK, R_PACK, R_WO, R_EX, R_ATT = 0, 3, 11, 14, 30

    keep = [
        pltpu.make_async_copy(up.at[y], wup.at[own], ls.at[0]),
        pltpu.make_async_copy(dn.at[y], wdn.at[own], ls.at[1]),
    ]
    for copy in keep:
        copy.start()
    greet(me, [me.at(c=nc), me.at(x=nx), me.at(x=nx, c=nc), me.at(y=ny)], True)

    def tok_copy(k, part, device):
        return remote(stream.at[part], stream.at[part], ss.at[S_TOK + k], rs.at[R_TOK + k], device)

    def pack_copy(kind, z, device):
        slot = 2 * z + y
        return remote(
            packs.at[slot], packs.at[slot], ss.at[S_PACK + 4 * kind + z], rs.at[R_PACK + slot], device
        )

    def pack_wait(slot):
        remote(packs.at[slot], packs.at[slot], ss.at[0], rs.at[R_PACK + slot], me.at(y=ny)).wait_recv()

    def ex_copies(kind, z, yy, device):
        slot = 2 * z + yy
        k = 2 * (8 * kind + slot)
        return [
            remote(ref.at[slot], ref.at[slot], ss.at[S_EX + k + n], rs.at[R_EX + 2 * slot + n], device)
            for n, ref in enumerate((wup, wdn))
        ]

    def ex_wait(slot):
        for n, ref in enumerate((wup, wdn)):
            remote(ref.at[slot], ref.at[slot], ss.at[0], rs.at[R_EX + 2 * slot + n], me.at(y=ny)).wait_recv()

    def ex_forward(z, yy, upward):
        if upward:
            @pl.when(l < LINE - 1)
            def _():
                for copy in ex_copies(0, z, yy, me.at(l=l + 1)):
                    copy.start()
        else:
            @pl.when(l > 0)
            def _():
                for copy in ex_copies(1, z, yy, me.at(l=l - 1)):
                    copy.start()

    stream[q] = tok[...]
    packs[own] = pack[...]
    tok_copy(1, q, me.at(x=nx)).start()
    tok_copy(0, q, me.at(c=nc)).start()

    def pack_up(z):
        @pl.when(l < LINE - 1)
        def _():
            pack_copy(0, z, me.at(l=l + 1)).start()

    def pack_down(z):
        @pl.when(l > 0)
        def _():
            pack_copy(1, z, me.at(l=l - 1)).start()

    def pack_over(z):
        pack_copy(2, z, me.at(y=ny)).start()

    pack_up(l)
    pack_down(l)
    pack_over(l)
    for step in range(1, LINE):
        @pl.when(l - step >= 0)
        def _():
            pack_wait(2 * (l - step) + y)
            pack_up(l - step)
            pack_over(l - step)

        @pl.when(l + step < LINE)
        def _():
            pack_wait(2 * (l + step) + y)
            pack_down(l + step)
            pack_over(l + step)

    for n, (src, ref) in enumerate(((up, wup), (dn, wdn))):
        remote(
            src.at[ny], ref.at[own], ss.at[S_EX + 32 + n], rs.at[R_EX + 2 * own + n], me.at(y=ny)
        ).start()
    for copy in keep:
        copy.wait()
    ex_forward(l, y, True)
    ex_forward(l, y, False)

    tok_copy(1, 2 * nx + c, me.at(x=nx)).wait_recv()
    tok_copy(2, 2 * nx + c, me.at(c=nc)).start()

    for z in range(LINE):
        pack_wait(2 * z + ny)

    wo_all[:, pl.ds(q * O_ROWS, O_ROWS), :] = packs[:, A_ROWS:A_ROWS + O_ROWS, :]

    def wo_copy(k, part, device):
        rows = pl.ds(part * O_ROWS, O_ROWS)
        return remote(
            wo_all.at[:, rows, :], wo_all.at[:, rows, :], ss.at[S_WO + k], rs.at[R_WO + k], device
        )

    wo_copy(1, q, me.at(x=nx)).start()
    wo_copy(0, q, me.at(c=nc)).start()

    for s in range(OUTER):
        for t in range(5):
            wq[t, 96 * s:96 * (s + 1), :] = packs[s, 96 * t:96 * (t + 1), :]
    for t in range(LOCAL_HEADS):
        wr[t] = mm(wq[t], turn[...]).astype(BF)
    gain = []
    for t in range(6):
        total = jnp.zeros((1, 128), F32)
        for s in range(OUTER):
            first = A_ROWS + O_ROWS + 16 * t
            total = total + packs[s, first:first + 16, :].astype(F32)[0:1]
        gain.append(total)
    gain = jnp.concatenate(gain, axis=1)

    tok_copy(0, 2 * x + nc, me.at(c=nc)).wait_recv()
    tok_copy(2, 2 * nx + nc, me.at(c=nc)).wait_recv()

    wo_copy(1, 2 * nx + c, me.at(x=nx)).wait_recv()
    wo_copy(2, 2 * nx + c, me.at(c=nc)).start()

    @pl.loop(0, 4)
    def _(part):
        values = stream[part].astype(F32)
        scale = lax.rsqrt(jnp.mean(values * values, axis=1, keepdims=True) + NORM_EPSILON)
        rows = pl.ds(pl.multiple_of(part * TOK, TOK), TOK)
        low = (values * scale * gain).astype(BF)
        normed[rows, :] = low
        cosine, sine = cos[rows, :], sin[rows, :]
        for h in range(LOCAL_HEADS):
            turned = mm(low, wq[h]) * cosine + mm(low, wr[h]) * sine
            qs[h, rows, :] = (turned[:, :64] * 0.125).astype(BF)
            ks[h, rows, :] = turned[:, 64:].astype(BF)
        both = mm(low, wq[3])
        vs[0, rows, :] = both[:, :64].astype(BF)
        vs[1, rows, :] = both[:, 64:].astype(BF)
        vs[2, rows, :] = mm(low, wq[4])[:, :64].astype(BF)

    def relay(step):
        @pl.when(l - step >= 0)
        def _():
            ex_wait(2 * (l - step) + y)
            ex_forward(l - step, y, True)
        @pl.when(l + step < LINE)
        def _():
            ex_wait(2 * (l + step) + y)
            ex_forward(l + step, y, False)
        @pl.when(l - step >= 0)
        def _():
            ex_wait(2 * (l - step) + ny)
            ex_forward(l - step, ny, True)
        @pl.when(l + step < LINE)
        def _():
            ex_wait(2 * (l + step) + ny)
            ex_forward(l + step, ny, False)

    ex_wait(2 * l + ny)
    ex_forward(l, ny, True)
    ex_forward(l, ny, False)

    block = 256

    def one_head(h):
        for b in range(STREAM // block):
            first, last = b * block, (b + 1) * block
            scores = mm_nt(qs[h, first:last, :], ks[h, 0:last, :])
            col = lax.broadcasted_iota(jnp.int32, (block, last), 1)
            row = lax.broadcasted_iota(jnp.int32, (block, last), 0) + first
            seen = (col >= begin[first:last, :]) & (col <= row)
            scores = jnp.where(seen, scores, NEGATIVE)
            top = jnp.max(scores, axis=1, keepdims=True)
            weight = jnp.exp(scores - top)
            total = jnp.sum(weight, axis=1, keepdims=True)
            result = mm(weight.astype(BF), vs[h, 0:last, :]) / total
            ohead[h, first:last, :] = result.astype(BF)
            logs = jnp.broadcast_to(top + jnp.log(total), (block, 128))
            lse[h, :, first:last] = jnp.transpose(logs)[0:8, :]

    pl.loop(0, 1)(one_head)
    relay(1)
    pl.loop(1, LOCAL_HEADS)(one_head)

    for part in range(4):
        rows = slice(part * TOK, (part + 1) * TOK)
        pk[part, 0:TOK, :] = jnp.concatenate([ohead[0, rows, :], ohead[1, rows, :]], axis=1)
        half = TOK // 2
        third = [ohead[2, part * TOK + k * half:part * TOK + (k + 1) * half, :] for k in range(2)]
        pk[part, TOK:ATT, :] = jnp.concatenate(third, axis=1)
    got[q] = pk[q]

    def att_copy(k, to, frm, device):
        return remote(pk.at[to], got.at[frm], ss.at[S_ATT + k], rs.at[R_ATT + k], device)

    others = [(2 * nx + c, me.at(x=nx)), (2 * nx + nc, me.at(x=nx, c=nc)), (2 * x + nc, me.at(c=nc))]
    for k, (other, device) in enumerate(others):
        att_copy(k, other, q, device).start()

    wo_copy(0, 2 * x + nc, me.at(c=nc)).wait_recv()
    wo_copy(2, 2 * nx + nc, me.at(c=nc)).wait_recv()
    for s in range(OUTER):
        for t in range(6):
            wo[96 * s:96 * (s + 1), 128 * t:128 * (t + 1)] = wo_all[s, 96 * t:96 * (t + 1), :]

    relay(2)
    for k, (other, device) in enumerate(others):
        att_copy(k, q, other, device).wait_recv()
    pieces = []
    for part in range(4):
        both = got[part, 0:TOK, :]
        half = TOK // 2
        low = got[part, TOK:ATT, :]
        pieces.append(both)
        pieces.append(jnp.concatenate([low[:, :64], low[:, 64:]], axis=0))
    whole = jnp.concatenate(pieces, axis=1)
    attended[...] = whole
    branch[...] = mm(whole, wo[...])

    relay(3)

    tok_copy(1, q, me.at(x=nx)).wait_send()
    tok_copy(0, q, me.at(c=nc)).wait_send()
    tok_copy(2, 2 * nx + c, me.at(c=nc)).wait_send()
    wo_copy(1, q, me.at(x=nx)).wait_send()
    wo_copy(0, q, me.at(c=nc)).wait_send()
    wo_copy(2, 2 * nx + c, me.at(c=nc)).wait_send()
    for k, (other, device) in enumerate(others):
        att_copy(k, other, q, device).wait_send()
    for n, (src, ref) in enumerate(((up, wup), (dn, wdn))):
        remote(
            src.at[ny], ref.at[own], ss.at[S_EX + 32 + n], rs.at[R_EX + 2 * own + n], me.at(y=ny)
        ).wait_send()
    for z in range(LINE):
        pack_copy(2, z, me.at(y=ny)).wait_send()

        @pl.when((l >= z) & (l < LINE - 1))
        def _():
            pack_copy(0, z, me.at(l=l + 1)).wait_send()
            for yy in range(2):
                for copy in ex_copies(0, z, yy, me.at(l=l + 1)):
                    copy.wait_send()

        @pl.when((l <= z) & (l > 0))
        def _():
            pack_copy(1, z, me.at(l=l - 1)).wait_send()
            for yy in range(2):
                for copy in ex_copies(1, z, yy, me.at(l=l - 1)):
                    copy.wait_send()


def forward_call(inner, tok, pack, up, dn, cos, sin, begin, turn):
    vm = pl.BlockSpec(memory_space=pltpu.VMEM)
    hbm = pl.BlockSpec(memory_space=pl.ANY)
    shapes = [
        ((4, TOK, D), BF, vm),
        ((OUTER, PACK, 128), BF, vm),
        ((OUTER, 576, 128), BF, vm),
        ((OUTER, 96, FF), BF, hbm),
        ((OUTER, 128, D), BF, hbm),
        ((STREAM, D), BF, vm),
        ((LOCAL_HEADS, STREAM, 64), BF, vm),
        ((LOCAL_HEADS, STREAM, 64), BF, vm),
        ((LOCAL_HEADS, STREAM, 64), BF, vm),
        ((LOCAL_HEADS, STREAM, 64), BF, vm),
        ((LOCAL_HEADS, 8, STREAM), F32, vm),
        ((TOK, D), BF, vm),
        ((TOK, D), F32, vm),
        ((D, D), BF, vm),
    ]
    return pl.pallas_call(
        functools.partial(forward_kernel, inner),
        out_shape=[jax.ShapeDtypeStruct(s, t) for s, t, _ in shapes],
        in_specs=[vm, vm, hbm, hbm, vm, vm, vm, vm],
        out_specs=[spec for _, _, spec in shapes],
        scratch_shapes=[
            pltpu.VMEM((5, D, 128), BF),
            pltpu.VMEM((3, D, 128), BF),
            pltpu.VMEM((4, ATT, 128), BF),
            pltpu.VMEM((4, ATT, 128), BF),
            pltpu.SemaphoreType.DMA((55,)),
            pltpu.SemaphoreType.DMA((33,)),
            pltpu.SemaphoreType.DMA((2,)),
        ],
        compiler_params=pltpu.CompilerParams(
            collective_id=0, has_side_effects=True, vmem_limit_bytes=VMEM_LIMIT
        ),
        name="gather_attend",
    )(tok, pack, up, dn, cos, sin, begin, turn)


def gather_inner(values, axis, inner):
    if inner == 1:
        return values
    count = lax.axis_size("shard")
    groups = [[o * inner + i for i in range(inner)] for o in range(count // inner)]
    return lax.all_gather(values, "shard", axis=axis, tiled=True, axis_index_groups=groups)


def pick(values, index, axis):
    return lax.dynamic_index_in_dim(values, index, axis, keepdims=False)


def pack_attention(w_in, w_out, w_router, w_vectors, q, outer):
    heads = pick(w_in.reshape(3, 96, 4, LOCAL_HEADS, 64), q, 2)
    tiles = [jnp.concatenate([heads[0, :, h], heads[1, :, h]], axis=1) for h in range(LOCAL_HEADS)]
    tiles.append(jnp.concatenate([heads[2, :, 0], heads[2, :, 1]], axis=1))
    tiles.append(jnp.pad(heads[2, :, 2], ((0, 0), (0, 64))))
    out_tiles = w_out.reshape(96, 6, 128).transpose(1, 0, 2).reshape(4, O_ROWS, 128)
    small = jnp.concatenate([w_vectors, w_router.T], axis=0)
    placed = lax.dynamic_update_slice(jnp.zeros((16, D), BF), small, (0, 96 * outer))
    small_tiles = placed.reshape(16, 6, 128).transpose(1, 0, 2).reshape(S_ROWS, 128)
    return jnp.concatenate(tiles + [pick(out_tiles, q, 0), small_tiles], axis=0)


def expert_pieces(w_up, w_down, x, c):
    ups = lax.dynamic_slice_in_dim(w_up, 2 * x, 2, 0).reshape(2, 96, 2, 8, 2, 128)
    ups = pick(ups, c, 4).reshape(2, 96, FF).astype(BF)
    downs = lax.dynamic_slice(w_down, (2 * x, 128 * c, 0), (2, 128, D)).astype(BF)
    return ups, downs


def expert_kernel(
    inner,
    bufh, bufg, wup, wdn,
    down_ret, gbuf_ret, gup, gdn,
    rowh, rowg, rowt, act, da, db, total, part_out, part_in, send, ss, rs,
):
    me = Place(inner)
    x, c, y = me.x, me.c, me.y
    nx, nc, ny = 1 - x, 1 - c, 1 - y
    mine = 2 * x + y
    chips = [(nx, y), (x, ny), (nx, ny)]
    greet(me, [me.at(c=nc)] + [me.at(x=cx, y=cy) for cx, cy in chips], False)
    base = 4 * c

    def out_copy(n, buf, row, k, cx, cy):
        return remote(
            buf.at[2 * cx + cy], row.at[base + mine], ss.at[16 * n + k], rs.at[16 * n + mine], me.at(x=cx, y=cy)
        )

    def in_wait(n, row, cx, cy):
        slot = 2 * cx + cy
        remote(
            row.at[base + slot], row.at[base + slot], ss.at[0], rs.at[16 * n + slot], me.at(x=cx, y=cy)
        ).wait_recv()

    def core_copy(n, row, first, k, slot):
        return remote(
            row.at[first + slot], row.at[first + slot], ss.at[16 * n + 3 + k], rs.at[16 * n + 4 + slot], me.at(c=nc)
        )

    for n, (buf, row) in enumerate(((bufh, rowh), (bufg, rowg))):
        for k, (cx, cy) in enumerate(chips):
            out_copy(n, buf, row, k, cx, cy).start()
        row[base + mine] = buf[mine]
        core_copy(n, row, base, 0, mine).start()

    def collect(n, row):
        for k, (cx, cy) in enumerate(chips):
            in_wait(n, row, cx, cy)
            core_copy(n, row, base, 1 + k, 2 * cx + cy).start()
        for slot in range(4):
            core_copy(n, row, 4 - base, 0, slot).wait_recv()

    collect(0, rowh)
    rows_h = rowh[...].reshape(8 * CAP, D)
    rowt[...] = jnp.transpose(rows_h.astype(F32)).astype(BF)
    total[...] = jnp.zeros_like(total)

    @pl.loop(0, 4)
    def _(j):
        gate_cols = pl.ds(pl.multiple_of(j * 256, 256), 256)
        lin_cols = pl.ds(pl.multiple_of(1024 + j * 256, 256), 256)
        rows_in = rowh[...].reshape(8 * CAP, D)
        gate = mm(rows_in, wup[:, :, gate_cols].reshape(D, 256))
        lin = mm(rows_in, wup[:, :, lin_cols].reshape(D, 256))
        sigma = jax.nn.sigmoid(gate)
        silu = gate * sigma
        low = (silu * lin).astype(BF)
        act[:, gate_cols] = low
        da[:, gate_cols] = lin * sigma * (1.0 + gate * (1.0 - sigma))
        db[:, gate_cols] = silu
        total[...] += mm(low, wdn[pl.ds(2 * j, 2)].reshape(256, D))

    def give_back(n, ret):
        other = pl.multiple_of((4 - base) * CAP, 4 * CAP)
        part_out[n] = total[pl.ds(other, 4 * CAP), :].astype(BF)
        swap = remote(part_out.at[n], part_in.at[n], ss.at[16 * n + 7], rs.at[16 * n + 8], me.at(c=nc))
        swap.start()
        swap.wait_recv()
        kept = total[pl.ds(pl.multiple_of(base * CAP, 4 * CAP), 4 * CAP), :]
        send[n] = (kept + part_in[n].astype(F32)).astype(BF).reshape(4, CAP, D)
        for k, (cx, cy) in enumerate(chips):
            back_copy(n, ret, k, cx, cy).start()
        ret[mine] = send[n, mine]

    def back_copy(n, ret, k, cx, cy):
        return remote(
            send.at[n, 2 * cx + cy], ret.at[mine], ss.at[16 * n + 8 + k], rs.at[16 * n + 9 + mine], me.at(x=cx, y=cy)
        )

    def back_wait(n, ret, cx, cy):
        slot = 2 * cx + cy
        remote(
            ret.at[slot], ret.at[slot], ss.at[0], rs.at[16 * n + 9 + slot], me.at(x=cx, y=cy)
        ).wait_recv()

    give_back(0, down_ret)
    collect(1, rowg)
    total[...] = jnp.zeros_like(total)

    @pl.loop(0, 4)
    def _(j):
        gate_cols = pl.ds(pl.multiple_of(j * 256, 256), 256)
        lin_cols = pl.ds(pl.multiple_of(1024 + j * 256, 256), 256)
        rows_g = rowg[...].reshape(8 * CAP, D)
        grad_act = mm_nt(rows_g, wdn[pl.ds(2 * j, 2)].reshape(256, D))
        grad_gate = (grad_act * da[:, gate_cols]).astype(BF)
        grad_lin = (grad_act * db[:, gate_cols]).astype(BF)
        gdn[pl.ds(2 * j, 2)] = mm_tn(act[:, gate_cols], rows_g).astype(BF).reshape(2, 128, D)
        gup[:, :, gate_cols] = mm(rowt[...], grad_gate).astype(BF).reshape(8, 96, 256)
        gup[:, :, lin_cols] = mm(rowt[...], grad_lin).astype(BF).reshape(8, 96, 256)
        total[...] += mm_nt(grad_gate, wup[:, :, gate_cols].reshape(D, 256)) + mm_nt(
            grad_lin, wup[:, :, lin_cols].reshape(D, 256)
        )

    give_back(1, gbuf_ret)
    for n, (buf, row, ret) in enumerate(((bufh, rowh, down_ret), (bufg, rowg, gbuf_ret))):
        for k, (cx, cy) in enumerate(chips):
            back_wait(n, ret, cx, cy)
            out_copy(n, buf, row, k, cx, cy).wait_send()
            back_copy(n, ret, k, cx, cy).wait_send()
            core_copy(n, row, base, 1 + k, 2 * cx + cy).wait_send()
        core_copy(n, row, base, 0, mine).wait_send()
        remote(part_out.at[n], part_in.at[n], ss.at[16 * n + 7], rs.at[16 * n + 8], me.at(c=nc)).wait_send()


def expert_call(inner, bufh, bufg, wup, wdn):
    vm = pl.BlockSpec(memory_space=pltpu.VMEM)
    rows = 8 * CAP
    return pl.pallas_call(
        functools.partial(expert_kernel, inner),
        out_shape=[
            jax.ShapeDtypeStruct((NFFN, CAP, D), BF),
            jax.ShapeDtypeStruct((NFFN, CAP, D), BF),
            jax.ShapeDtypeStruct((OUTER, 96, FF), BF),
            jax.ShapeDtypeStruct((OUTER, 128, D), BF),
        ],
        in_specs=[vm] * 4,
        out_specs=[vm] * 4,
        scratch_shapes=[
            pltpu.VMEM((8, CAP, D), BF),
            pltpu.VMEM((8, CAP, D), BF),
            pltpu.VMEM((D, rows), BF),
            pltpu.VMEM((rows, 1024), BF),
            pltpu.VMEM((rows, 1024), F32),
            pltpu.VMEM((rows, 1024), F32),
            pltpu.VMEM((rows, D), F32),
            pltpu.VMEM((2, 4 * CAP, D), BF),
            pltpu.VMEM((2, 4 * CAP, D), BF),
            pltpu.VMEM((2, 4, CAP, D), BF),
            pltpu.SemaphoreType.DMA((32,)),
            pltpu.SemaphoreType.DMA((32,)),
        ],
        compiler_params=pltpu.CompilerParams(
            collective_id=1, has_side_effects=True, vmem_limit_bytes=VMEM_LIMIT
        ),
        name="experts",
    )(bufh, bufg, wup, wdn)


def backward_kernel(
    inner,
    gbranch, attended, wo, qs, ks, vs, ohead, lse, begin, cos, sin, turn, normed, packs, stream, small,
    gup, gdn,
    gnorm_ret, apack, gup_all, gdn_all,
    pk, got, kt, grad, dq, dk, dv, dk_sum, dv_sum, delta, gr, wall, wo_out, wo_in, ap, ap_in, ap_line, gn_out, gn_in, gn_send,
    gn_ret, apall_in, upr, dnr, upf, dnf, ss, rs, ls,
):
    me = Place(inner)
    x, c, l, y, q, own = me.x, me.c, me.l, me.y, me.q, me.own
    nx, nc, ny = 1 - x, 1 - c, 1 - y
    devices = [me.at(c=nc), me.at(x=nx), me.at(x=nx, c=nc), me.at(y=ny), me.at(x=nx, y=ny)]
    greet(me, devices, True)
    S_LINE, S_ATT, S_WO, S_AY, S_AL, S_GN, S_AA, S_GP = 0, 32, 35, 38, 42, 50, 54, 60
    R_LINE, R_ATT, R_WO, R_AY, R_AL, R_GN, R_AA, R_GP = 0, 32, 35, 38, 42, 50, 54, 60
    kinds = ((gup, upr, upf, gup_all), (gdn, dnr, dnf, gdn_all))

    def line_copy(d, z, yy, n, src, device, last):
        k = ((d * 4 + z) * 2 + yy) * 2 + n
        slot = 8 + yy if last and d == 1 else 2 * z + yy
        return remote(src, kinds[n][1].at[slot], ss.at[S_LINE + k], rs.at[R_LINE + k], device)

    def first_sends(d, order, device):
        for z in order:
            for yy in range(2):
                for n in range(2):
                    line_copy(d, z, yy, n, kinds[n][0].at[2 * z + yy], device, z == order[2]).start()

    @pl.when(l == 0)
    def _():
        first_sends(0, (3, 2, 1), me.at(l=l + 1))

    @pl.when(l == LINE - 1)
    def _():
        first_sends(1, (0, 1, 2), me.at(l=l - 1))

    def add_own(n, slot):
        own_ref, ring = kinds[n][0], kinds[n][1]
        rows = own_ref.shape[1]

        @pl.loop(0, rows // 16)
        def _(r):
            part = pl.ds(pl.multiple_of(r * 16, 16), 16)
            total = own_ref[slot, part, :].astype(F32) + ring[slot, part, :].astype(F32)
            ring[slot, part, :] = total.astype(BF)

    def line_step(t):
        for d in range(2):
            far = l if d == 0 else LINE - 1 - l
            z = 3 + l - t if d == 0 else t - 3 + l

            @pl.when((far >= 1) & (far <= t))
            def _():
                device = me.at(l=l + 1) if d == 0 else me.at(l=l - 1)
                for yy in range(2):
                    for n in range(2):
                        slot = 2 * z + yy
                        ring = kinds[n][1]
                        line_copy(d, z, yy, n, ring.at[slot], me.at(y=ny), t == 3).wait_recv()
                        if t < 3:
                            add_own(n, slot)
                            line_copy(d, z, yy, n, ring.at[slot], device, t == 2).start()

    grad_att = mm_nt(gbranch[...], wo[...])
    half = TOK // 2
    for part in range(4):
        cols = grad_att[:, 192 * part:192 * (part + 1)]
        pk[part, 0:TOK, :] = cols[:, :128].astype(BF)
        low = cols[:, 128:]
        pk[part, TOK:ATT, :] = jnp.concatenate([low[:half], low[half:]], axis=1).astype(BF)
    got[q] = pk[q]

    def att_copy(k, to, frm, device):
        return remote(pk.at[to], got.at[frm], ss.at[S_ATT + k], rs.at[R_ATT + k], device)

    others = [(2 * nx + c, me.at(x=nx)), (2 * nx + nc, me.at(x=nx, c=nc)), (2 * x + nc, me.at(c=nc))]
    for k, (other, device) in enumerate(others):
        att_copy(k, other, q, device).start()

    grad_wo = mm_tn(attended[...], gbranch[...]).astype(BF)
    for s in range(OUTER):
        for t in range(6):
            tile = grad_wo[96 * s:96 * (s + 1), 128 * t:128 * (t + 1)]
            wo_out[s, 96 * t:96 * (t + 1), :] = tile

    def wo_rows(part):
        return pl.ds(pl.multiple_of(part * O_ROWS, O_ROWS), O_ROWS)

    def wo_copy(k, to, frm, device):
        return remote(
            wo_out.at[:, wo_rows(to), :], wo_in.at[frm], ss.at[S_WO + k], rs.at[R_WO + k], device
        )

    for k, (other, device) in enumerate(others):
        wo_copy(k, other, q, device).start()

    for h in range(LOCAL_HEADS):
        kt[h] = jnp.transpose(ks[h].astype(F32)).astype(BF)
    for s in range(OUTER):
        for t in range(5):
            wall[96 * s:96 * (s + 1), 128 * t:128 * (t + 1)] = packs[s, 96 * t:96 * (t + 1), :]

    for k, (other, device) in enumerate(others):
        att_copy(k, q, other, device).wait_recv()
    for part in range(4):
        rows = slice(part * TOK, (part + 1) * TOK)
        both = got[part, 0:TOK, :]
        low = got[part, TOK:ATT, :]
        grad[0, rows, :] = both[:, :64]
        grad[1, rows, :] = both[:, 64:]
        grad[2, rows, :] = jnp.concatenate([low[:, :64], low[:, 64:]], axis=0)
    for h in range(LOCAL_HEADS):
        dots = jnp.sum(grad[h].astype(F32) * ohead[h], axis=1, keepdims=True)
        delta[h] = jnp.transpose(jnp.broadcast_to(dots, (STREAM, 128)))[0:8, :]

    block = 256

    def one_head(h):
        dk_sum[...] = jnp.zeros((STREAM, 64), F32)
        dv_sum[...] = jnp.zeros((STREAM, 64), F32)
        for b in range(STREAM // block):
            first, last = b * block, (b + 1) * block
            q_rows, g_rows = qs[h, first:last, :], grad[h, first:last, :]
            scores = mm_nt(ks[h, 0:last, :], q_rows)
            key = lax.broadcasted_iota(jnp.int32, (last, block), 0)
            col = lax.broadcasted_iota(jnp.int32, (last, block), 1) + first
            seen = (key >= begin[0:1, first:last]) & (key <= col)
            probs = jnp.exp(jnp.where(seen, scores, NEGATIVE) - lse[h, 0:1, first:last])
            grad_probs = mm_nt(vs[h, 0:last, :], g_rows)
            grad_scores = (probs * (grad_probs - delta[h, 0:1, first:last])).astype(BF)
            dv_sum[0:last, :] += mm(probs.astype(BF), g_rows)
            dk_sum[0:last, :] += mm(grad_scores, q_rows)
            dq[h, first:last, :] = (jnp.transpose(mm(kt[h, :, 0:last], grad_scores)) * 0.125).astype(BF)
        dk[h] = dk_sum[...].astype(BF)
        dv[h] = dv_sum[...].astype(BF)

    pl.loop(0, 1)(one_head)
    line_step(1)
    pl.loop(1, LOCAL_HEADS)(one_head)
    line_step(2)

    for part in range(4):
        rows = slice(part * TOK, (part + 1) * TOK)
        cosine, sine = cos[rows, :], sin[rows, :]
        for h in range(LOCAL_HEADS):
            turned = jnp.concatenate([dq[h, rows, :], dk[h, rows, :]], axis=1)
            raw = turned.astype(F32) * cosine - mm(turned, turn[...]) * sine
            gr[rows, 128 * h:128 * (h + 1)] = raw.astype(BF)
        gr[rows, 384:512] = jnp.concatenate([dv[0, rows, :], dv[1, rows, :]], axis=1)
        gr[rows, 512:640] = jnp.concatenate([dv[2, rows, :], jnp.zeros((TOK, 64), BF)], axis=1)

    grad_a = mm_tn(normed[...], gr[...]).astype(BF)
    for s in range(OUTER):
        for t in range(5):
            ap[s, 96 * t:96 * (t + 1), :] = grad_a[96 * s:96 * (s + 1), 128 * t:128 * (t + 1)]
    for k, (other, device) in enumerate(others):
        wo_copy(k, q, other, device).wait_recv()
    wo_total = wo_out[:, wo_rows(q), :].astype(F32)
    for other, _ in others:
        wo_total = wo_total + wo_in[other].astype(F32)
    ap[:, A_ROWS:A_ROWS + O_ROWS, :] = wo_total.astype(BF)

    gain_sum = jnp.zeros((1, D), F32)
    for part in range(4):
        rows = slice(part * TOK, (part + 1) * TOK)
        grad_n = mm_nt(gr[rows, :], wall[...])
        values = stream[part].astype(F32)
        scale = lax.rsqrt(jnp.mean(values * values, axis=1, keepdims=True) + NORM_EPSILON)
        gain_sum = gain_sum + jnp.sum(grad_n * (values * scale), axis=0, keepdims=True)
        gn_out[part] = grad_n.astype(BF)

    def gn_swap(a):
        return remote(gn_out.at[2 * a + nc], gn_in.at[a], ss.at[S_GN + a], rs.at[R_GN + a], me.at(c=nc))

    for a in range(2):
        gn_swap(a).start()

    first_row = lax.broadcasted_iota(jnp.int32, (16, 1), 0) == 0
    small_all = small[...] + jnp.where(first_row, gain_sum, 0.0)
    for s in range(OUTER):
        piece = small_all[:, 96 * s:96 * (s + 1)]
        piece = jnp.concatenate([piece, jnp.zeros((16, 32), F32)], axis=1)
        ap[s, A_ROWS + O_ROWS:A_ROWS + O_ROWS + 16, :] = piece.astype(BF)

    def ay_copy(z):
        return remote(ap.at[2 * z + ny], ap_in.at[z], ss.at[S_AY + z], rs.at[R_AY + z], me.at(y=ny))

    for z in range(LINE):
        ay_copy(z).start()

    for a in range(2):
        gn_swap(a).wait_recv()
    for a in range(2):
        gn_send[a] = (gn_out[2 * a + c].astype(F32) + gn_in[a].astype(F32)).astype(BF)
    gn_over = remote(gn_send.at[nx], gn_ret, ss.at[S_GN + 2], rs.at[R_GN + 2], me.at(x=nx))
    gn_over.start()

    for z in range(LINE):
        ay_copy(z).wait_recv()
        ap_in[z] = (ap[2 * z + y].astype(F32) + ap_in[z].astype(F32)).astype(BF)

    def al_copy(d, z, src, device):
        k = 4 * d + z
        return remote(src, ap_line.at[d, z], ss.at[S_AL + k], rs.at[R_AL + k], device)

    @pl.when(l == 0)
    def _():
        for z in (3, 2, 1):
            al_copy(0, z, ap_in.at[z], me.at(l=l + 1)).start()

    @pl.when(l == LINE - 1)
    def _():
        for z in (0, 1, 2):
            al_copy(1, z, ap_in.at[z], me.at(l=l - 1)).start()

    for t in range(1, 4):
        for d in range(2):
            far = l if d == 0 else LINE - 1 - l
            z = 3 + l - t if d == 0 else t - 3 + l

            @pl.when((far >= 1) & (far <= t))
            def _():
                device = me.at(l=l + 1) if d == 0 else me.at(l=l - 1)
                al_copy(d, z, ap_line.at[d, z], me.at(y=ny)).wait_recv()
                if t < 3:
                    ap_line[d, z] = (ap_line[d, z].astype(F32) + ap_in[z].astype(F32)).astype(BF)
                    al_copy(d, z, ap_line.at[d, z], device).start()

    @pl.when(l == 0)
    def _():
        ap_line[0, l] = jnp.zeros((PACKG, 128), BF)

    @pl.when(l == LINE - 1)
    def _():
        ap_line[1, l] = jnp.zeros((PACKG, 128), BF)

    own_sum = ap_in[l].astype(F32) + ap_line[0, l].astype(F32) + ap_line[1, l].astype(F32)
    apack[q] = own_sum.astype(BF)

    def aa_copy(k, part, device):
        return remote(apack.at[part], apack.at[part], ss.at[S_AA + k], rs.at[R_AA + k], device)

    for k, (other, device) in enumerate(others):
        aa_copy(k, q, device).start()

    line_step(3)

    for n in range(2):
        own_ref, ring, fin, _ = kinds[n]
        rows = own_ref.shape[1]
        for yy in range(2):
            slot = 2 * l + yy

            @pl.loop(0, rows // 16)
            def _(r):
                part = pl.ds(pl.multiple_of(r * 16, 16), 16)
                up_sum = jnp.where(l >= 1, ring[slot, part, :].astype(F32), 0.0)
                dn_sum = jnp.where(l <= 2, ring[8 + yy, part, :].astype(F32), 0.0)
                total = own_ref[slot, part, :].astype(F32) + up_sum + dn_sum
                fin[yy, part, :] = total.astype(BF)

    chips = [(nx, y), (x, ny), (nx, ny)]
    mine = 2 * x + y

    def gp_copy(n, k, cx, cy):
        return remote(
            kinds[n][2].at[cy], kinds[n][3].at[2 * mine + c], ss.at[S_GP + 7 * n + k],
            rs.at[R_GP + 8 * n + 2 * mine + c], me.at(x=cx, y=cy)
        )

    def gp_wait(n, slot):
        ref = kinds[n][3]
        remote(ref.at[slot], ref.at[slot], ss.at[0], rs.at[R_GP + 8 * n + slot], me.at(c=nc)).wait_recv()

    def gp_own(n):
        return pltpu.make_async_copy(kinds[n][2].at[y], kinds[n][3].at[2 * mine + c], ls.at[n])

    def gp_core(n, k, slot, src=None):
        ref = kinds[n][3]
        return remote(
            ref.at[slot] if src is None else src, ref.at[slot], ss.at[S_GP + 7 * n + 3 + k], rs.at[R_GP + 8 * n + slot], me.at(c=nc)
        )

    for n in range(2):
        for k, (cx, cy) in enumerate(chips):
            gp_copy(n, k, cx, cy).start()
        gp_own(n).start()
        gp_core(n, 0, 2 * mine + c, kinds[n][2].at[y]).start()
    for n in range(2):
        for k, (cx, cy) in enumerate(chips):
            slot = 2 * (2 * cx + cy) + c
            gp_wait(n, slot)
            gp_core(n, 1 + k, slot).start()

    gn_over.wait_recv()
    gnorm_ret[...] = gn_send[x].astype(F32) + gn_ret[...].astype(F32)

    for n in range(2):
        for slot in range(4):
            gp_wait(n, 2 * slot + nc)
    for k, (other, device) in enumerate(others):
        aa_copy(k, other, device).wait_recv()

    for k, (other, device) in enumerate(others):
        att_copy(k, other, q, device).wait_send()
        wo_copy(k, other, q, device).wait_send()
        aa_copy(k, q, device).wait_send()
    for a in range(2):
        gn_swap(a).wait_send()
    gn_over.wait_send()
    for z in range(LINE):
        ay_copy(z).wait_send()
    for n in range(2):
        for k, (cx, cy) in enumerate(chips):
            gp_copy(n, k, cx, cy).wait_send()
            gp_core(n, 1 + k, 2 * (2 * cx + cy) + c).wait_send()
        gp_core(n, 0, 2 * mine + c, kinds[n][2].at[y]).wait_send()
        gp_own(n).wait()
    for d in range(2):
        for z in range(LINE):
            sent = (z > l) & (l < LINE - 1) if d == 0 else (z < l) & (l > 0)

            @pl.when(sent)
            def _():
                device = me.at(l=l + 1) if d == 0 else me.at(l=l - 1)
                al_copy(d, z, ap_line.at[d, z], device).wait_send()
                for yy in range(2):
                    for n in range(2):
                        line_copy(d, z, yy, n, kinds[n][1].at[2 * z + yy], device, False).wait_send()


PACKG = A_ROWS + O_ROWS + 16


def backward_call(inner, *args):
    vm = pl.BlockSpec(memory_space=pltpu.VMEM)
    heads = (LOCAL_HEADS, STREAM, 64)
    return pl.pallas_call(
        functools.partial(backward_kernel, inner),
        out_shape=[
            jax.ShapeDtypeStruct((TOK, D), F32),
            jax.ShapeDtypeStruct((4, PACKG, 128), BF),
            jax.ShapeDtypeStruct((8, 96, FF), BF),
            jax.ShapeDtypeStruct((8, 128, D), BF),
        ],
        in_specs=[vm] * len(args),
        out_specs=[vm] * 2 + [pl.BlockSpec(memory_space=pl.ANY)] * 2,
        scratch_shapes=[
            pltpu.VMEM((4, ATT, 128), BF),
            pltpu.VMEM((4, ATT, 128), BF),
            pltpu.VMEM((LOCAL_HEADS, 64, STREAM), BF),
            pltpu.VMEM(heads, BF),
            pltpu.VMEM(heads, BF),
            pltpu.VMEM(heads, BF),
            pltpu.VMEM(heads, BF),
            pltpu.VMEM((STREAM, 64), F32),
            pltpu.VMEM((STREAM, 64), F32),
            pltpu.VMEM((LOCAL_HEADS, 8, STREAM), F32),
            pltpu.VMEM((STREAM, 640), BF),
            pltpu.VMEM((D, 640), BF),
            pltpu.VMEM((OUTER, 576, 128), BF),
            pltpu.VMEM((4, OUTER, O_ROWS, 128), BF),
            pltpu.VMEM((OUTER, PACKG, 128), BF),
            pltpu.VMEM((LINE, PACKG, 128), BF),
            pltpu.VMEM((2, LINE, PACKG, 128), BF),
            pltpu.VMEM((4, TOK, D), BF),
            pltpu.VMEM((2, TOK, D), BF),
            pltpu.VMEM((2, TOK, D), BF),
            pltpu.VMEM((TOK, D), BF),
            pltpu.VMEM((8, 128), BF),
            pltpu.VMEM((10, 96, FF), BF),
            pltpu.VMEM((10, 128, D), BF),
            pltpu.VMEM((2, 96, FF), BF),
            pltpu.VMEM((2, 128, D), BF),
            pltpu.SemaphoreType.DMA((74,)),
            pltpu.SemaphoreType.DMA((76,)),
            pltpu.SemaphoreType.DMA((2,)),
        ],
        compiler_params=pltpu.CompilerParams(
            collective_id=2, has_side_effects=True, vmem_limit_bytes=57 * 2**20
        ),
        name="attend_back",
    )(*args)


def scatter_inner(values, axis, inner):
    if inner == 1:
        return values
    count = lax.axis_size("shard")
    groups = [[o * inner + i for i in range(inner)] for o in range(count // inner)]
    return lax.psum_scatter(
        values, "shard", scatter_dimension=axis, axis_index_groups=groups, tiled=True
    )


def norm_rows(values, gain_row):
    scale_rows = lax.rsqrt(jnp.mean(values * values, axis=-1, keepdims=True) + NORM_EPSILON)
    return values * scale_rows * gain_row, scale_rows


def norm_back(grad_rows, values, scale_rows, gain_row):
    normal_rows = values * scale_rows
    inner_term = grad_rows * gain_row
    return scale_rows * (
        inner_term - normal_rows * jnp.mean(inner_term * normal_rows, axis=-1, keepdims=True)
    )


def adam_update(weight, grad, first, second, rate, decay):
    first_new = MOMENT_DECAY * first + (1.0 - MOMENT_DECAY) * grad
    second_new = MOMENT_DECAY * second + (1.0 - MOMENT_DECAY) * grad * grad
    correction = 1.0 - MOMENT_DECAY**STEP
    update = first_new / correction / (jnp.sqrt(second_new / correction) + ADAM_EPSILON)
    return weight - rate * (update + decay * weight), first_new, second_new


def local(
    tokens, route_residual, doc_lengths, routes, priority, grad_out,
    attend_in, attend_in_first, attend_in_second,
    attend_out, attend_out_first, attend_out_second,
    expert_up, expert_up_first, expert_up_second,
    expert_down, expert_down_first, expert_down_second,
    router_mix, router_mix_first, router_mix_second,
    vectors, vectors_first, vectors_second,
):
    inner = lax.axis_size("shard") // OUTER
    q = lax.axis_index("seq")
    outer = lax.axis_index("shard") // inner
    x, c = q // 2, q % 2

    w_in = gather_inner(attend_in.astype(BF), 1, inner)
    w_out = gather_inner(attend_out.astype(BF), 0, inner)
    w_router = gather_inner(router_mix.astype(BF), 0, inner)
    w_vectors = gather_inner(vectors.astype(BF), 1, inner)
    pack = pack_attention(w_in, w_out, w_router, w_vectors, q, outer)
    if inner == 1:
        ups, downs = expert_pieces(expert_up, expert_down, x, c)
    else:
        ups, downs = expert_pieces(
            gather_inner(expert_up.astype(BF), 1, inner), gather_inner(expert_down.astype(BF), 1, inner), x, c
        )
    cosine, sine, turn = rope_constants(STREAM)
    cosine, sine, turn = jnp.asarray(cosine), jnp.asarray(sine), jnp.asarray(turn, BF)
    ids = jnp.arange(STREAM, dtype=jnp.int32)
    starts = jnp.cumsum(doc_lengths[0]) - doc_lengths[0]
    begin = jnp.max(jnp.where(starts[None, :] <= ids[:, None], starts[None, :], 0), axis=1).astype(jnp.int32)

    stream, packs, _, wup, wdn, normed, qs, ks, vs, ohead, lse, attended, branch, wo = forward_call(
        inner, tokens[0], pack, ups, downs, cosine, sine, begin[:, None], turn
    )

    smalls = jnp.sum(packs[:, A_ROWS + O_ROWS:].astype(F32), axis=0)
    smalls = smalls.reshape(6, 16, 128).transpose(1, 0, 2).reshape(16, D)
    vector_rows, router_rows = smalls[:4], smalls[4:]
    residual_in = tokens[0].astype(F32)
    middle = residual_in + branch
    hidden, scale_two = norm_rows(middle, vector_rows[1])
    hidden_low = hidden.astype(BF)
    hidden_val = hidden_low.astype(F32)
    logits = mm_nt(hidden_low, router_rows.astype(BF))
    route_ids = routes[0]
    route_logits = logits[:, :NEXP] + route_residual[0]
    onehot = (route_ids[:, :, None] == jnp.arange(NEXP, dtype=jnp.int32)[None, None, :]).astype(F32)
    picked = jnp.sum(onehot * route_logits[:, None, :], axis=2)
    gates = jax.nn.softmax(picked, axis=-1)
    coefficient = jax.nn.softmax(logits[:, NEXP:].reshape(TOK, 2, 2), axis=-1)
    expert_id = route_ids.T.reshape(-1)
    order_key = (jnp.arange(TOPK, dtype=jnp.int32)[:, None] * STREAM + priority[0][None, :]).reshape(-1)
    earlier = (expert_id[:, None] == expert_id[None, :]) & (order_key[None, :] < order_key[:, None])
    slot_rank = jnp.sum(earlier.astype(jnp.int32), axis=1)
    kept_pair = (expert_id < NFFN) & (slot_rank < CAP)
    flat_slot = jnp.where(kept_pair, expert_id * CAP + slot_rank, -1)
    slots = jnp.arange(NFFN * CAP, dtype=jnp.int32)
    maps = [(slots[:, None] == flat_slot[None, k * TOK:(k + 1) * TOK]).astype(BF) for k in range(TOPK)]
    both_map = maps[0] + maps[1]
    grad_top = grad_out[0].astype(F32)
    bufh = mm(both_map, hidden_low).astype(BF).reshape(NFFN, CAP, D)
    bufg = sum(mm(maps[k], (gates[:, k:k + 1] * grad_top).astype(BF)) for k in range(TOPK))
    bufg = bufg.astype(BF).reshape(NFFN, CAP, D)

    down_ret, gbuf_ret, gup, gdn = expert_call(inner, bufh, bufg, wup, wdn)

    down_rows = down_ret.reshape(NFFN * CAP, D)
    grad_buffer = gbuf_ret.reshape(NFFN * CAP, D)
    consts = [
        coefficient[:, j, 0:1] * hidden_val + coefficient[:, j, 1:2] * vector_rows[2 + j][None, :] for j in range(2)
    ]
    values = []
    for k in range(TOPK):
        column = route_ids[:, k:k + 1]
        value = mm_tn(maps[k], down_rows)
        value = jnp.where(column == NFFN + 1, hidden_val, value)
        for j in range(2):
            value = jnp.where(column == NFFN + 2 + j, consts[j], value)
        values.append(value)
    layer_out = (middle + gates[:, 0:1] * values[0] + gates[:, 1:2] * values[1]).astype(BF)
    grad_gate = jnp.stack([jnp.sum(grad_top * value, axis=1) for value in values], axis=1)
    grad_pick = gates * (grad_gate - jnp.sum(gates * grad_gate, axis=1, keepdims=True))
    grad_route = jnp.sum(onehot * grad_pick[:, :, None], axis=1)
    g_hidden = jnp.sum(grad_top * hidden_val, axis=1)
    direct = jnp.sum(gates * (route_ids == NFFN + 1).astype(F32), axis=1)
    grad_mix = []
    grad_vec = []
    for j in range(2):
        weight = jnp.sum(gates * (route_ids == NFFN + 2 + j).astype(F32), axis=1)
        coef = coefficient[:, j]
        direct = direct + weight * coef[:, 0]
        grad_coef = jnp.stack(
            [weight * g_hidden, weight * jnp.sum(grad_top * vector_rows[2 + j][None, :], axis=1)], axis=1
        )
        grad_mix.append(coef * (grad_coef - jnp.sum(coef * grad_coef, axis=1, keepdims=True)))
        grad_vec.append(jnp.sum((weight * coef[:, 1])[:, None] * grad_top, axis=0))
    grad_logits = jnp.concatenate([grad_route, grad_mix[0], grad_mix[1]], axis=1)
    grad_hidden = direct[:, None] * grad_top + mm_tn(both_map, grad_buffer)
    grad_hidden = grad_hidden + jnp.dot(grad_logits, router_rows, precision=lax.Precision.HIGHEST)
    grad_router = jnp.einsum("te,td->ed", grad_logits, hidden_val, precision=lax.Precision.HIGHEST)
    grad_gain_two = jnp.sum(grad_hidden * (middle * scale_two), axis=0)
    grad_middle = grad_top + norm_back(grad_hidden, middle, scale_two, vector_rows[1])
    small = jnp.concatenate(
        [jnp.stack([jnp.zeros_like(grad_gain_two), grad_gain_two, grad_vec[0], grad_vec[1]]), grad_router], axis=0
    )

    grad_normed, apack, gup_all, gdn_all = backward_call(
        inner,
        grad_middle.astype(BF), attended, wo, qs, ks, vs, ohead, lse, jnp.broadcast_to(begin[None, :], (8, STREAM)),
        cosine, sine, turn, normed, packs, stream, small, gup, gdn,
    )

    scale_one = lax.rsqrt(jnp.mean(residual_in * residual_in, axis=-1, keepdims=True) + NORM_EPSILON)
    grad_tokens = grad_middle + norm_back(grad_normed, residual_in, scale_one, vector_rows[0])

    tiles = apack[:, :A_ROWS].reshape(4, 5, 96, 128)
    heads = [
        tiles[:, 0:3, :, :64].transpose(2, 0, 1, 3),
        tiles[:, 0:3, :, 64:].transpose(2, 0, 1, 3),
        jnp.stack([tiles[:, 3, :, :64], tiles[:, 3, :, 64:], tiles[:, 4, :, :64]], axis=1).transpose(2, 0, 1, 3),
    ]
    g_in = jnp.stack([head.reshape(96, D) for head in heads])
    g_out = apack[:, A_ROWS:A_ROWS + O_ROWS].reshape(6, 96, 128).transpose(1, 0, 2).reshape(96, D)
    g_small = jnp.sum(apack[:, A_ROWS + O_ROWS:, :96].astype(F32), axis=0)
    g_up = gup_all.reshape(NFFN, 2, 96, 2, 8, 128).transpose(0, 2, 3, 4, 1, 5).reshape(NFFN, 96, 2 * FF)
    g_down = gdn_all.reshape(NFFN, 256, D)
    grads = (
        scatter_inner(g_in.astype(F32), 1, inner),
        scatter_inner(g_out.astype(F32), 0, inner),
        scatter_inner(g_up.astype(F32), 1, inner),
        scatter_inner(g_down.astype(F32), 1, inner),
        scatter_inner(g_small[4:].T, 0, inner),
        scatter_inner(g_small[:4], 1, inner),
    )
    states = (
        (attend_in, attend_in_first, attend_in_second),
        (attend_out, attend_out_first, attend_out_second),
        (expert_up, expert_up_first, expert_up_second),
        (expert_down, expert_down_first, expert_down_second),
        (router_mix, router_mix_first, router_mix_second),
        (vectors, vectors_first, vectors_second),
    )
    results = []
    for kind, (weight, first, second) in enumerate(states):
        results.extend(adam_update(weight, grads[kind], first, second, STEP_RATES[kind], STEP_DECAYS[kind]))
    return (layer_out[None], grad_tokens[None], grad_route[None], *results)


def solution(mesh):
    token = P("shard", "seq", None)
    middle = P(None, "shard", None)
    front = P("shard", None)
    back = P(None, "shard")
    weights = (middle,) * 3 + (front,) * 3 + (middle,) * 6 + (front,) * 3 + (back,) * 3
    return jax.shard_map(
        local,
        mesh=mesh,
        in_specs=(token, token, front, token, P("shard", "seq"), token) + weights,
        out_specs=(token, token, token) + weights,
        check_vma=False,
    )
```

```python
import functools

import jax
import jax.numpy as jnp
import numpy as np
from jax import lax
from jax.experimental import pallas as pl
from jax.experimental.pallas import tpu as pltpu
from jax.sharding import PartitionSpec as P

D = 768
HEADS = 12
HEAD_DIM = 64
FF = 2048
NFFN = 4
NEXP = 8
TOPK = 2
STEP = 5
CAP = 96
LINE = 4
OUTER = 8
LOCAL_HEADS = 3

NORM_EPSILON = 1e-05
ROPE_BASE = 10000.0
NEGATIVE = -1e30
MOMENT_DECAY = 0.5
ADAM_EPSILON = 1e-08
STEP_RATES = (0.04, 0.1, 0.04, 0.02, 0.02, 0.2)
STEP_DECAYS = (0.1, 0.1, 0.1, 0.1, 0.1, 0.0)
BF = jnp.bfloat16
F32 = jnp.float32
MESH = pl.DeviceIdType.MESH
VMEM_LIMIT = 58 * 2**20


def mm(left, right):
    return jnp.dot(left, right, preferred_element_type=F32)


def mm_nt(left, right):
    return lax.dot_general(left, right, (((1,), (1,)), ((), ())), preferred_element_type=F32)


def mm_tn(left, right):
    return lax.dot_general(left, right, (((0,), (0,)), ((), ())), preferred_element_type=F32)


class Place:
    def __init__(self, inner):
        q = lax.axis_index("seq")
        shard = lax.axis_index("shard")
        self.inner = inner
        self.rest = lax.rem(shard, inner) if inner > 1 else 0
        outer = lax.div(shard, inner) if inner > 1 else shard
        self.q = q
        self.x = lax.div(q, 2)
        self.c = lax.rem(q, 2)
        self.l = lax.div(outer, 2)
        self.y = lax.rem(outer, 2)
        self.own = outer

    def at(self, x=None, c=None, l=None, y=None):
        x = self.x if x is None else x
        c = self.c if c is None else c
        l = self.l if l is None else l
        y = self.y if y is None else y
        return (2 * x + c, (2 * l + y) * self.inner + self.rest)


def greet(me, devices, line):
    barrier = pltpu.get_barrier_semaphore()
    for device in devices:
        pl.semaphore_signal(barrier, inc=1, device_id=device, device_id_type=MESH)
    if not line:
        pl.semaphore_wait(barrier, len(devices))
        return

    @pl.when(me.l > 0)
    def _():
        pl.semaphore_signal(barrier, inc=1, device_id=me.at(l=me.l - 1), device_id_type=MESH)

    @pl.when(me.l < LINE - 1)
    def _():
        pl.semaphore_signal(barrier, inc=1, device_id=me.at(l=me.l + 1), device_id_type=MESH)

    near = jnp.minimum(me.l, 1) + jnp.minimum(LINE - 1 - me.l, 1)
    pl.semaphore_wait(barrier, len(devices) + near)


def remote(src, dst, send, recv, device):
    return pltpu.make_async_remote_copy(
        src_ref=src, dst_ref=dst, send_sem=send, recv_sem=recv, device_id=device, device_id_type=MESH
    )


def rope_constants(stream_len):
    frequency = ROPE_BASE ** (-(np.arange(HEAD_DIM // 2, dtype=np.float64) * 2.0 / HEAD_DIM))
    angles = np.arange(stream_len, dtype=np.float64)[:, None] * frequency[None, :]
    cosine = np.tile(np.cos(angles), (1, 4)).astype(np.float32)
    sine = np.tile(np.sin(angles), (1, 4)).astype(np.float32)
    turn = np.zeros((128, 128), np.float32)
    for j in range(128):
        if j % 64 < 32:
            turn[j + 32, j] = -1.0
        else:
            turn[j - 32, j] = 1.0
    return cosine, sine, turn


A_ROWS = 5 * 96
O_ROWS = 144
S_ROWS = 96
PACK = A_ROWS + O_ROWS + S_ROWS
PACKG = A_ROWS + O_ROWS + 16
TOK = 384
STREAM = 1536
ATT = 576
HALF = TOK // 2
BLOCK = 256
KEYS = 512
ROWS = 128


class Counter:
    def __init__(self):
        self.used = 0

    def take(self, count):
        first = self.used
        self.used += count
        return first


def semaphores():
    s, r = Counter(), Counter()
    send = {
        "tok": s.take(3), "pack": s.take(12), "wo": s.take(3), "ex": s.take(34), "att": s.take(3),
        "row": s.take(6), "core": s.take(8), "part": s.take(2), "back": s.take(6),
        "line": s.take(32), "att2": s.take(3), "wo2": s.take(3), "ay": s.take(4), "al": s.take(8), "gn": s.take(3),
        "aa": s.take(3), "gp": s.take(14),
    }
    recv = {
        "tok": r.take(3), "pack": r.take(8), "wo": r.take(3), "ex": r.take(16), "att": r.take(3),
        "row": r.take(8), "core": r.take(8), "part": r.take(2), "back": r.take(8),
        "line": r.take(32), "att2": r.take(3), "wo2": r.take(3), "ay": r.take(4), "al": r.take(8), "gn": r.take(3),
        "aa": r.take(3), "gp": r.take(16),
    }
    return send, recv, s.used, r.used


def small_rows(packs):
    tiles = []
    for t in range(6):
        first = A_ROWS + O_ROWS + 16 * t
        total = packs[0, first:first + 16, :].astype(F32)
        for s in range(1, OUTER):
            total = total + packs[s, first:first + 16, :].astype(F32)
        tiles.append(total)
    return jnp.concatenate(tiles, axis=1)


def split_low(values):
    high = values.astype(BF)
    return high, (values - high.astype(F32)).astype(BF)


def layer_kernel(
    inner,
    tok, gout_in, w_in, w_out, w_up, w_dn, cos_in, sin_in, turn, lengths, routes, residual, priority, router, vectors,
    layer_out, gtokens, groute, apack, gup_all, gdn_all,
    stream, packs, wo_all, wo, wup, wdn, ringx_up, ringx_dn, gup, gdn, rowh, rowg, part_in, ret, got, wo_in,
    ap_in, ap_line, gn_ret, normed, qk, vo, ks, lse, attended, hidden, cos, sin, gout, bufs, begin,
    cols, facts, ss, rs, ls, ready,
):
    me = Place(inner)
    x, c, l, y, q, own = me.x, me.c, me.l, me.y, me.q, me.own
    nx, nc, ny = 1 - x, 1 - c, 1 - y
    mine = 2 * x + y
    S, R, _, _ = semaphores()
    chips = [(x, ny), (nx, y), (nx, ny)]
    others = [(2 * nx + c, me.at(x=nx)), (2 * nx + nc, me.at(x=nx, c=nc)), (2 * x + nc, me.at(c=nc))]

    def load(src, dst, k):
        return pltpu.make_async_copy(src, dst, ls.at[k])

    def tok_copy(k, part, device):
        return remote(stream.at[part], stream.at[part], ss.at[S["tok"] + k], rs.at[R["tok"] + k], device)

    def pack_copy(kind, z, device):
        slot = 2 * z + y
        return remote(
            packs.at[slot], packs.at[slot], ss.at[S["pack"] + 4 * kind + z], rs.at[R["pack"] + slot], device
        )

    def pack_wait(slot):
        remote(packs.at[slot], packs.at[slot], ss.at[0], rs.at[R["pack"] + slot], me.at(y=ny)).wait_recv()

    def pack_up(z):
        @pl.when(l < LINE - 1)
        def _():
            pack_copy(0, z, me.at(l=l + 1)).start()

    def pack_down(z):
        @pl.when(l > 0)
        def _():
            pack_copy(1, z, me.at(l=l - 1)).start()

    def pack_over(z):
        pack_copy(2, z, me.at(y=ny)).start()

    def pack_step(step):
        @pl.when(l - step >= 0)
        def _():
            pack_wait(2 * (l - step) + y)
            pack_up(l - step)
            pack_over(l - step)

        @pl.when(l + step < LINE)
        def _():
            pack_wait(2 * (l + step) + y)
            pack_down(l + step)
            pack_over(l + step)

    weights = (wup, wdn)

    def ex_copy(kind, n, z, yy, device):
        slot = 2 * z + yy
        k = 2 * (8 * kind + slot) + n
        ref = weights[n]
        return remote(ref.at[slot], ref.at[slot], ss.at[S["ex"] + k], rs.at[R["ex"] + 2 * slot + n], device)

    def ex_wait(slot):
        for n, ref in enumerate(weights):
            remote(ref.at[slot], ref.at[slot], ss.at[0], rs.at[R["ex"] + 2 * slot + n], me.at(y=ny)).wait_recv()

    def ex_forward(z, yy, upward, kinds=(0, 1)):
        if upward:
            @pl.when(l < LINE - 1)
            def _():
                for n in kinds:
                    ex_copy(0, n, z, yy, me.at(l=l + 1)).start()
        else:
            @pl.when(l > 0)
            def _():
                for n in kinds:
                    ex_copy(1, n, z, yy, me.at(l=l - 1)).start()

    def relay(step, yy):
        @pl.when(l - step >= 0)
        def _():
            ex_wait(2 * (l - step) + yy)
            ex_forward(l - step, yy, True)

        @pl.when(l + step < LINE)
        def _():
            ex_wait(2 * (l + step) + yy)
            ex_forward(l + step, yy, False)

    def wo_copy(k, part, device):
        rows = pl.ds(pl.multiple_of(part * O_ROWS, O_ROWS), O_ROWS)
        return remote(
            wo_all.at[:, rows, :], wo_all.at[:, rows, :], ss.at[S["wo"] + k], rs.at[R["wo"] + k], device
        )

    def row_copy(n, k, cx, cy):
        row = (rowh, rowg)[n]
        return remote(
            bufs.at[n, 2 * cx + cy], row.at[4 * c + mine], ss.at[S["row"] + 3 * n + k], rs.at[R["row"] + 4 * n + mine],
            me.at(x=cx, y=cy)
        )

    def row_wait(n, cx, cy):
        row, slot = (rowh, rowg)[n], 2 * cx + cy
        remote(
            row.at[4 * c + slot], row.at[4 * c + slot], ss.at[0], rs.at[R["row"] + 4 * n + slot], me.at(x=cx, y=cy)
        ).wait_recv()

    def core_copy(n, k, first, slot):
        row = (rowh, rowg)[n]
        return remote(
            row.at[first + slot], row.at[first + slot], ss.at[S["core"] + 4 * n + k], rs.at[R["core"] + 4 * n + slot],
            me.at(c=nc)
        )

    def row_send(n):
        for k, (cx, cy) in enumerate(chips):
            row_copy(n, k, cx, cy).start()
        (rowh, rowg)[n][4 * c + mine] = bufs[n, mine]
        core_copy(n, 0, 4 * c, mine).start()

    def row_pass(n):
        for k, (cx, cy) in enumerate(chips):
            row_wait(n, cx, cy)
            core_copy(n, 1 + k, 4 * c, 2 * cx + cy).start()

    def row_collect(n):
        for slot in range(4):
            core_copy(n, 0, 4 * nc, slot).wait_recv()

    def back_copy(n, k, cx, cy):
        return remote(
            bufs.at[n, 2 * cx + cy], ret.at[n, mine], ss.at[S["back"] + 3 * n + k], rs.at[R["back"] + 4 * n + mine],
            me.at(x=cx, y=cy)
        )

    def back_wait(n, cx, cy):
        slot = 2 * cx + cy
        remote(
            ret.at[n, slot], ret.at[n, slot], ss.at[0], rs.at[R["back"] + 4 * n + slot], me.at(x=cx, y=cy)
        ).wait_recv()

    loads = [
        load(tok, stream.at[q], 0), load(cos_in, cos, 1), load(sin_in, sin, 2), load(gout_in, gout, 3),
    ]
    for copy in loads:
        copy.start()

    def forward(st_in, st_out, st_up, st_dn, upx, dnx, wo_tiles, wq, wr, pk, begin_col):
        from_hbm = [load(w_in, st_in, 4), load(w_out, st_out, 5)]
        experts = [2 * x + y, 2 * x + ny]
        from_hbm += [load(w_up.at[e], st_up.at[k], 6 + k) for k, e in enumerate(experts)]
        half_rows = pl.ds(pl.multiple_of(128 * c, 128), 128)
        from_hbm += [load(w_dn.at[e, half_rows, :], st_dn.at[k], 8 + k) for k, e in enumerate(experts)]
        for copy in from_hbm:
            copy.start()
        greet(me, [me.at(c=nc), me.at(x=nx), me.at(x=nx, c=nc), me.at(y=ny), me.at(x=nx, y=ny)], True)
        loads[0].wait()
        tok_copy(1, q, me.at(x=nx)).start()
        tok_copy(0, q, me.at(c=nc)).start()

        from_hbm[0].wait()
        from_hbm[1].wait()
        for t in range(6):
            wo_tiles[96 * t:96 * (t + 1), :] = st_out[:, 128 * t:128 * (t + 1)].astype(BF)
        for part in range(4):

            @pl.when(q == part)
            def _():
                def head(kind, h):
                    first = 192 * part + 64 * h
                    return st_in[kind, :, first:first + 64]

                tiles = [(head(0, h), head(1, h)) for h in range(LOCAL_HEADS)]
                tiles += [(head(2, 0), head(2, 1)), (head(2, 2), jnp.zeros((96, 64), F32))]
                for t, pair in enumerate(tiles):
                    packs[own, 96 * t:96 * (t + 1), :] = jnp.concatenate(pair, axis=1).astype(BF)

        rows = pl.ds(pl.multiple_of(q * O_ROWS, O_ROWS), O_ROWS)
        packs[own, A_ROWS:A_ROWS + O_ROWS, :] = wo_tiles[rows, :]
        small = jnp.concatenate([router[...], vectors[...]], axis=0)
        small = jnp.concatenate([small, jnp.zeros((16, 32), F32)], axis=1).astype(BF)
        to_col = lax.broadcasted_iota(jnp.int32, (128, D), 1) - 96 * own
        from_row = lax.broadcasted_iota(jnp.int32, (128, D), 0)
        place = ((to_col == from_row) & (from_row < 96)).astype(F32).astype(BF)
        placed = mm(small, place).astype(BF)
        for t in range(6):
            first = A_ROWS + O_ROWS + 16 * t
            packs[own, first:first + 16, :] = placed[:, 128 * t:128 * (t + 1)]
        pack_up(l)
        pack_down(l)
        pack_over(l)

        for k in range(2):
            from_hbm[4 + k].wait()
        wdn[own] = st_dn[0].astype(BF)
        ex_forward(l, y, True, (1,))
        ex_forward(l, y, False, (1,))
        dnx[...] = st_dn[1].astype(BF)
        for k in range(2):
            from_hbm[2 + k].wait()
        for j in range(16):
            part = pl.ds(pl.multiple_of(256 * j + 128 * c, 128), 128)
            wup[own, :, 128 * j:128 * (j + 1)] = st_up[0, :, part].astype(BF)
            upx[:, 128 * j:128 * (j + 1)] = st_up[1, :, part].astype(BF)

        pack_step(1)
        pack_step(2)
        tok_copy(1, 2 * nx + c, me.at(x=nx)).wait_recv()
        tok_copy(2, 2 * nx + c, me.at(c=nc)).start()
        pack_step(3)
        ex_forward(l, y, True, (0,))
        ex_forward(l, y, False, (0,))

        def ex_over(n):
            return remote(
                (upx, dnx)[n], weights[n].at[own], ss.at[S["ex"] + 32 + n], rs.at[R["ex"] + 2 * own + n], me.at(y=ny)
            )

        for n in range(2):
            ex_over(n).start()

        ids = lax.broadcasted_iota(jnp.int32, (8, STREAM), 1)
        first = lengths[0, 0] * 0
        at = jnp.zeros((8, STREAM), jnp.int32)
        for k in range(8):
            at = jnp.maximum(at, jnp.where(ids >= first, first, 0))
            first = first + lengths[0, k]
        begin[...] = at
        begin_col[...] = jnp.transpose(jnp.broadcast_to(at[0:1].astype(F32), (128, STREAM)))

        for z in range(LINE):
            pack_wait(2 * z + ny)
        wo_all[:, rows, :] = packs[:, A_ROWS:A_ROWS + O_ROWS, :]
        wo_copy(1, q, me.at(x=nx)).start()
        wo_copy(0, q, me.at(c=nc)).start()
        for s in range(OUTER):
            for t in range(5):
                wq[t, 96 * s:96 * (s + 1), :] = packs[s, 96 * t:96 * (t + 1), :]
        for t in range(LOCAL_HEADS):
            wr[t] = mm(wq[t], turn[...]).astype(BF)
        gain = small_rows(packs)[12:13]
        tok_copy(0, 2 * x + nc, me.at(c=nc)).wait_recv()
        tok_copy(2, 2 * nx + nc, me.at(c=nc)).wait_recv()
        loads[1].wait()
        loads[2].wait()

        halves = jnp.where(lax.broadcasted_iota(jnp.int32, (1, 128), 1) < 64, 0.125, 1.0)

        @pl.loop(0, 4)
        def _(part):
            values = stream[part].astype(F32)
            scale = lax.rsqrt(jnp.mean(values * values, axis=1, keepdims=True) + NORM_EPSILON)
            rows = pl.ds(pl.multiple_of(part * TOK, TOK), TOK)
            low = (values * scale * gain).astype(BF)
            normed[rows, :] = low
            cosine, sine = cos[rows, :], sin[rows, :]
            for h in range(LOCAL_HEADS):
                turned = mm(low, wq[h]) * cosine + mm(low, wr[h]) * sine
                qk[h, rows, :] = (turned * halves).astype(BF)
            both = mm(low, wq[3]).astype(BF)
            vo[0, rows, 0:64] = both[:, :64]
            vo[1, rows, 0:64] = both[:, 64:]
            vo[2, rows, 0:64] = mm(low, wq[4])[:, :64].astype(BF)

        ex_wait(2 * l + ny)
        ex_forward(l, ny, True)
        ex_forward(l, ny, False)

        def one_head(h):
            ks[...] = qk[h, :, 64:128]
            for b in range(STREAM // BLOCK):
                first, last = b * BLOCK, (b + 1) * BLOCK
                scores = mm_nt(qk[h, first:last, 0:64], ks[0:last, :])
                col = lax.broadcasted_iota(jnp.int32, (BLOCK, last), 1)
                row = lax.broadcasted_iota(jnp.int32, (BLOCK, last), 0) + first
                starts = begin_col[first:last, 0:1].astype(jnp.int32)
                scores = jnp.where((col >= starts) & (col <= row), scores, NEGATIVE)
                top = jnp.max(scores, axis=1, keepdims=True)
                weight = jnp.exp(scores - top)
                total = jnp.sum(weight, axis=1, keepdims=True)
                vo[h, first:last, 64:128] = (mm(weight.astype(BF), vo[h, 0:last, 0:64]) / total).astype(BF)
                logs = jnp.broadcast_to(top + jnp.log(total), (BLOCK, 128))
                lse[h, :, first:last] = jnp.transpose(logs)[0:8, :]

        pl.loop(0, 1)(one_head)
        wo_copy(1, 2 * nx + c, me.at(x=nx)).wait_recv()
        wo_copy(2, 2 * nx + c, me.at(c=nc)).start()
        relay(1, y)
        pl.loop(1, LOCAL_HEADS)(one_head)

        for part in range(4):
            rows = slice(part * TOK, (part + 1) * TOK)
            pk[part, 0:TOK, :] = jnp.concatenate([vo[0, rows, 64:128], vo[1, rows, 64:128]], axis=1)
            third = [vo[2, part * TOK + k * HALF:part * TOK + (k + 1) * HALF, 64:128] for k in range(2)]
            pk[part, TOK:ATT, :] = jnp.concatenate(third, axis=1)
        got[q] = pk[q]

        def att_copy(k, to, frm, device):
            return remote(pk.at[to], got.at[frm], ss.at[S["att"] + k], rs.at[R["att"] + k], device)

        for k, (other, device) in enumerate(others):
            att_copy(k, other, q, device).start()
        relay(1, ny)

        wo_copy(0, 2 * x + nc, me.at(c=nc)).wait_recv()
        wo_copy(2, 2 * nx + nc, me.at(c=nc)).wait_recv()
        for s in range(OUTER):
            for t in range(6):
                wo[96 * s:96 * (s + 1), 128 * t:128 * (t + 1)] = wo_all[s, 96 * t:96 * (t + 1), :]
        for k, (other, device) in enumerate(others):
            att_copy(k, q, other, device).wait_recv()
        pieces = []
        for part in range(4):
            low = got[part, TOK:ATT, :]
            pieces.append(got[part, 0:TOK, :])
            pieces.append(jnp.concatenate([low[:, :64], low[:, 64:]], axis=0))
        whole = jnp.concatenate(pieces, axis=1)
        attended[...] = whole
        middle = stream[q].astype(F32) + mm(whole, wo[...])
        gtokens[...] = middle

        smalls = small_rows(packs)
        scale = lax.rsqrt(jnp.mean(middle * middle, axis=1, keepdims=True) + NORM_EPSILON)
        low = (middle * scale * smalls[13:14]).astype(BF)
        hidden[...] = low
        logits = mm_nt(smalls.astype(BF), low)
        route_logits = logits[0:8] + residual[...]
        expert_row = lax.broadcasted_iota(jnp.int32, (8, TOK), 0)
        picks = [routes[k:k + 1, :] for k in range(TOPK)]
        picked = [
            jnp.sum(jnp.where(expert_row == pick, route_logits, 0.0), axis=0, keepdims=True) for pick in picks
        ]

        def pair_softmax(first, second):
            top = jnp.maximum(first, second)
            one, two = jnp.exp(first - top), jnp.exp(second - top)
            return [one / (one + two), two / (one + two)]

        gates = pair_softmax(*picked)
        coefs = pair_softmax(logits[8:9], logits[9:10]) + pair_softmax(logits[10:11], logits[11:12])
        expert = jnp.concatenate(picks, axis=1).astype(F32)
        order = jnp.concatenate([priority[...], priority[...] + STREAM], axis=1).astype(F32)
        base = expert * 4096.0
        rank_key = base + order
        key_rows = jnp.transpose(jnp.broadcast_to(rank_key, (128, 2 * TOK)))[:, 0:1]
        ahead = jnp.where((key_rows < rank_key) & (key_rows >= base), 1.0, 0.0)
        rank = jnp.sum(ahead, axis=0, keepdims=True)
        slot = jnp.where((expert < NFFN) & (rank < CAP), expert * CAP + rank, -1.0)
        slots = [slot[:, :TOK], slot[:, TOK:]]
        lanes = gates + coefs + slots + [pick.astype(F32) for pick in picks]
        lanes = jnp.concatenate(lanes + [jnp.zeros((128 - len(lanes), TOK), F32)], axis=0)
        cols[...] = jnp.transpose(lanes)
        slot_row = lax.broadcasted_iota(jnp.int32, (NFFN * CAP, TOK), 0).astype(F32)
        maps = [(slot_row == slots[k]).astype(F32).astype(BF) for k in range(TOPK)]
        bufs[0] = mm(maps[0] + maps[1], low).astype(BF).reshape(NFFN, CAP, D)
        row_send(0)
        loads[3].wait()
        grad_top = gout[...].astype(F32)
        grad_rows = sum(mm(maps[k], (cols[:, k:k + 1] * grad_top).astype(BF)) for k in range(TOPK))
        bufs[1] = grad_rows.astype(BF).reshape(NFFN, CAP, D)
        row_send(1)

        for n in range(2):
            ex_over(n).wait_send()
        for k, (other, device) in enumerate(others):
            att_copy(k, other, q, device).wait_send()

    pl.run_scoped(
        forward,
        pltpu.VMEM((3, 96, D), F32),
        pltpu.VMEM((96, D), F32),
        pltpu.VMEM((2, 96, 2 * FF), F32),
        pltpu.VMEM((2, 128, D), F32),
        pltpu.VMEM((96, FF), BF),
        pltpu.VMEM((128, D), BF),
        pltpu.VMEM((576, 128), BF),
        pltpu.VMEM((5, D, 128), BF),
        pltpu.VMEM((3, D, 128), BF),
        pltpu.VMEM((4, ATT, 128), BF),
        pltpu.VMEM((STREAM, 128), F32),
    )
    relay(2, y)
    row_pass(0)
    relay(2, ny)
    row_pass(1)
    row_collect(0)
    row_collect(1)

    def experts(rowt, down_sum, back_sum, part_out):
        rowt[...] = jnp.transpose(rowh[...].reshape(8 * CAP, D).astype(F32)).astype(BF)
        down_sum[...] = jnp.zeros_like(down_sum)
        back_sum[...] = jnp.zeros_like(back_sum)
        relay(3, y)
        relay(3, ny)

        @pl.loop(0, 4)
        def _(j):
            gate_cols = pl.ds(pl.multiple_of(j * 256, 256), 256)
            lin_cols = pl.ds(pl.multiple_of(1024 + j * 256, 256), 256)
            rows_h = rowh[...].reshape(8 * CAP, D)
            rows_g = rowg[...].reshape(8 * CAP, D)
            w_gate = wup[:, :, gate_cols].reshape(D, 256)
            w_lin = wup[:, :, lin_cols].reshape(D, 256)
            w_down = wdn[pl.ds(2 * j, 2)].reshape(256, D)
            gate = mm(rows_h, w_gate)
            lin = mm(rows_h, w_lin)
            grad_act = mm_nt(rows_g, w_down)
            sigma = jax.nn.sigmoid(gate)
            silu = gate * sigma
            low = (silu * lin).astype(BF)
            down_sum[...] += mm(low, w_down)
            grad_gate = (grad_act * lin * sigma * (1.0 + gate * (1.0 - sigma))).astype(BF)
            grad_lin = (grad_act * silu).astype(BF)
            back_sum[...] += mm_nt(grad_gate, w_gate) + mm_nt(grad_lin, w_lin)
            gdn[pl.ds(2 * j, 2)] = mm_tn(low, rows_g).astype(BF).reshape(2, 128, D)
            gup[:, :, gate_cols] = mm(rowt[...], grad_gate).astype(BF).reshape(8, 96, 256)
            gup[:, :, lin_cols] = mm(rowt[...], grad_lin).astype(BF).reshape(8, 96, 256)

        for z in range(LINE):
            for yy in range(2):
                for n in range(2):

                    @pl.when((l >= z) & (l < LINE - 1))
                    def _():
                        ex_copy(0, n, z, yy, me.at(l=l + 1)).wait_send()

                    @pl.when((l <= z) & (l > 0))
                    def _():
                        ex_copy(1, n, z, yy, me.at(l=l - 1)).wait_send()

        @pl.when(l < LINE - 1)
        def _():
            pl.semaphore_signal(ready.at[0], inc=1, device_id=me.at(l=l + 1), device_id_type=MESH)

        @pl.when(l > 0)
        def _():
            pl.semaphore_signal(ready.at[1], inc=1, device_id=me.at(l=l - 1), device_id_type=MESH)

        for n in range(2):
            for k, (cx, cy) in enumerate(chips):
                row_copy(n, k, cx, cy).wait_send()

        def swap(n):
            return remote(
                part_out.at[n], part_in.at[n], ss.at[S["part"] + n], rs.at[R["part"] + n], me.at(c=nc)
            )

        sums = (down_sum, back_sum)
        away = pl.ds(pl.multiple_of(nc * 4 * CAP, 4 * CAP), 4 * CAP)
        here = pl.ds(pl.multiple_of(c * 4 * CAP, 4 * CAP), 4 * CAP)
        for n in range(2):
            part_out[n] = sums[n][away, :].astype(BF).reshape(4, CAP, D)
            swap(n).start()
        for n in range(2):
            swap(n).wait_recv()
            kept = sums[n][here, :].reshape(4, CAP, D)
            bufs[n] = (kept + part_in[n].astype(F32)).astype(BF)
            for k, (cx, cy) in enumerate(chips):
                back_copy(n, k, cx, cy).start()
            ret[n, mine] = bufs[n, mine]
        for n in range(2):
            swap(n).wait_send()

    pl.run_scoped(
        experts,
        pltpu.VMEM((D, 8 * CAP), BF),
        pltpu.VMEM((8 * CAP, D), F32),
        pltpu.VMEM((8 * CAP, D), F32),
        pltpu.VMEM((2, 4, CAP, D), BF),
    )

    kinds = ((gup, wup, ringx_up, gup_all), (gdn, wdn, ringx_dn, gdn_all))

    def line_copy(d, z, yy, n, src, device, last):
        k = ((d * 4 + z) * 2 + yy) * 2 + n
        dst = kinds[n][2].at[yy] if last and d == 1 else kinds[n][1].at[2 * z + yy]
        return remote(src, dst, ss.at[S["line"] + k], rs.at[R["line"] + k], device)

    def first_sends(d, order, device):
        for z in order:
            for yy in range(2):
                for n in range(2):
                    line_copy(d, z, yy, n, kinds[n][0].at[2 * z + yy], device, z == order[2]).start()

    @pl.when(l < LINE - 1)
    def _():
        pl.semaphore_wait(ready.at[1], 1)

    @pl.when(l > 0)
    def _():
        pl.semaphore_wait(ready.at[0], 1)

    @pl.when(l == 0)
    def _():
        first_sends(0, (3, 2, 1), me.at(l=l + 1))

    @pl.when(l == LINE - 1)
    def _():
        first_sends(1, (0, 1, 2), me.at(l=l - 1))

    def add_own(n, slot):
        own_ref, ring = kinds[n][0], kinds[n][1]

        @pl.loop(0, own_ref.shape[1] // 16)
        def _(r):
            part = pl.ds(pl.multiple_of(r * 16, 16), 16)
            total = own_ref[slot, part, :].astype(F32) + ring[slot, part, :].astype(F32)
            ring[slot, part, :] = total.astype(BF)

    def line_step(t, yy):
        for d in range(2):
            far = l if d == 0 else LINE - 1 - l
            z = 3 + l - t if d == 0 else t - 3 + l

            @pl.when((far >= 1) & (far <= t))
            def _():
                device = me.at(l=l + 1) if d == 0 else me.at(l=l - 1)
                for n in range(2):
                    slot = 2 * z + yy
                    ring = kinds[n][1]
                    line_copy(d, z, yy, n, ring.at[slot], me.at(y=ny), t == 3).wait_recv()
                    if t < 3:
                        add_own(n, slot)
                        line_copy(d, z, yy, n, ring.at[slot], device, t == 2).start()

    for n in range(2):
        for cx, cy in chips:
            back_wait(n, cx, cy)
    smalls = small_rows(packs)
    down_rows = ret[0].reshape(NFFN * CAP, D)
    back_rows = ret[1].reshape(NFFN * CAP, D)
    vector = [smalls[14 + j:15 + j] for j in range(2)]
    router_row = lax.broadcasted_iota(jnp.int32, (16, 1), 0)
    router_low = jnp.where(router_row < 12, smalls, 0.0)
    router_low = jnp.concatenate([router_low, jnp.zeros((112, D), F32)], axis=0).astype(BF)
    facts[...] = jnp.zeros_like(facts)

    @pl.loop(0, TOK // ROWS)
    def _(i):
        rows = pl.ds(pl.multiple_of(i * ROWS, ROWS), ROWS)
        middle = gtokens[rows, :]
        low = hidden[rows, :]
        grad_low = gout[rows, :]
        info = cols[rows, :]
        token_lane = lax.broadcasted_iota(jnp.int32, (ROWS, NFFN * CAP), 1).astype(F32)
        gates = [info[:, k:k + 1] for k in range(TOPK)]
        coefs = [[info[:, 2 + 2 * j:3 + 2 * j], info[:, 3 + 2 * j:4 + 2 * j]] for j in range(2)]
        spread = [(token_lane == info[:, 6 + k:7 + k]).astype(F32).astype(BF) for k in range(TOPK)]
        picks = [info[:, 8 + k:9 + k] for k in range(TOPK)]
        chosen = [[(pick == e).astype(F32) for e in (5.0, 6.0, 7.0)] for pick in picks]
        grad_top = grad_low.astype(F32)
        value_hidden = low.astype(F32)
        grad_gate, mixture = [], middle
        for k in range(TOPK):
            copy, one, two = chosen[k]
            value = mm(spread[k], down_rows)
            value = value + (copy + one * coefs[0][0] + two * coefs[1][0]) * value_hidden
            value = value + (one * coefs[0][1]) * vector[0] + (two * coefs[1][1]) * vector[1]
            mixture = mixture + gates[k] * value
            grad_gate.append(jnp.sum(grad_top * value, axis=1, keepdims=True))
        layer_out[rows, :] = mixture.astype(BF)
        mean_gate = gates[0] * grad_gate[0] + gates[1] * grad_gate[1]
        grad_pick = [gates[k] * (grad_gate[k] - mean_gate) for k in range(TOPK)]
        lane = lax.broadcasted_iota(jnp.int32, (ROWS, 128), 1).astype(F32)
        grad_logits = sum(jnp.where(lane == picks[k], grad_pick[k], 0.0) for k in range(TOPK))
        groute[rows, :] = grad_logits[:, :NEXP]
        on_hidden = jnp.sum(grad_top * value_hidden, axis=1, keepdims=True)
        direct = gates[0] * chosen[0][0] + gates[1] * chosen[1][0]
        on_vectors = jnp.zeros((ROWS, 128), F32)
        for j in range(2):
            weight = gates[0] * chosen[0][1 + j] + gates[1] * chosen[1][1 + j]
            direct = direct + weight * coefs[j][0]
            grad_coef = [weight * on_hidden, weight * jnp.sum(grad_top * vector[j], axis=1, keepdims=True)]
            mean_coef = coefs[j][0] * grad_coef[0] + coefs[j][1] * grad_coef[1]
            for n in range(2):
                grad_logits = grad_logits + jnp.where(
                    lane == 8.0 + 2 * j + n, coefs[j][n] * (grad_coef[n] - mean_coef), 0.0
                )
            on_vectors = on_vectors + jnp.where(lane == 14.0 + j, weight * coefs[j][1], 0.0)
        logit_parts = split_low(grad_logits)
        vector_parts = split_low(on_vectors)
        grad_hidden = direct * grad_top + mm(spread[0] + spread[1], back_rows)
        grad_hidden = grad_hidden + mm(logit_parts[0], router_low) + mm(logit_parts[1], router_low)
        small_sum = mm_tn(logit_parts[0], low) + mm_tn(logit_parts[1], low)
        small_sum = small_sum + mm_tn(vector_parts[0], grad_low) + mm_tn(vector_parts[1], grad_low)
        scale = lax.rsqrt(jnp.mean(middle * middle, axis=1, keepdims=True) + NORM_EPSILON)
        normal = middle * scale
        gain_sum = jnp.sum(grad_hidden * normal, axis=0, keepdims=True)
        facts[...] += small_sum[0:16] + jnp.where(router_row == 13, gain_sum, 0.0)
        inner_term = grad_hidden * smalls[13:14]
        gtokens[rows, :] = grad_top + scale * (
            inner_term - normal * jnp.mean(inner_term * normal, axis=1, keepdims=True)
        )

    def backward(pk, kt, grad, dq, dv, dk_sum, dv_sum, delta, gr, wall, ap):
        grad_att = mm_nt(gtokens[...].astype(BF), wo[...])
        for part in range(4):
            wide = grad_att[:, 192 * part:192 * (part + 1)]
            pk[part, 0:TOK, :] = wide[:, :128].astype(BF)
            third = wide[:, 128:]
            pk[part, TOK:ATT, :] = jnp.concatenate([third[:HALF], third[HALF:]], axis=1).astype(BF)
        got[q] = pk[q]

        def att_copy(k, to, frm, device):
            return remote(pk.at[to], got.at[frm], ss.at[S["att2"] + k], rs.at[R["att2"] + k], device)

        for k, (other, device) in enumerate(others):
            att_copy(k, other, q, device).start()

        wo_copy(1, q, me.at(x=nx)).wait_send()
        wo_copy(0, q, me.at(c=nc)).wait_send()
        wo_copy(2, 2 * nx + c, me.at(c=nc)).wait_send()

        @pl.loop(0, 2)
        def _(i):
            wide = pl.ds(pl.multiple_of(i * 384, 384), 384)
            grad_wo = mm_tn(attended[:, wide], gtokens[...].astype(BF)).astype(BF)
            for s in range(4):
                for t in range(6):
                    tile = grad_wo[96 * s:96 * (s + 1), 128 * t:128 * (t + 1)]
                    wo_all[4 * i + s, 96 * t:96 * (t + 1), :] = tile

        def wo_rows(part):
            return pl.ds(pl.multiple_of(part * O_ROWS, O_ROWS), O_ROWS)

        def wo_share(k, to, device):
            return remote(
                wo_all.at[:, wo_rows(to), :], wo_in.at[k], ss.at[S["wo2"] + k], rs.at[R["wo2"] + k], device
            )

        for s in range(OUTER):
            for t in range(5):
                wall[96 * s:96 * (s + 1), 128 * t:128 * (t + 1)] = packs[s, 96 * t:96 * (t + 1), :]

        for k, (other, device) in enumerate(others):
            att_copy(k, q, other, device).wait_recv()
        for k, (other, device) in enumerate(others):
            wo_share(k, other, device).start()
        for part in range(4):
            rows = slice(part * TOK, (part + 1) * TOK)
            both = got[part, 0:TOK, :]
            third = got[part, TOK:ATT, :]
            grad[0, rows, :] = both[:, :64]
            grad[1, rows, :] = both[:, 64:]
            grad[2, rows, :] = jnp.concatenate([third[:, :64], third[:, 64:]], axis=0)
        for h in range(LOCAL_HEADS):
            dots = jnp.sum(grad[h].astype(F32) * vo[h, :, 64:128].astype(F32), axis=1, keepdims=True)
            delta[h] = jnp.transpose(jnp.broadcast_to(dots, (STREAM, 128)))[0:8, :]

        def one_head(h):
            ks[...] = qk[h, :, 64:128]
            kt[...] = jnp.transpose(ks[...].astype(F32)).astype(BF)
            dk_sum[...] = jnp.zeros((STREAM, 64), F32)
            dv_sum[...] = jnp.zeros((STREAM, 64), F32)
            for b in range(STREAM // BLOCK):
                first, last = b * BLOCK, (b + 1) * BLOCK
                q_rows, g_rows = qk[h, first:last, 0:64], grad[h, first:last, :]
                grad_q = jnp.zeros((64, BLOCK), F32)
                for start in range(0, last, KEYS):
                    keys = slice(start, min(start + KEYS, last))
                    size = keys.stop - start
                    scores = mm_nt(ks[keys, :], q_rows)
                    key = lax.broadcasted_iota(jnp.int32, (size, BLOCK), 0) + start
                    col = lax.broadcasted_iota(jnp.int32, (size, BLOCK), 1) + first
                    seen = (key >= begin[0:1, first:last]) & (key <= col)
                    probs = jnp.exp(jnp.where(seen, scores, NEGATIVE) - lse[h, 0:1, first:last])
                    grad_probs = mm_nt(vo[h, keys, 0:64], g_rows)
                    grad_scores = (probs * (grad_probs - delta[h, 0:1, first:last])).astype(BF)
                    dv_sum[keys, :] += mm(probs.astype(BF), g_rows)
                    dk_sum[keys, :] += mm(grad_scores, q_rows)
                    grad_q = grad_q + mm(kt[:, keys], grad_scores)
                dq[first:last, :] = (jnp.transpose(grad_q) * 0.125).astype(BF)
            dv[h] = dv_sum[...].astype(BF)
            for part in range(4):
                rows = slice(part * TOK, (part + 1) * TOK)
                turned = jnp.concatenate([dq[rows, :], dk_sum[rows, :].astype(BF)], axis=1)
                raw = turned.astype(F32) * cos[rows, :] - mm(turned, turn[...]) * sin[rows, :]
                gr[rows, pl.ds(pl.multiple_of(h * 128, 128), 128)] = raw.astype(BF)

        line_step(1, 0)
        pl.loop(0, LOCAL_HEADS)(one_head)
        line_step(1, 1)
        for part in range(4):
            rows = slice(part * TOK, (part + 1) * TOK)
            gr[rows, 384:512] = jnp.concatenate([dv[0, rows, :], dv[1, rows, :]], axis=1)
            gr[rows, 512:640] = jnp.concatenate([dv[2, rows, :], jnp.zeros((TOK, 64), BF)], axis=1)

        @pl.loop(0, 2)
        def _(i):
            wide = pl.ds(pl.multiple_of(i * 384, 384), 384)
            grad_a = mm_tn(normed[:, wide], gr[...]).astype(BF)
            for s in range(4):
                for t in range(5):
                    ap[4 * i + s, 96 * t:96 * (t + 1), :] = grad_a[96 * s:96 * (s + 1), 128 * t:128 * (t + 1)]

        for k, (other, device) in enumerate(others):
            wo_share(k, q, device).wait_recv()
        wo_total = wo_all[:, wo_rows(q), :].astype(F32)
        for k in range(3):
            wo_total = wo_total + wo_in[k].astype(F32)
        ap[:, A_ROWS:A_ROWS + O_ROWS, :] = wo_total.astype(BF)

        for n in range(2):
            core_copy(n, 0, 4 * c, mine).wait_send()
            for k, (cx, cy) in enumerate(chips):
                core_copy(n, 1 + k, 4 * c, 2 * cx + cy).wait_send()
                back_copy(n, k, cx, cy).wait_send()
        gain_sum = jnp.zeros((1, D), F32)
        for part in range(4):
            rows = slice(part * TOK, (part + 1) * TOK)
            grad_n = mm_nt(gr[rows, :], wall[...])
            values = stream[part].astype(F32)
            scale = lax.rsqrt(jnp.mean(values * values, axis=1, keepdims=True) + NORM_EPSILON)
            gain_sum = gain_sum + jnp.sum(grad_n * (values * scale), axis=0, keepdims=True)
            first = 4 * (part % 2)
            (rowh, rowg)[part // 2][first:first + 4] = grad_n.astype(BF).reshape(4, CAP, D)

        def gn_swap(a):
            row = (rowh, rowg)[a]
            return remote(
                row.at[pl.ds(4 * nc, 4)], part_in.at[a], ss.at[S["gn"] + a], rs.at[R["gn"] + a], me.at(c=nc)
            )

        for a in range(2):
            gn_swap(a).start()
        small_all = facts[...] + jnp.where(router_row == 12, gain_sum, 0.0)
        for s in range(OUTER):
            piece = jnp.concatenate([small_all[:, 96 * s:96 * (s + 1)], jnp.zeros((16, 32), F32)], axis=1)
            ap[s, A_ROWS + O_ROWS:PACKG, :] = piece.astype(BF)

        def ay_copy(z):
            return remote(ap.at[2 * z + ny], ap_in.at[z], ss.at[S["ay"] + z], rs.at[R["ay"] + z], me.at(y=ny))

        for z in range(LINE):
            ay_copy(z).start()
        line_step(2, 0)
        for a in range(2):
            gn_swap(a).wait_recv()
            bufs[a] = ((rowh, rowg)[a][pl.ds(4 * c, 4)].astype(F32) + part_in[a].astype(F32)).astype(BF)
        gn_over = remote(bufs.at[nx], gn_ret, ss.at[S["gn"] + 2], rs.at[R["gn"] + 2], me.at(x=nx))
        gn_over.start()
        line_step(2, 1)
        for z in range(LINE):
            ay_copy(z).wait_recv()
            ap_in[z] = (ap[2 * z + y].astype(F32) + ap_in[z].astype(F32)).astype(BF)

        for k, (other, device) in enumerate(others):
            att_copy(k, other, q, device).wait_send()
            wo_share(k, other, device).wait_send()
        for a in range(2):
            gn_swap(a).wait_send()
        for z in range(LINE):
            ay_copy(z).wait_send()

    heads = (LOCAL_HEADS, STREAM, 64)
    pl.run_scoped(
        backward,
        pltpu.VMEM((4, ATT, 128), BF),
        pltpu.VMEM((64, STREAM), BF),
        pltpu.VMEM(heads, BF),
        pltpu.VMEM((STREAM, 64), BF),
        pltpu.VMEM(heads, BF),
        pltpu.VMEM((STREAM, 64), F32),
        pltpu.VMEM((STREAM, 64), F32),
        pltpu.VMEM((LOCAL_HEADS, 8, STREAM), F32),
        pltpu.VMEM((STREAM, 640), BF),
        pltpu.VMEM((D, 640), BF),
        pltpu.VMEM((OUTER, PACKG, 128), BF),
    )

    def al_copy(d, z, src, device):
        k = 4 * d + z
        return remote(src, ap_line.at[d, z], ss.at[S["al"] + k], rs.at[R["al"] + k], device)

    @pl.when(l == 0)
    def _():
        for z in (3, 2, 1):
            al_copy(0, z, ap_in.at[z], me.at(l=l + 1)).start()

    @pl.when(l == LINE - 1)
    def _():
        for z in (0, 1, 2):
            al_copy(1, z, ap_in.at[z], me.at(l=l - 1)).start()

    def al_step(t):
        for d in range(2):
            far = l if d == 0 else LINE - 1 - l
            z = 3 + l - t if d == 0 else t - 3 + l

            @pl.when((far >= 1) & (far <= t))
            def _():
                device = me.at(l=l + 1) if d == 0 else me.at(l=l - 1)
                al_copy(d, z, ap_line.at[d, z], me.at(y=ny)).wait_recv()
                if t < 3:
                    ap_line[d, z] = (ap_line[d, z].astype(F32) + ap_in[z].astype(F32)).astype(BF)
                    al_copy(d, z, ap_line.at[d, z], device).start()

    def gp_over(n, k, cx, cy):
        return remote(
            kinds[n][2].at[cy], kinds[n][3].at[2 * mine + c], ss.at[S["gp"] + 7 * n + k],
            rs.at[R["gp"] + 8 * n + 2 * mine + c], me.at(x=cx, y=cy)
        )

    def gp_wait(n, slot):
        ref = kinds[n][3]
        remote(ref.at[slot], ref.at[slot], ss.at[0], rs.at[R["gp"] + 8 * n + slot], me.at(c=nc)).wait_recv()

    def gp_own(n):
        return pltpu.make_async_copy(kinds[n][2].at[y], kinds[n][3].at[2 * mine + c], ls.at[10 + n])

    def gp_core(n, k, slot, src=None):
        ref = kinds[n][3]
        return remote(
            ref.at[slot] if src is None else src, ref.at[slot], ss.at[S["gp"] + 7 * n + 3 + k],
            rs.at[R["gp"] + 8 * n + slot], me.at(c=nc)
        )

    def line_end(yy):
        line_step(3, yy)
        for n in range(2):
            own_ref, ring, fin, _ = kinds[n]
            slot = 2 * l + yy

            @pl.loop(0, own_ref.shape[1] // 16)
            def _(r):
                part = pl.ds(pl.multiple_of(r * 16, 16), 16)
                up_sum = jnp.where(l >= 1, ring[slot, part, :].astype(F32), 0.0)
                dn_sum = jnp.where(l <= 2, fin[yy, part, :].astype(F32), 0.0)
                total = own_ref[slot, part, :].astype(F32) + up_sum + dn_sum
                fin[yy, part, :] = total.astype(BF)

            @pl.when(y == yy)
            def _():
                gp_over(n, 1, nx, y).start()
                gp_own(n).start()
                gp_core(n, 0, 2 * mine + c, fin.at[yy]).start()

            @pl.when(y != yy)
            def _():
                gp_over(n, 0, x, ny).start()
                gp_over(n, 2, nx, ny).start()

    al_step(1)

    gn_over = remote(bufs.at[nx], gn_ret, ss.at[S["gn"] + 2], rs.at[R["gn"] + 2], me.at(x=nx))
    gn_over.wait_recv()
    values = stream[q].astype(F32)
    scale = lax.rsqrt(jnp.mean(values * values, axis=1, keepdims=True) + NORM_EPSILON)
    normal = values * scale
    grad_n = (bufs[x].astype(F32) + gn_ret[...].astype(F32)).reshape(TOK, D)
    inner_term = grad_n * small_rows(packs)[12:13]
    gtokens[...] = gtokens[...] + scale * (
        inner_term - normal * jnp.mean(inner_term * normal, axis=1, keepdims=True)
    )

    line_end(0)
    al_step(2)
    line_end(1)
    al_step(3)

    @pl.when(l == 0)
    def _():
        ap_line[0, l] = jnp.zeros((PACKG, 128), BF)

    @pl.when(l == LINE - 1)
    def _():
        ap_line[1, l] = jnp.zeros((PACKG, 128), BF)

    own_sum = ap_in[l].astype(F32) + ap_line[0, l].astype(F32) + ap_line[1, l].astype(F32)
    apack[q] = own_sum.astype(BF)

    def aa_copy(k, part, device):
        return remote(apack.at[part], apack.at[part], ss.at[S["aa"] + k], rs.at[R["aa"] + k], device)

    for k, (other, device) in enumerate(others):
        aa_copy(k, q, device).start()

    for k, (cx, cy) in enumerate(chips):
        for n in range(2):
            slot = 2 * (2 * cx + cy) + c
            gp_wait(n, slot)
            gp_core(n, 1 + k, slot).start()
    for n in range(2):
        for slot in range(4):
            gp_wait(n, 2 * slot + nc)
    for k, (other, device) in enumerate(others):
        aa_copy(k, other, device).wait_recv()

    tok_copy(1, q, me.at(x=nx)).wait_send()
    tok_copy(0, q, me.at(c=nc)).wait_send()
    tok_copy(2, 2 * nx + c, me.at(c=nc)).wait_send()
    gn_over.wait_send()
    for k, (other, device) in enumerate(others):
        aa_copy(k, q, device).wait_send()
    for n in range(2):
        for k, (cx, cy) in enumerate(chips):
            gp_over(n, k, cx, cy).wait_send()
            gp_core(n, 1 + k, 2 * (2 * cx + cy) + c).wait_send()
        gp_core(n, 0, 2 * mine + c, kinds[n][2].at[y]).wait_send()
        gp_own(n).wait()
    for z in range(LINE):
        pack_copy(2, z, me.at(y=ny)).wait_send()

        @pl.when((l >= z) & (l < LINE - 1))
        def _():
            pack_copy(0, z, me.at(l=l + 1)).wait_send()

        @pl.when((l <= z) & (l > 0))
        def _():
            pack_copy(1, z, me.at(l=l - 1)).wait_send()
    for d in range(2):
        for z in range(LINE):
            sent = (z > l) & (l < LINE - 1) if d == 0 else (z < l) & (l > 0)

            @pl.when(sent)
            def _():
                device = me.at(l=l + 1) if d == 0 else me.at(l=l - 1)
                al_copy(d, z, ap_line.at[d, z], device).wait_send()
                for yy in range(2):
                    for n in range(2):
                        line_copy(d, z, yy, n, kinds[n][1].at[2 * z + yy], device, False).wait_send()


def layer_call(inner, *args):
    vm = pl.BlockSpec(memory_space=pltpu.VMEM)
    hbm = pl.BlockSpec(memory_space=pl.ANY)
    smem = pl.BlockSpec(memory_space=pltpu.SMEM)
    heads = (LOCAL_HEADS, STREAM, 64)
    wide = (LOCAL_HEADS, STREAM, 128)
    _, _, sends, recvs = semaphores()
    scratch = [
        ((4, TOK, D), BF), ((OUTER, PACK, 128), BF), ((OUTER, 576, 128), BF), ((D, D), BF),
        ((OUTER, 96, FF), BF), ((OUTER, 128, D), BF), ((2, 96, FF), BF), ((2, 128, D), BF),
        ((OUTER, 96, FF), BF), ((OUTER, 128, D), BF),
        ((8, CAP, D), BF), ((8, CAP, D), BF), ((2, 4, CAP, D), BF), ((2, 4, CAP, D), BF),
        ((4, ATT, 128), BF), ((3, OUTER, O_ROWS, 128), BF),
        ((LINE, PACKG, 128), BF), ((2, LINE, PACKG, 128), BF), ((4, CAP, D), BF),
        ((STREAM, D), BF), (wide, BF), (wide, BF), ((STREAM, 64), BF), ((LOCAL_HEADS, 8, STREAM), F32),
        ((TOK, D), BF), ((TOK, D), BF), ((STREAM, 128), F32), ((STREAM, 128), F32), ((TOK, D), BF),
        ((2, 4, CAP, D), BF), ((8, STREAM), jnp.int32), ((TOK, 128), F32), ((16, D), F32),
    ]
    return pl.pallas_call(
        functools.partial(layer_kernel, inner),
        out_shape=[
            jax.ShapeDtypeStruct((TOK, D), BF),
            jax.ShapeDtypeStruct((TOK, D), F32),
            jax.ShapeDtypeStruct((TOK, NEXP), F32),
            jax.ShapeDtypeStruct((4, PACKG, 128), BF),
            jax.ShapeDtypeStruct((8, 96, FF), BF),
            jax.ShapeDtypeStruct((8, 128, D), BF),
        ],
        in_specs=[hbm] * 8 + [vm, smem] + [vm] * 5,
        out_specs=[vm] * 4 + [hbm] * 2,
        scratch_shapes=[pltpu.VMEM(s, t) for s, t in scratch]
        + [
            pltpu.SemaphoreType.DMA((sends,)),
            pltpu.SemaphoreType.DMA((recvs,)),
            pltpu.SemaphoreType.DMA((12,)),
            pltpu.SemaphoreType.REGULAR((2,)),
        ],
        compiler_params=pltpu.CompilerParams(
            collective_id=0, has_side_effects=True, vmem_limit_bytes=VMEM_LIMIT
        ),
        name="layer",
    )(*args)


def adam(weight, grad, first, second, rate, decay):
    first_new = MOMENT_DECAY * first + (1.0 - MOMENT_DECAY) * grad
    second_new = MOMENT_DECAY * second + (1.0 - MOMENT_DECAY) * grad * grad
    correction = 1.0 - MOMENT_DECAY**STEP
    update = first_new / correction / (jnp.sqrt(second_new / correction) + ADAM_EPSILON)
    return weight - rate * (update + decay * weight), first_new, second_new


UP_PARTS = 2


def update_kernel(
    apack, gu, gd,
    in_w, in_m, in_v, out_w, out_m, out_v, rt_w, rt_m, rt_v, vec_w, vec_m, vec_v,
    up_w, up_m, up_v, dn_w, dn_m, dn_v,
    in_w2, in_m2, in_v2, out_w2, out_m2, out_v2, rt_w2, rt_m2, rt_v2, vec_w2, vec_m2, vec_v2,
    up_w2, up_m2, up_v2, dn_w2, dn_m2, dn_v2,
):
    step = pl.program_id(0)

    for j in range(16):
        cols, part = slice(256 * j, 256 * (j + 1)), slice(128 * j, 128 * (j + 1))
        grad = jnp.concatenate([gu[0, :, part], gu[1, :, part]], axis=1).astype(F32)
        new = adam(up_w[0, :, cols], grad, up_m[0, :, cols], up_v[0, :, cols], STEP_RATES[2], STEP_DECAYS[2])
        up_w2[0, :, cols], up_m2[0, :, cols], up_v2[0, :, cols] = new
    for half in range(2):
        rows = slice(128 * half, 128 * (half + 1))
        grad = gd[half].astype(F32)
        new = adam(dn_w[0, rows, :], grad, dn_m[0, rows, :], dn_v[0, rows, :], STEP_RATES[3], STEP_DECAYS[3])
        dn_w2[0, rows, :], dn_m2[0, rows, :], dn_v2[0, rows, :] = new

    @pl.when(step == 0)
    def _():
        tiles = [[apack[p, 96 * t:96 * (t + 1), :].astype(F32) for t in range(5)] for p in range(4)]
        for kind in range(3):
            pieces = []
            for p in range(4):
                if kind < 2:
                    pieces += [tiles[p][h][:, 64 * kind:64 * kind + 64] for h in range(LOCAL_HEADS)]
                else:
                    pieces += [tiles[p][3][:, :64], tiles[p][3][:, 64:], tiles[p][4][:, :64]]
            grad = jnp.concatenate(pieces, axis=1)
            new = adam(in_w[kind], grad, in_m[kind], in_v[kind], STEP_RATES[0], STEP_DECAYS[0])
            in_w2[kind], in_m2[kind], in_v2[kind] = new
        rows = jnp.concatenate([apack[p, A_ROWS:A_ROWS + O_ROWS, :] for p in range(4)], axis=0)
        for t in range(6):
            cols = slice(128 * t, 128 * (t + 1))
            grad = rows[96 * t:96 * (t + 1), :].astype(F32)
            new = adam(out_w[:, cols], grad, out_m[:, cols], out_v[:, cols], STEP_RATES[1], STEP_DECAYS[1])
            out_w2[:, cols], out_m2[:, cols], out_v2[:, cols] = new
        small = jnp.zeros((16, 128), F32)
        for p in range(4):
            small = small + apack[p, A_ROWS + O_ROWS:A_ROWS + O_ROWS + 16, :].astype(F32)
        new = adam(vec_w[...], small[12:, :96], vec_m[...], vec_v[...], STEP_RATES[5], STEP_DECAYS[5])
        vec_w2[...], vec_m2[...], vec_v2[...] = new
        new = adam(rt_w[...], small[:12, :96], rt_m[...], rt_v[...], STEP_RATES[4], STEP_DECAYS[4])
        rt_w2[...], rt_m2[...], rt_v2[...] = new


def update_call(apack, gu, gd, states):
    flat = [a for group in states for a in group]

    def whole(a):
        return pl.BlockSpec(a.shape, lambda e: (0,) * a.ndim)

    def by_expert(a):
        return pl.BlockSpec((1,) + a.shape[1:], lambda e: (e, 0, 0))

    specs = [whole(a) for a in flat[:12]] + [by_expert(a) for a in flat[12:]]
    pairs = [pl.BlockSpec((2,) + a.shape[1:], lambda e: (e, 0, 0)) for a in (gu, gd)]
    return pl.pallas_call(
        update_kernel,
        grid=(NFFN,),
        out_shape=[jax.ShapeDtypeStruct(a.shape, a.dtype) for a in flat],
        in_specs=[whole(apack)] + pairs + specs,
        out_specs=specs,
        compiler_params=pltpu.CompilerParams(vmem_limit_bytes=56 * 2**20),
        name="update",
    )(apack, gu, gd, *flat)


def gather_inner(values, axis, inner):
    if inner == 1:
        return values
    count = lax.axis_size("shard")
    groups = [[o * inner + i for i in range(inner)] for o in range(count // inner)]
    return lax.all_gather(values, "shard", axis=axis, tiled=True, axis_index_groups=groups)


def scatter_inner(values, axis, inner):
    count = lax.axis_size("shard")
    groups = [[o * inner + i for i in range(inner)] for o in range(count // inner)]
    return lax.psum_scatter(
        values, "shard", scatter_dimension=axis, axis_index_groups=groups, tiled=True
    )


def whole_gradients(apack, gup_all, gdn_all):
    tiles = apack[:, :A_ROWS].reshape(4, 5, 96, 128)
    heads = [
        tiles[:, 0:3, :, :64].transpose(2, 0, 1, 3),
        tiles[:, 0:3, :, 64:].transpose(2, 0, 1, 3),
        jnp.stack([tiles[:, 3, :, :64], tiles[:, 3, :, 64:], tiles[:, 4, :, :64]], axis=1).transpose(2, 0, 1, 3),
    ]
    g_in = jnp.stack([head.reshape(96, D) for head in heads])
    g_out = apack[:, A_ROWS:A_ROWS + O_ROWS].reshape(6, 96, 128).transpose(1, 0, 2).reshape(96, D)
    g_small = jnp.sum(apack[:, A_ROWS + O_ROWS:, :96].astype(F32), axis=0)
    g_up = gup_all.reshape(NFFN, 2, 96, 2, 8, 128).transpose(0, 2, 3, 4, 1, 5).reshape(NFFN, 96, 2 * FF)
    g_down = gdn_all.reshape(NFFN, 256, D)
    grads = (g_in, g_out, g_small[:12].T, g_small[12:], g_up, g_down)
    return [grad.astype(F32) for grad in grads]


def local(
    tokens, route_residual, doc_lengths, routes, priority, grad_out,
    attend_in, attend_in_first, attend_in_second,
    attend_out, attend_out_first, attend_out_second,
    expert_up, expert_up_first, expert_up_second,
    expert_down, expert_down_first, expert_down_second,
    router_mix, router_mix_first, router_mix_second,
    vectors, vectors_first, vectors_second,
):
    inner = lax.axis_size("shard") // OUTER
    cosine, sine, turn = rope_constants(STREAM)
    layer_out, grad_tokens, grad_route, apack, gup_all, gdn_all = layer_call(
        inner,
        tokens[0], grad_out[0],
        gather_inner(attend_in, 1, inner), gather_inner(attend_out, 0, inner),
        gather_inner(expert_up, 1, inner), gather_inner(expert_down, 1, inner),
        jnp.asarray(cosine), jnp.asarray(sine), jnp.asarray(turn, BF), doc_lengths,
        routes[0].T, route_residual[0].T, priority,
        gather_inner(router_mix, 0, inner).T, gather_inner(vectors, 1, inner),
    )
    states = (
        (attend_in, attend_in_first, attend_in_second),
        (attend_out, attend_out_first, attend_out_second),
        (router_mix, router_mix_first, router_mix_second),
        (vectors, vectors_first, vectors_second),
        (expert_up, expert_up_first, expert_up_second),
        (expert_down, expert_down_first, expert_down_second),
    )
    if inner == 1:
        turned = [a.T for a in states[2]]
        updated = update_call(apack, gup_all, gdn_all, (states[0], states[1], turned, *states[3:]))
        router = [a.T for a in updated[6:9]]
        results = (*updated[0:6], *updated[12:18], *router, *updated[9:12])
        return (layer_out[None], grad_tokens[None], grad_route[None], *results)

    grads = whole_gradients(apack, gup_all, gdn_all)
    axes = (1, 0, 0, 1, 1, 1)
    rates = [STEP_RATES[k] for k in (0, 1, 4, 5, 2, 3)]
    decays = [STEP_DECAYS[k] for k in (0, 1, 4, 5, 2, 3)]
    updated = [
        adam(weight, scatter_inner(grad, axis, inner), first, second, rate, decay)
        for (weight, first, second), grad, axis, rate, decay in zip(states, grads, axes, rates, decays)
    ]
    results = [a for k in (0, 1, 4, 5, 2, 3) for a in updated[k]]
    return (layer_out[None], grad_tokens[None], grad_route[None], *results)


def solution(mesh):
    token = P("shard", "seq", None)
    middle = P(None, "shard", None)
    front = P("shard", None)
    back = P(None, "shard")
    weights = (middle,) * 3 + (front,) * 3 + (middle,) * 6 + (front,) * 3 + (back,) * 3
    return jax.shard_map(
        local,
        mesh=mesh,
        in_specs=(token, token, front, token, P("shard", "seq"), token) + weights,
        out_specs=(token, token, token) + weights,
        check_vma=False,
    )
```

```python
import functools

import jax
import jax.numpy as jnp
import numpy as np
from jax import lax
from jax.experimental import pallas as pl
from jax.experimental.pallas import tpu as pltpu
from jax.sharding import PartitionSpec as P

D = 768
HEADS = 12
HEAD_DIM = 64
FF = 2048
NFFN = 4
NEXP = 8
TOPK = 2
STEP = 5
CAP = 96
LINE = 4
OUTER = 8
LOCAL_HEADS = 3

NORM_EPSILON = 1e-05
ROPE_BASE = 10000.0
NEGATIVE = -1e30
MOMENT_DECAY = 0.5
ADAM_EPSILON = 1e-08
STEP_RATES = (0.04, 0.1, 0.04, 0.02, 0.02, 0.2)
STEP_DECAYS = (0.1, 0.1, 0.1, 0.1, 0.1, 0.0)
BF = jnp.bfloat16
F32 = jnp.float32
MESH = pl.DeviceIdType.MESH
VMEM_LIMIT = 58 * 2**20


def mm(left, right):
    return jnp.dot(left, right, preferred_element_type=F32)


def mm_nt(left, right):
    return lax.dot_general(left, right, (((1,), (1,)), ((), ())), preferred_element_type=F32)


def mm_tn(left, right):
    return lax.dot_general(left, right, (((0,), (0,)), ((), ())), preferred_element_type=F32)


class Place:
    def __init__(self, inner):
        q = lax.axis_index("seq")
        shard = lax.axis_index("shard")
        self.inner = inner
        self.rest = lax.rem(shard, inner) if inner > 1 else 0
        outer = lax.div(shard, inner) if inner > 1 else shard
        self.q = q
        self.x = lax.div(q, 2)
        self.c = lax.rem(q, 2)
        self.l = lax.div(outer, 2)
        self.y = lax.rem(outer, 2)
        self.own = outer

    def at(self, x=None, c=None, l=None, y=None):
        x = self.x if x is None else x
        c = self.c if c is None else c
        l = self.l if l is None else l
        y = self.y if y is None else y
        return (2 * x + c, (2 * l + y) * self.inner + self.rest)


def greet(devices):
    barrier = pltpu.get_barrier_semaphore()
    for device in devices:
        pl.semaphore_signal(barrier, inc=1, device_id=device, device_id_type=MESH)
    pl.semaphore_wait(barrier, len(devices))


def remote(src, dst, send, recv, device):
    return pltpu.make_async_remote_copy(
        src_ref=src, dst_ref=dst, send_sem=send, recv_sem=recv, device_id=device, device_id_type=MESH
    )


def rope_constants(stream_len):
    frequency = ROPE_BASE ** (-(np.arange(HEAD_DIM // 2, dtype=np.float64) * 2.0 / HEAD_DIM))
    angles = np.arange(stream_len, dtype=np.float64)[:, None] * frequency[None, :]
    cosine = np.tile(np.cos(angles), (1, 4)).astype(np.float32)
    sine = np.tile(np.sin(angles), (1, 4)).astype(np.float32)
    turn = np.zeros((128, 128), np.float32)
    for j in range(128):
        if j % 64 < 32:
            turn[j + 32, j] = -1.0
        else:
            turn[j - 32, j] = 1.0
    return cosine, sine, turn


A_ROWS = 5 * 96
O_ROWS = 144
S_ROWS = 96
PACK = A_ROWS + S_ROWS
PACKG = A_ROWS + O_ROWS + 16
A_PARTS = (slice(0, 192), slice(192, A_ROWS + O_ROWS), slice(A_ROWS + O_ROWS, PACKG))
TOK = 384
STREAM = 1536
ATT = 576
HALF = TOK // 2
BLOCK = 256
KEYS = 512
ROWS = 128


class Counter:
    def __init__(self):
        self.used = 0

    def take(self, count):
        first = self.used
        self.used += count
        return first


def semaphores():
    s, r = Counter(), Counter()
    counts = {
        "tok": (3, 3), "pack": (7, 8), "wo8": (7, 8), "wo": (3, 3), "ex": (8, 18), "over": (8, 0), "last": (2, 0),
        "att": (6, 6), "row": (9, 12), "core": (12, 12), "part": (2, 2), "back": (6, 8), "pair": (8, 8), "line": (8, 10),
        "att2": (3, 3), "wo2": (3, 3), "ay": (12, 12), "al": (9, 12), "gn": (3, 3), "aa": (9, 9), "gp": (12, 16),
    }
    send = {name: s.take(count[0]) for name, count in counts.items()}
    recv = {name: r.take(count[1]) for name, count in counts.items()}
    return send, recv, s.used, r.used


def small_rows(packs):
    tiles = []
    for t in range(6):
        first = A_ROWS + 16 * t
        total = packs[0, first:first + 16, :].astype(F32)
        for s in range(1, OUTER):
            total = total + packs[s, first:first + 16, :].astype(F32)
        tiles.append(total)
    return jnp.concatenate(tiles, axis=1)


def split_low(values):
    high = values.astype(BF)
    return high, (values - high.astype(F32)).astype(BF)


def layer_kernel(
    inner,
    tok, gout_in, w_in, w_out, w_up, w_dn, cos_in, sin_in, turn, lengths, routes, residual, priority, router, vectors,
    layer_out, gtokens, groute, apack, gup_all, gdn_all,
    stream, packs, wo_all, wo, wup, wdn, ringx_up, ringx_dn, gup, gdn, rowh, rowg, part_in, ret, got, wo_in,
    ap_in, ap_line, gn_ret, normed, qk, vo, ks, lse, attended, hidden, cos, sin, gout, bufs, begin,
    cols, facts, gate_out, gate_in, ss, rs, ls, ready,
):
    me = Place(inner)
    x, c, l, y, q, own = me.x, me.c, me.l, me.y, me.q, me.own
    nx, nc, ny = 1 - x, 1 - c, 1 - y
    side = lax.div(l, 2)
    far = 1 - side
    outer = (l == 0) | (l == LINE - 1)
    inside = (l == 1) | (l == 2)
    out, near, far_near, far_out = 3 * side, 1 + side, 2 - side, 3 - 3 * side
    mate = 1 - l + 4 * side
    mine = 2 * side + x
    S, R, _, _ = semaphores()
    chips = [(nx, side), (x, far), (nx, far)]
    others = [(2 * nx + c, me.at(x=nx)), (2 * nx + nc, me.at(x=nx, c=nc)), (2 * x + nc, me.at(c=nc))]

    def load(src, dst, k):
        return pltpu.make_async_copy(src, dst, ls.at[k])

    def tok_copy(k, part, device):
        return remote(stream.at[part], stream.at[part], ss.at[S["tok"] + k], rs.at[R["tok"] + k], device)

    turns = [lax.rem(l + dl, LINE) for dl in range(LINE)]
    shards = [me.at(l=turns[dl]) for dl in (1, 3, 2)] + [me.at(l=turns[dl], y=ny) for dl in (0, 1, 3, 2)]

    def pack_copy(k, z, device):
        slot = 2 * z + y
        return remote(packs.at[slot], packs.at[slot], ss.at[S["pack"] + k], rs.at[R["pack"] + slot], device)

    def pack_wait(slot):
        remote(packs.at[slot], packs.at[slot], ss.at[0], rs.at[R["pack"] + slot], me.at(y=ny)).wait_recv()

    def pack_over(z):
        return pack_copy(3 + z, z, me.at(y=ny))

    def pack_step(step):
        @pl.when(l - step >= 0)
        def _():
            pack_wait(2 * (l - step) + y)
            pack_over(l - step).start()

        @pl.when(l + step < LINE)
        def _():
            pack_wait(2 * (l + step) + y)
            pack_over(l + step).start()

    weights = (wup, wdn)

    def ex_ref(n, z, yy):
        return weights[n].at[2 * z + yy]

    def ex_send(n, k, src, dst, recv, device):
        return remote(src, dst, ss.at[S["ex"] + 2 * k + n], rs.at[R["ex"] + recv], device)

    def ex_recv(n, z, yy):
        ref = ex_ref(n, z, yy)
        remote(ref, ref, ss.at[0], rs.at[R["ex"] + 2 * (2 * z + yy) + n], me.at(y=ny)).wait_recv()

    def ex_line(n, k, z, node, src=None):
        ref = ex_ref(n, z, y)
        return ex_send(n, k, ref if src is None else src, ref, 2 * (2 * z + y) + n, me.at(l=node))

    def ex_through(n, src):
        return ex_send(n, 0, src, ring_extra[n].at[0], 16 + n, me.at(l=near))

    def ex_through_wait(n):
        ref = ring_extra[n].at[0]
        remote(ref, ref, ss.at[0], rs.at[R["ex"] + 16 + n], me.at(l=out)).wait_recv()

    def ex_over(n, z):
        ref = ex_ref(n, z, y)
        return remote(ref, ref, ss.at[S["over"] + 2 * z + n], rs.at[R["ex"] + 2 * (2 * z + y) + n], me.at(y=ny))

    def ex_first(n, other):
        @pl.when(outer)
        def _():
            ex_through(n, other).start()
            ex_line(n, 1, l, near).start()

        @pl.when(inside)
        def _():
            ex_line(n, 0, l, far_near, other).start()
            ex_line(n, 1, l, out).start()

        ex_over(n, l).start()

    def relay(step):
        for n in range(2):
            if step == 1:
                @pl.when(inside)
                def _():
                    ex_through_wait(n)
                    ex_line(n, 2, out, far_near, ring_extra[n].at[0]).start()
                    ex_recv(n, far_near, y)
                    ex_line(n, 3, far_near, out).start()
                    ex_over(n, far_near).start()

                @pl.when(outer)
                def _():
                    ex_recv(n, near, y)
                    ex_over(n, near).start()
            elif step == 2:
                @pl.when(inside)
                def _():
                    ex_recv(n, out, y)
                    ex_over(n, out).start()

                @pl.when(outer)
                def _():
                    ex_recv(n, far_near, y)
                    ex_over(n, far_near).start()
            else:
                @pl.when(inside)
                def _():
                    ex_recv(n, far_out, y)
                    ex_line_last(n).start()
                    ex_over(n, far_out).start()

    def ex_line_last(n):
        ref = ex_ref(n, far_out, y)
        return remote(ref, ref, ss.at[S["last"] + n], rs.at[R["ex"] + 2 * (2 * far_out + y) + n], me.at(l=out))

    def wo_copy(k, part, device):
        rows = pl.ds(pl.multiple_of(part * O_ROWS, O_ROWS), O_ROWS)
        return remote(
            wo_all.at[:, rows, :], wo_all.at[:, rows, :], ss.at[S["wo"] + k], rs.at[R["wo"] + k], device
        )

    row_src = (bufs.at[0], bufs.at[1], gate_out)
    row_dst = (rowh, rowg, gate_in)

    def row_copy(n, k, cx, cy):
        return remote(
            row_src[n].at[2 * cy + cx], row_dst[n].at[4 * c + mine], ss.at[S["row"] + 3 * n + k],
            rs.at[R["row"] + 4 * n + mine], me.at(x=cx, l=l + 2 * (cy - side))
        )

    def row_wait(n, cx, cy):
        row, slot = row_dst[n], 2 * cy + cx
        remote(
            row.at[4 * c + slot], row.at[4 * c + slot], ss.at[0], rs.at[R["row"] + 4 * n + slot],
            me.at(x=cx, l=l + 2 * (cy - side))
        ).wait_recv()

    def core_copy(n, k, first, slot):
        row = row_dst[n]
        return remote(
            row.at[first + slot], row.at[first + slot], ss.at[S["core"] + 4 * n + k], rs.at[R["core"] + 4 * n + slot],
            me.at(c=nc)
        )

    def row_send(n):
        for k, (cx, cy) in enumerate(chips):
            row_copy(n, k, cx, cy).start()
        row_dst[n][4 * c + mine] = row_src[n][mine]
        core_copy(n, 0, 4 * c, mine).start()

    def row_pass(n):
        for k, (cx, cy) in enumerate(chips):
            row_wait(n, cx, cy)
            core_copy(n, 1 + k, 4 * c, 2 * cy + cx).start()

    def row_collect(n):
        for slot in range(4):
            core_copy(n, 0, 4 * nc, slot).wait_recv()

    def back_copy(n, k, cx, cy):
        return remote(
            bufs.at[n, 2 * cy + cx], ret.at[n, mine], ss.at[S["back"] + 3 * n + k], rs.at[R["back"] + 4 * n + mine],
            me.at(x=cx, l=l + 2 * (cy - side))
        )

    def back_wait(n, cx, cy):
        slot = 2 * cy + cx
        remote(
            ret.at[n, slot], ret.at[n, slot], ss.at[0], rs.at[R["back"] + 4 * n + slot], me.at(x=cx, l=l + 2 * (cy - side))
        ).wait_recv()

    loads = [
        load(tok, stream.at[q], 0), load(cos_in, cos, 1), load(sin_in, sin, 2), load(gout_in, gout, 3),
    ]
    for copy in loads:
        copy.start()

    ring_extra = (ringx_up, ringx_dn)

    def forward(st_in, st_out, st_up, st_dn, upx, dnx, wo_tiles, wo_mine, wq, wr, pk, begin_col, maps, slot_lanes):
        from_hbm = [load(w_in, st_in, 4), load(w_out, st_out, 5)]
        experts = [2 * side + x, 2 * far + x]
        from_hbm += [load(w_up.at[e], st_up.at[k], 6 + k) for k, e in enumerate(experts)]
        half_rows = pl.ds(pl.multiple_of(128 * c, 128), 128)
        from_hbm += [load(w_dn.at[e, half_rows, :], st_dn.at[k], 8 + k) for k, e in enumerate(experts)]
        for copy in from_hbm:
            copy.start()
        away = l + 2 * (far - side)
        greet([me.at(c=nc), me.at(x=nx), me.at(x=nx, c=nc), me.at(x=nx, l=away)] + shards)
        loads[0].wait()
        tok_copy(1, q, me.at(x=nx)).start()
        tok_copy(0, q, me.at(c=nc)).start()

        from_hbm[0].wait()
        from_hbm[1].wait()
        for t in range(6):
            wo_tiles[96 * t:96 * (t + 1), :] = st_out[:, 128 * t:128 * (t + 1)].astype(BF)
        for part in range(4):

            @pl.when(q == part)
            def _():
                def head(kind, h):
                    first = 192 * part + 64 * h
                    return st_in[kind, :, first:first + 64]

                tiles = [(head(0, h), head(1, h)) for h in range(LOCAL_HEADS)]
                tiles += [(head(2, 0), head(2, 1)), (head(2, 2), jnp.zeros((96, 64), F32))]
                for t, pair in enumerate(tiles):
                    packs[own, 96 * t:96 * (t + 1), :] = jnp.concatenate(pair, axis=1).astype(BF)

        rows = pl.ds(pl.multiple_of(q * O_ROWS, O_ROWS), O_ROWS)
        wo_mine[...] = wo_tiles[rows, :]
        wo_all[own, rows, :] = wo_tiles[rows, :]
        small = jnp.concatenate([router[...], vectors[...]], axis=0)
        small = jnp.concatenate([small, jnp.zeros((16, 32), F32)], axis=1).astype(BF)
        to_col = lax.broadcasted_iota(jnp.int32, (128, D), 1) - 96 * own
        from_row = lax.broadcasted_iota(jnp.int32, (128, D), 0)
        place = ((to_col == from_row) & (from_row < 96)).astype(F32).astype(BF)
        placed = mm(small, place).astype(BF)
        for t in range(6):
            first = A_ROWS + 16 * t
            packs[own, first:first + 16, :] = placed[:, 128 * t:128 * (t + 1)]
        for k in range(3):
            pack_copy(k, l, shards[k]).start()
        pack_over(l).start()

        for k in range(2):
            from_hbm[4 + k].wait()
        wdn[own] = st_dn[0].astype(BF)
        dnx[...] = st_dn[1].astype(BF)
        for k in range(2):
            from_hbm[2 + k].wait()
        for j in range(16):
            part = pl.ds(pl.multiple_of(256 * j + 128 * c, 128), 128)
            wup[own, :, 128 * j:128 * (j + 1)] = st_up[0, :, part].astype(BF)
            upx[:, 128 * j:128 * (j + 1)] = st_up[1, :, part].astype(BF)

        expert = jnp.concatenate([routes[k:k + 1, :] for k in range(TOPK)], axis=1).astype(F32)
        order = jnp.concatenate([priority[...], priority[...] + STREAM], axis=1).astype(F32)
        base = expert * 4096.0
        rank_key = base + order
        key_rows = jnp.transpose(jnp.broadcast_to(rank_key, (128, 2 * TOK)))[:, 0:1]
        ahead = jnp.where((key_rows < rank_key) & (key_rows >= base), 1.0, 0.0)
        rank = jnp.sum(ahead, axis=0, keepdims=True)
        slot = jnp.where((expert < NFFN) & (rank < CAP), expert * CAP + rank, -1.0)
        slots = [slot[:, :TOK], slot[:, TOK:]]
        slot_row = lax.broadcasted_iota(jnp.int32, (NFFN * CAP, TOK), 0).astype(F32)
        for k in range(TOPK):
            slot_lanes[k:k + 1, :] = slots[k]
            maps[k] = (slot_row == slots[k]).astype(F32).astype(BF)
        loads[3].wait()
        bufs[1] = mm(maps[0] + maps[1], gout[...]).astype(BF).reshape(NFFN, CAP, D)

        pack_step(1)
        pack_step(2)
        tok_copy(1, 2 * nx + c, me.at(x=nx)).wait_recv()
        tok_copy(2, 2 * nx + c, me.at(c=nc)).start()
        pack_step(3)
        def wo_send(k):
            return remote(
                wo_mine, wo_all.at[own, rows, :], ss.at[S["wo8"] + k], rs.at[R["wo8"] + own], shards[k]
            )

        def wo_arrive(k):
            slot = 2 * turns[(1, 3, 2, 0, 1, 3, 2)[k]] + (y if k < 3 else ny)
            remote(
                wo_all.at[slot, rows, :], wo_all.at[slot, rows, :], ss.at[0], rs.at[R["wo8"] + slot], shards[k]
            ).wait_recv()

        for k in range(7):
            wo_send(k).start()
        for n, other in enumerate((upx, dnx)):
            ex_first(n, other)
        row_send(1)

        ids = lax.broadcasted_iota(jnp.int32, (8, STREAM), 1)
        first = lengths[0, 0] * 0
        at = jnp.zeros((8, STREAM), jnp.int32)
        for k in range(8):
            at = jnp.maximum(at, jnp.where(ids >= first, first, 0))
            first = first + lengths[0, k]
        begin[...] = at
        begin_col[...] = jnp.transpose(jnp.broadcast_to(at[0:1].astype(F32), (128, STREAM)))

        for z in range(LINE):
            pack_wait(2 * z + ny)
        for s in range(OUTER):
            for t in range(5):
                wq[t, 96 * s:96 * (s + 1), :] = packs[s, 96 * t:96 * (t + 1), :]
        for t in range(LOCAL_HEADS):
            wr[t] = mm(wq[t], turn[...]).astype(BF)
        gain = small_rows(packs)[12:13]
        tok_copy(0, 2 * x + nc, me.at(c=nc)).wait_recv()
        tok_copy(2, 2 * nx + nc, me.at(c=nc)).wait_recv()
        loads[1].wait()
        loads[2].wait()

        halves = jnp.where(lax.broadcasted_iota(jnp.int32, (1, 128), 1) < 64, 0.125, 1.0)

        @pl.loop(0, 4)
        def _(part):
            values = stream[part].astype(F32)
            scale = lax.rsqrt(jnp.mean(values * values, axis=1, keepdims=True) + NORM_EPSILON)
            rows = pl.ds(pl.multiple_of(part * TOK, TOK), TOK)
            low = (values * scale * gain).astype(BF)
            normed[rows, :] = low
            cosine, sine = cos[rows, :], sin[rows, :]
            for h in range(LOCAL_HEADS):
                turned = mm(low, wq[h]) * cosine + mm(low, wr[h]) * sine
                qk[h, rows, :] = (turned * halves).astype(BF)
            both = mm(low, wq[3]).astype(BF)
            vo[0, rows, 0:64] = both[:, :64]
            vo[1, rows, 0:64] = both[:, 64:]
            vo[2, rows, 0:64] = mm(low, wq[4])[:, :64].astype(BF)

        def one_head(h):
            ks[...] = qk[h, :, 64:128]
            for b in range(STREAM // BLOCK):
                first, last = b * BLOCK, (b + 1) * BLOCK
                scores = mm_nt(qk[h, first:last, 0:64], ks[0:last, :])
                col = lax.broadcasted_iota(jnp.int32, (BLOCK, last), 1)
                row = lax.broadcasted_iota(jnp.int32, (BLOCK, last), 0) + first
                starts = begin_col[first:last, 0:1].astype(jnp.int32)
                scores = jnp.where((col >= starts) & (col <= row), scores, NEGATIVE)
                top = jnp.max(scores, axis=1, keepdims=True)
                weight = jnp.exp(scores - top)
                total = jnp.sum(weight, axis=1, keepdims=True)
                vo[h, first:last, 64:128] = (mm(weight.astype(BF), vo[h, 0:last, 0:64]) / total).astype(BF)
                logs = jnp.broadcast_to(top + jnp.log(total), (BLOCK, 128))
                lse[h, :, first:last] = jnp.transpose(logs)[0:8, :]

        att_rows = (slice(0, TOK), slice(TOK, ATT))

        def att_copy(k, piece, to, frm, device):
            part = att_rows[piece]
            return remote(
                pk.at[to, part, :], got.at[frm, part, :], ss.at[S["att"] + 2 * k + piece],
                rs.at[R["att"] + 2 * k + piece], device
            )

        pl.loop(0, 1)(one_head)
        for k in range(7):
            wo_arrive(k)
        wo_copy(1, q, me.at(x=nx)).start()
        wo_copy(0, q, me.at(c=nc)).start()
        relay(1)
        pl.loop(1, 2)(one_head)
        for part in range(4):
            here = slice(part * TOK, (part + 1) * TOK)
            pk[part, 0:TOK, :] = jnp.concatenate([vo[0, here, 64:128], vo[1, here, 64:128]], axis=1)
        for k, (other, device) in enumerate(others):
            att_copy(k, 0, other, q, device).start()
        pl.loop(2, LOCAL_HEADS)(one_head)
        wo_copy(1, 2 * nx + c, me.at(x=nx)).wait_recv()
        wo_copy(2, 2 * nx + c, me.at(c=nc)).start()
        for part in range(4):
            third = [vo[2, part * TOK + k * HALF:part * TOK + (k + 1) * HALF, 64:128] for k in range(2)]
            pk[part, TOK:ATT, :] = jnp.concatenate(third, axis=1)
        for k, (other, device) in enumerate(others):
            att_copy(k, 1, other, q, device).start()
        got[q] = pk[q]
        relay(2)

        wo_copy(0, 2 * x + nc, me.at(c=nc)).wait_recv()
        wo_copy(2, 2 * nx + nc, me.at(c=nc)).wait_recv()
        for s in range(OUTER):
            for t in range(6):
                wo[96 * s:96 * (s + 1), 128 * t:128 * (t + 1)] = wo_all[s, 96 * t:96 * (t + 1), :]
        row_pass(1)
        for k, (other, device) in enumerate(others):
            for piece in range(2):
                att_copy(k, piece, q, other, device).wait_recv()
        pieces = []
        for part in range(4):
            low = got[part, TOK:ATT, :]
            pieces.append(got[part, 0:TOK, :])
            pieces.append(jnp.concatenate([low[:, :64], low[:, 64:]], axis=0))
        whole = jnp.concatenate(pieces, axis=1)
        attended[...] = whole
        middle = stream[q].astype(F32) + mm(whole, wo[...])
        gtokens[...] = middle

        smalls = small_rows(packs)
        scale = lax.rsqrt(jnp.mean(middle * middle, axis=1, keepdims=True) + NORM_EPSILON)
        low = (middle * scale * smalls[13:14]).astype(BF)
        hidden[...] = low
        logits = mm_nt(smalls.astype(BF), low)
        route_logits = logits[0:8] + residual[...]
        expert_row = lax.broadcasted_iota(jnp.int32, (8, TOK), 0)
        picks = [routes[k:k + 1, :] for k in range(TOPK)]
        picked = [
            jnp.sum(jnp.where(expert_row == pick, route_logits, 0.0), axis=0, keepdims=True) for pick in picks
        ]

        def pair_softmax(first, second):
            top = jnp.maximum(first, second)
            one, two = jnp.exp(first - top), jnp.exp(second - top)
            return [one / (one + two), two / (one + two)]

        gates = pair_softmax(*picked)
        coefs = pair_softmax(logits[8:9], logits[9:10]) + pair_softmax(logits[10:11], logits[11:12])
        slots = [slot_lanes[k:k + 1, :] for k in range(TOPK)]
        lanes = gates + coefs + slots + [pick.astype(F32) for pick in picks]
        lanes = jnp.concatenate(lanes + [jnp.zeros((128 - len(lanes), TOK), F32)], axis=0)
        cols[...] = jnp.transpose(lanes)
        bufs[0] = mm(maps[0] + maps[1], low).astype(BF).reshape(NFFN, CAP, D)
        row_send(0)
        slot_gate = jnp.zeros((NFFN * CAP, 1), F32)
        for k in range(TOPK):
            slot_gate = slot_gate + jnp.sum(maps[k].astype(F32) * gates[k], axis=1, keepdims=True)
        high, rest = split_low(slot_gate)
        lane = lax.broadcasted_iota(jnp.int32, (NFFN * CAP, 128), 1)
        packed = jnp.where(lane == 0, high.astype(F32), jnp.where(lane == 1, rest.astype(F32), 0.0))
        gate_out[...] = packed.astype(BF).reshape(NFFN, CAP, 128)
        row_send(2)

        for n, other in enumerate((upx, dnx)):
            @pl.when(outer)
            def _():
                ex_through(n, other).wait_send()

            @pl.when(inside)
            def _():
                ex_line(n, 0, l, far_near, other).wait_send()

        for k, (other, device) in enumerate(others):
            for piece in range(2):
                att_copy(k, piece, other, q, device).wait_send()
        for k in range(7):
            wo_send(k).wait_send()

    pl.run_scoped(
        forward,
        pltpu.VMEM((3, 96, D), F32),
        pltpu.VMEM((96, D), F32),
        pltpu.VMEM((2, 96, 2 * FF), F32),
        pltpu.VMEM((2, 128, D), F32),
        pltpu.VMEM((96, FF), BF),
        pltpu.VMEM((128, D), BF),
        pltpu.VMEM((576, 128), BF),
        pltpu.VMEM((O_ROWS, 128), BF),
        pltpu.VMEM((5, D, 128), BF),
        pltpu.VMEM((3, D, 128), BF),
        pltpu.VMEM((4, ATT, 128), BF),
        pltpu.VMEM((STREAM, 128), F32),
        pltpu.VMEM((TOPK, NFFN * CAP, TOK), BF),
        pltpu.VMEM((8, TOK), F32),
    )
    relay(3)
    row_pass(0)
    row_pass(2)
    row_collect(1)
    row_collect(0)

    def experts(rowt, total, part_out, act, slope_gate, slope_lin):
        rowt[...] = jnp.transpose(rowh[...].reshape(8 * CAP, D).astype(F32)).astype(BF)
        total[...] = jnp.zeros_like(total)
        for n in range(2):
            @pl.when(outer)
            def _():
                ex_recv(n, far_out, y)
                ex_over(n, far_out).start()

            for z in range(LINE):
                ex_recv(n, z, ny)

        def swap(n):
            return remote(
                part_out.at[n], part_in.at[n], ss.at[S["part"] + n], rs.at[R["part"] + n], me.at(c=nc)
            )

        away = pl.ds(pl.multiple_of(nc * 4 * CAP, 4 * CAP), 4 * CAP)
        here = pl.ds(pl.multiple_of(c * 4 * CAP, 4 * CAP), 4 * CAP)

        def swap_start(n):
            part_out[n] = total[away, :].astype(BF).reshape(4, CAP, D)
            swap(n).start()

        def give_back(n):
            swap(n).wait_recv()
            bufs[n] = (total[here, :].reshape(4, CAP, D) + part_in[n].astype(F32)).astype(BF)
            for k, (cx, cy) in enumerate(chips):
                back_copy(n, k, cx, cy).start()
            ret[n, mine] = bufs[n, mine]

        def columns(j):
            gate_cols = pl.ds(pl.multiple_of(j * 256, 256), 256)
            return gate_cols, pl.ds(pl.multiple_of(1024 + j * 256, 256), 256)

        @pl.loop(0, 4)
        def _(j):
            gate_cols, lin_cols = columns(j)
            rows_h = rowh[...].reshape(8 * CAP, D)
            gate = mm(rows_h, wup[:, :, gate_cols].reshape(D, 256))
            lin = mm(rows_h, wup[:, :, lin_cols].reshape(D, 256))
            sigma = jax.nn.sigmoid(gate)
            silu = gate * sigma
            low = (silu * lin).astype(BF)
            act[:, gate_cols] = low
            slope_gate[:, gate_cols] = (lin * sigma * (1.0 + gate * (1.0 - sigma))).astype(BF)
            slope_lin[:, gate_cols] = silu.astype(BF)
            total[...] += mm(low, wdn[pl.ds(2 * j, 2)].reshape(256, D))

        for n in range(3):
            for k, (cx, cy) in enumerate(chips):
                row_copy(n, k, cx, cy).wait_send()
        swap_start(0)
        row_collect(2)
        for n in range(3):
            core_copy(n, 0, 4 * c, mine).wait_send()
            for k, (cx, cy) in enumerate(chips):
                core_copy(n, 1 + k, 4 * c, 2 * cy + cx).wait_send()
        for slot in range(8):
            gate = gate_in[slot].astype(F32)
            rowg[slot] = ((gate[:, 0:1] + gate[:, 1:2]) * rowg[slot].astype(F32)).astype(BF)
        give_back(0)
        total[...] = jnp.zeros_like(total)

        @pl.loop(0, 4)
        def _(j):
            gate_cols, lin_cols = columns(j)
            rows_g = rowg[...].reshape(8 * CAP, D)
            grad_act = mm_nt(rows_g, wdn[pl.ds(2 * j, 2)].reshape(256, D))
            grad_gate = (grad_act * slope_gate[:, gate_cols].astype(F32)).astype(BF)
            grad_lin = (grad_act * slope_lin[:, gate_cols].astype(F32)).astype(BF)
            total[...] += mm_nt(grad_gate, wup[:, :, gate_cols].reshape(D, 256))
            total[...] += mm_nt(grad_lin, wup[:, :, lin_cols].reshape(D, 256))
            gdn[pl.ds(2 * j, 2)] = mm_tn(act[:, gate_cols], rows_g).astype(BF).reshape(2, 128, D)
            gup[:, :, gate_cols] = mm(rowt[...], grad_gate).astype(BF).reshape(8, 96, 256)
            gup[:, :, lin_cols] = mm(rowt[...], grad_lin).astype(BF).reshape(8, 96, 256)

        swap_start(1)
        for n in range(2):
            @pl.when(outer)
            def _():
                ex_line(n, 1, l, near).wait_send()

            @pl.when(inside)
            def _():
                ex_line(n, 1, l, out).wait_send()
                ex_line(n, 2, out, far_near, ring_extra[n].at[0]).wait_send()
                ex_line(n, 3, far_near, out).wait_send()
                ex_line_last(n).wait_send()

            for z in range(LINE):
                ex_over(n, z).wait_send()

        @pl.when(l < LINE - 1)
        def _():
            pl.semaphore_signal(ready.at[0], inc=1, device_id=me.at(l=l + 1), device_id_type=MESH)

        @pl.when(l > 0)
        def _():
            pl.semaphore_signal(ready.at[1], inc=1, device_id=me.at(l=l - 1), device_id_type=MESH)

        pl.semaphore_signal(ready.at[2], inc=1, device_id=me.at(y=ny), device_id_type=MESH)

        @pl.when(outer)
        def _():
            pl.semaphore_signal(ready.at[3], inc=1, device_id=me.at(l=far_near), device_id_type=MESH)


        give_back(1)
        for n in range(2):
            swap(n).wait_send()

    pl.run_scoped(
        experts,
        pltpu.VMEM((D, 8 * CAP), BF),
        pltpu.VMEM((8 * CAP, D), F32),
        pltpu.VMEM((2, 4, CAP, D), BF),
        pltpu.VMEM((8 * CAP, 1024), BF),
        pltpu.VMEM((8 * CAP, 1024), BF),
        pltpu.VMEM((8 * CAP, 1024), BF),
    )

    grads = (gup, gdn)

    def room(n, i):
        return weights[n].at[i] if isinstance(i, jax.Array) or i < 8 else ring_extra[n].at[0]

    pieces = [far_out, far_near, mate, l]

    def pair_copy(n, j):
        z = pieces[j]
        return remote(
            grads[n].at[2 * z + ny], weights[n].at[z], ss.at[S["pair"] + 2 * j + n], rs.at[R["pair"] + 2 * j + n],
            me.at(y=ny)
        )

    def line_copy(n, k, src, to, node):
        return remote(
            src, room(n, to), ss.at[S["line"] + 2 * k + n], rs.at[R["line"] + 2 * (to - 4) + n], me.at(l=node)
        )

    def line_wait(n, to):
        remote(room(n, to), room(n, to), ss.at[0], rs.at[R["line"] + 2 * (to - 4) + n], me.at(y=ny)).wait_recv()

    def add(n, into, other):
        rows = grads[n].shape[1]

        @pl.loop(0, rows // 16)
        def _(r):
            part = pl.ds(pl.multiple_of(r * 16, 16), 16)
            into[part, :] = (into[part, :].astype(F32) + other[part, :].astype(F32)).astype(BF)

    def pair_end(n, j):
        pair_copy(n, j).wait_recv()
        add(n, weights[n].at[pieces[j]], grads[n].at[2 * pieces[j] + y])

    def line_step(j):
        for n in range(2):
            pair_end(n, j)
            if j == 2:
                line_copy(n, 2, weights[n].at[mate], 8, mate).start()
                continue

            @pl.when(outer)
            def _():
                line_copy(n, j, weights[n].at[pieces[j]], 4 + j, near).start()

    def line_cross(j):
        for n in range(2):
            @pl.when(inside)
            def _():
                if j == 0 and n == 0:
                    pl.semaphore_wait(ready.at[3], 1)
                line_wait(n, 4 + j)
                add(n, weights[n].at[4 + j], weights[n].at[pieces[j]])
                line_copy(n, j, weights[n].at[4 + j], 7, (far_out, far_near)[j]).start()

    @pl.when(l < LINE - 1)
    def _():
        pl.semaphore_wait(ready.at[1], 1)

    @pl.when(l > 0)
    def _():
        pl.semaphore_wait(ready.at[0], 1)

    pl.semaphore_wait(ready.at[2], 1)
    def pair_start(j):
        for n in range(2):
            pair_copy(n, j).start()

    pair_start(0)
    pair_start(1)

    for n in range(2):
        for cx, cy in chips:
            back_wait(n, cx, cy)
    smalls = small_rows(packs)
    down_rows = ret[0].reshape(NFFN * CAP, D)
    back_rows = ret[1].reshape(NFFN * CAP, D)
    vector = [smalls[14 + j:15 + j] for j in range(2)]
    router_row = lax.broadcasted_iota(jnp.int32, (16, 1), 0)
    router_low = jnp.where(router_row < 12, smalls, 0.0)
    router_low = jnp.concatenate([router_low, jnp.zeros((112, D), F32)], axis=0).astype(BF)
    facts[...] = jnp.zeros_like(facts)

    @pl.loop(0, TOK // ROWS)
    def _(i):
        rows = pl.ds(pl.multiple_of(i * ROWS, ROWS), ROWS)
        middle = gtokens[rows, :]
        low = hidden[rows, :]
        grad_low = gout[rows, :]
        info = cols[rows, :]
        token_lane = lax.broadcasted_iota(jnp.int32, (ROWS, NFFN * CAP), 1).astype(F32)
        gates = [info[:, k:k + 1] for k in range(TOPK)]
        coefs = [[info[:, 2 + 2 * j:3 + 2 * j], info[:, 3 + 2 * j:4 + 2 * j]] for j in range(2)]
        spread = [(token_lane == info[:, 6 + k:7 + k]).astype(F32).astype(BF) for k in range(TOPK)]
        picks = [info[:, 8 + k:9 + k] for k in range(TOPK)]
        chosen = [[(pick == e).astype(F32) for e in (5.0, 6.0, 7.0)] for pick in picks]
        grad_top = grad_low.astype(F32)
        value_hidden = low.astype(F32)
        grad_gate, mixture = [], middle
        for k in range(TOPK):
            copy, one, two = chosen[k]
            value = mm(spread[k], down_rows)
            value = value + (copy + one * coefs[0][0] + two * coefs[1][0]) * value_hidden
            value = value + (one * coefs[0][1]) * vector[0] + (two * coefs[1][1]) * vector[1]
            mixture = mixture + gates[k] * value
            grad_gate.append(jnp.sum(grad_top * value, axis=1, keepdims=True))
        layer_out[rows, :] = mixture.astype(BF)
        mean_gate = gates[0] * grad_gate[0] + gates[1] * grad_gate[1]
        grad_pick = [gates[k] * (grad_gate[k] - mean_gate) for k in range(TOPK)]
        lane = lax.broadcasted_iota(jnp.int32, (ROWS, 128), 1).astype(F32)
        grad_logits = sum(jnp.where(lane == picks[k], grad_pick[k], 0.0) for k in range(TOPK))
        groute[rows, :] = grad_logits[:, :NEXP]
        on_hidden = jnp.sum(grad_top * value_hidden, axis=1, keepdims=True)
        direct = gates[0] * chosen[0][0] + gates[1] * chosen[1][0]
        on_vectors = jnp.zeros((ROWS, 128), F32)
        for j in range(2):
            weight = gates[0] * chosen[0][1 + j] + gates[1] * chosen[1][1 + j]
            direct = direct + weight * coefs[j][0]
            grad_coef = [weight * on_hidden, weight * jnp.sum(grad_top * vector[j], axis=1, keepdims=True)]
            mean_coef = coefs[j][0] * grad_coef[0] + coefs[j][1] * grad_coef[1]
            for n in range(2):
                grad_logits = grad_logits + jnp.where(
                    lane == 8.0 + 2 * j + n, coefs[j][n] * (grad_coef[n] - mean_coef), 0.0
                )
            on_vectors = on_vectors + jnp.where(lane == 14.0 + j, weight * coefs[j][1], 0.0)
        logit_parts = split_low(grad_logits)
        vector_parts = split_low(on_vectors)
        grad_hidden = direct * grad_top + mm(spread[0] + spread[1], back_rows)
        grad_hidden = grad_hidden + mm(logit_parts[0], router_low) + mm(logit_parts[1], router_low)
        small_sum = mm_tn(logit_parts[0], low) + mm_tn(logit_parts[1], low)
        small_sum = small_sum + mm_tn(vector_parts[0], grad_low) + mm_tn(vector_parts[1], grad_low)
        scale = lax.rsqrt(jnp.mean(middle * middle, axis=1, keepdims=True) + NORM_EPSILON)
        normal = middle * scale
        gain_sum = jnp.sum(grad_hidden * normal, axis=0, keepdims=True)
        facts[...] += small_sum[0:16] + jnp.where(router_row == 13, gain_sum, 0.0)
        inner_term = grad_hidden * smalls[13:14]
        gtokens[rows, :] = grad_top + scale * (
            inner_term - normal * jnp.mean(inner_term * normal, axis=1, keepdims=True)
        )

    def al_copy(p, k):
        z, rows = turns[(1, 3, 2)[k]], A_PARTS[p]
        return remote(
            ap_in.at[z, rows, :], ap_line.at[l, rows, :], ss.at[S["al"] + 3 * p + k], rs.at[R["al"] + 4 * p + l], shards[k]
        )

    def backward(pk, kt, grad, dq, dv, dk_sum, dv_sum, delta, gr, wall, ap):
        line_step(0)
        pair_start(2)
        grad_att = mm_nt(gtokens[...].astype(BF), wo[...])
        for part in range(4):
            wide = grad_att[:, 192 * part:192 * (part + 1)]
            pk[part, 0:TOK, :] = wide[:, :128].astype(BF)
            third = wide[:, 128:]
            pk[part, TOK:ATT, :] = jnp.concatenate([third[:HALF], third[HALF:]], axis=1).astype(BF)
        got[q] = pk[q]

        def att_copy(k, to, frm, device):
            return remote(pk.at[to], got.at[frm], ss.at[S["att2"] + k], rs.at[R["att2"] + k], device)

        for k, (other, device) in enumerate(others):
            att_copy(k, other, q, device).start()

        wo_copy(1, q, me.at(x=nx)).wait_send()
        wo_copy(0, q, me.at(c=nc)).wait_send()
        wo_copy(2, 2 * nx + c, me.at(c=nc)).wait_send()

        @pl.loop(0, 2)
        def _(i):
            wide = pl.ds(pl.multiple_of(i * 384, 384), 384)
            grad_wo = mm_tn(attended[:, wide], gtokens[...].astype(BF)).astype(BF)
            for s in range(4):
                for t in range(6):
                    tile = grad_wo[96 * s:96 * (s + 1), 128 * t:128 * (t + 1)]
                    wo_all[4 * i + s, 96 * t:96 * (t + 1), :] = tile

        def wo_rows(part):
            return pl.ds(pl.multiple_of(part * O_ROWS, O_ROWS), O_ROWS)

        def wo_share(k, to, device):
            return remote(
                wo_all.at[:, wo_rows(to), :], wo_in.at[k], ss.at[S["wo2"] + k], rs.at[R["wo2"] + k], device
            )

        for s in range(OUTER):
            for t in range(5):
                wall[96 * s:96 * (s + 1), 128 * t:128 * (t + 1)] = packs[s, 96 * t:96 * (t + 1), :]

        for k, (other, device) in enumerate(others):
            att_copy(k, q, other, device).wait_recv()
        for k, (other, device) in enumerate(others):
            wo_share(k, other, device).start()
        for part in range(4):
            rows = slice(part * TOK, (part + 1) * TOK)
            both = got[part, 0:TOK, :]
            third = got[part, TOK:ATT, :]
            grad[0, rows, :] = both[:, :64]
            grad[1, rows, :] = both[:, 64:]
            grad[2, rows, :] = jnp.concatenate([third[:, :64], third[:, 64:]], axis=0)
        for h in range(LOCAL_HEADS):
            dots = jnp.sum(grad[h].astype(F32) * vo[h, :, 64:128].astype(F32), axis=1, keepdims=True)
            delta[h] = jnp.transpose(jnp.broadcast_to(dots, (STREAM, 128)))[0:8, :]

        def one_head(h):
            ks[...] = qk[h, :, 64:128]
            kt[...] = jnp.transpose(ks[...].astype(F32)).astype(BF)
            dk_sum[...] = jnp.zeros((STREAM, 64), F32)
            dv_sum[...] = jnp.zeros((STREAM, 64), F32)
            for b in range(STREAM // BLOCK):
                first, last = b * BLOCK, (b + 1) * BLOCK
                q_rows, g_rows = qk[h, first:last, 0:64], grad[h, first:last, :]
                grad_q = jnp.zeros((64, BLOCK), F32)
                for start in range(0, last, KEYS):
                    keys = slice(start, min(start + KEYS, last))
                    size = keys.stop - start
                    scores = mm_nt(ks[keys, :], q_rows)
                    key = lax.broadcasted_iota(jnp.int32, (size, BLOCK), 0) + start
                    col = lax.broadcasted_iota(jnp.int32, (size, BLOCK), 1) + first
                    seen = (key >= begin[0:1, first:last]) & (key <= col)
                    probs = jnp.exp(jnp.where(seen, scores, NEGATIVE) - lse[h, 0:1, first:last])
                    grad_probs = mm_nt(vo[h, keys, 0:64], g_rows)
                    grad_scores = (probs * (grad_probs - delta[h, 0:1, first:last])).astype(BF)
                    dv_sum[keys, :] += mm(probs.astype(BF), g_rows)
                    dk_sum[keys, :] += mm(grad_scores, q_rows)
                    grad_q = grad_q + mm(kt[:, keys], grad_scores)
                dq[first:last, :] = (jnp.transpose(grad_q) * 0.125).astype(BF)
            dv[h] = dv_sum[...].astype(BF)
            for part in range(4):
                rows = slice(part * TOK, (part + 1) * TOK)
                turned = jnp.concatenate([dq[rows, :], dk_sum[rows, :].astype(BF)], axis=1)
                raw = turned.astype(F32) * cos[rows, :] - mm(turned, turn[...]) * sin[rows, :]
                gr[rows, pl.ds(pl.multiple_of(h * 128, 128), 128)] = raw.astype(BF)

        def grad_tiles(first, last):
            @pl.loop(0, 2)
            def _(i):
                wide = pl.ds(pl.multiple_of(i * 384, 384), 384)
                grad_a = mm_tn(normed[:, wide], gr[:, 128 * first:128 * last]).astype(BF)
                for s in range(4):
                    for t in range(first, last):
                        tile = grad_a[96 * s:96 * (s + 1), 128 * (t - first):128 * (t - first + 1)]
                        ap[4 * i + s, 96 * t:96 * (t + 1), :] = tile

        def ay_copy(p, z):
            rows = A_PARTS[p]
            return remote(
                ap.at[2 * z + ny, rows, :], ap_in.at[z, rows, :], ss.at[S["ay"] + 4 * p + z],
                rs.at[R["ay"] + 4 * p + z], me.at(y=ny)
            )

        def ay_start(p):
            for z in range(LINE):
                ay_copy(p, z).start()

        def ay_end(p):
            rows = A_PARTS[p]
            for z in range(LINE):
                ay_copy(p, z).wait_recv()
                ap_in[z, rows, :] = (ap[2 * z + y, rows, :].astype(F32) + ap_in[z, rows, :].astype(F32)).astype(BF)
            for k in range(3):
                al_copy(p, k).start()

        pl.loop(0, 1)(one_head)
        line_step(1)
        line_cross(0)
        pl.loop(1, 2)(one_head)
        grad_tiles(0, 2)
        ay_start(0)
        pair_start(3)
        pl.loop(2, LOCAL_HEADS)(one_head)
        line_cross(1)
        for part in range(4):
            rows = slice(part * TOK, (part + 1) * TOK)
            gr[rows, 384:512] = jnp.concatenate([dv[0, rows, :], dv[1, rows, :]], axis=1)
            gr[rows, 512:640] = jnp.concatenate([dv[2, rows, :], jnp.zeros((TOK, 64), BF)], axis=1)

        grad_tiles(2, 5)
        for k, (other, device) in enumerate(others):
            wo_share(k, q, device).wait_recv()
        wo_total = wo_all[:, wo_rows(q), :].astype(F32)
        for k in range(3):
            wo_total = wo_total + wo_in[k].astype(F32)
        ap[:, A_ROWS:A_ROWS + O_ROWS, :] = wo_total.astype(BF)
        ay_start(1)

        for n in range(2):
            for k, (cx, cy) in enumerate(chips):
                back_copy(n, k, cx, cy).wait_send()
        gain_sum = jnp.zeros((1, D), F32)
        for part in range(4):
            rows = slice(part * TOK, (part + 1) * TOK)
            grad_n = mm_nt(gr[rows, :], wall[...])
            values = stream[part].astype(F32)
            scale = lax.rsqrt(jnp.mean(values * values, axis=1, keepdims=True) + NORM_EPSILON)
            gain_sum = gain_sum + jnp.sum(grad_n * (values * scale), axis=0, keepdims=True)
            first = 4 * (part % 2)
            (rowh, rowg)[part // 2][first:first + 4] = grad_n.astype(BF).reshape(4, CAP, D)

        def gn_swap(a):
            row = (rowh, rowg)[a]
            return remote(
                row.at[pl.ds(4 * nc, 4)], part_in.at[a], ss.at[S["gn"] + a], rs.at[R["gn"] + a], me.at(c=nc)
            )

        for a in range(2):
            gn_swap(a).start()
        small_all = facts[...] + jnp.where(router_row == 12, gain_sum, 0.0)
        for s in range(OUTER):
            piece = jnp.concatenate([small_all[:, 96 * s:96 * (s + 1)], jnp.zeros((16, 32), F32)], axis=1)
            ap[s, A_ROWS + O_ROWS:PACKG, :] = piece.astype(BF)

        ay_start(2)
        ay_end(0)
        line_step(2)
        for a in range(2):
            gn_swap(a).wait_recv()
            bufs[a] = ((rowh, rowg)[a][pl.ds(4 * c, 4)].astype(F32) + part_in[a].astype(F32)).astype(BF)
        gn_over = remote(bufs.at[nx], gn_ret, ss.at[S["gn"] + 2], rs.at[R["gn"] + 2], me.at(x=nx))
        gn_over.start()
        ay_end(1)
        ay_end(2)
        for k, (other, device) in enumerate(others):
            att_copy(k, other, q, device).wait_send()
            wo_share(k, other, device).wait_send()
        for a in range(2):
            gn_swap(a).wait_send()
        for p in range(3):
            for z in range(LINE):
                ay_copy(p, z).wait_send()

    heads = (LOCAL_HEADS, STREAM, 64)
    pl.run_scoped(
        backward,
        pltpu.VMEM((4, ATT, 128), BF),
        pltpu.VMEM((64, STREAM), BF),
        pltpu.VMEM(heads, BF),
        pltpu.VMEM((STREAM, 64), BF),
        pltpu.VMEM(heads, BF),
        pltpu.VMEM((STREAM, 64), F32),
        pltpu.VMEM((STREAM, 64), F32),
        pltpu.VMEM((LOCAL_HEADS, 8, STREAM), F32),
        pltpu.VMEM((STREAM, 640), BF),
        pltpu.VMEM((D, 640), BF),
        pltpu.VMEM((OUTER, PACKG, 128), BF),
    )

    def aa_copy(p, k, part, device):
        rows = A_PARTS[p]
        return remote(
            apack.at[part, rows, :], apack.at[part, rows, :], ss.at[S["aa"] + 3 * p + k], rs.at[R["aa"] + 3 * p + k], device
        )

    def al_end(p):
        rows = A_PARTS[p]
        total = ap_in[l, rows, :].astype(F32)
        for k in range(3):
            z = turns[(1, 3, 2)[k]]
            ref = ap_line.at[z, rows, :]
            remote(ref, ref, ss.at[0], rs.at[R["al"] + 4 * p + z], shards[k]).wait_recv()
            total = total + ap_line[z, rows, :].astype(F32)
        apack[q, rows, :] = total.astype(BF)
        for k, (other, device) in enumerate(others):
            aa_copy(p, k, q, device).start()

    spread_out = (gup_all, gdn_all)

    def gp_slot(k, cx, cc):
        return 2 * (2 * (side if k == 0 else far) + cx) + cc

    def gp_src(n, k):
        return ring_extra[n].at[0] if k == 0 else weights[n].at[7]

    def gp_over(n, k):
        slot = gp_slot(k, x, c)
        return remote(
            gp_src(n, k), spread_out[n].at[slot], ss.at[S["gp"] + 6 * n + k], rs.at[R["gp"] + 8 * n + slot], me.at(x=nx)
        )

    def gp_wait(n, slot):
        ref = spread_out[n].at[slot]
        remote(ref, ref, ss.at[0], rs.at[R["gp"] + 8 * n + slot], me.at(c=nc)).wait_recv()

    def gp_own(n, k):
        return pltpu.make_async_copy(gp_src(n, k), spread_out[n].at[gp_slot(k, x, c)], ls.at[10 + 2 * n + k])

    def gp_core(n, k):
        slot = gp_slot(k, x, c)
        return remote(
            gp_src(n, k), spread_out[n].at[slot], ss.at[S["gp"] + 6 * n + 2 + k], rs.at[R["gp"] + 8 * n + slot],
            me.at(c=nc)
        )

    def gp_pass(n, k):
        slot = gp_slot(k, nx, c)
        ref = spread_out[n].at[slot]
        return remote(ref, ref, ss.at[S["gp"] + 6 * n + 4 + k], rs.at[R["gp"] + 8 * n + slot], me.at(c=nc))

    def gp_start(n, k):
        gp_over(n, k).start()
        gp_own(n, k).start()
        gp_core(n, k).start()

    def line_other():
        for n in range(2):
            line_wait(n, 7)
            gp_start(n, 1)

    def line_own():
        for n in range(2):
            pair_end(n, 3)
            line_wait(n, 8)
            add(n, ring_extra[n].at[0], weights[n].at[l])
            gp_start(n, 0)

    al_end(0)

    gn_over = remote(bufs.at[nx], gn_ret, ss.at[S["gn"] + 2], rs.at[R["gn"] + 2], me.at(x=nx))
    gn_over.wait_recv()
    values = stream[q].astype(F32)
    scale = lax.rsqrt(jnp.mean(values * values, axis=1, keepdims=True) + NORM_EPSILON)
    normal = values * scale
    grad_n = (bufs[x].astype(F32) + gn_ret[...].astype(F32)).reshape(TOK, D)
    inner_term = grad_n * small_rows(packs)[12:13]
    gtokens[...] = gtokens[...] + scale * (
        inner_term - normal * jnp.mean(inner_term * normal, axis=1, keepdims=True)
    )

    line_other()
    al_end(1)
    al_end(2)
    line_own()

    for k in (1, 0):
        for n in range(2):
            gp_wait(n, gp_slot(k, nx, c))
            gp_pass(n, k).start()
    for k in range(2):
        for n in range(2):
            gp_wait(n, gp_slot(k, x, nc))
            gp_wait(n, gp_slot(k, nx, nc))
    for p in range(3):
        for k, (other, device) in enumerate(others):
            aa_copy(p, k, other, device).wait_recv()

    tok_copy(1, q, me.at(x=nx)).wait_send()
    tok_copy(0, q, me.at(c=nc)).wait_send()
    tok_copy(2, 2 * nx + c, me.at(c=nc)).wait_send()
    gn_over.wait_send()
    for p in range(3):
        for k, (other, device) in enumerate(others):
            aa_copy(p, k, q, device).wait_send()
            al_copy(p, k).wait_send()
    for n in range(2):
        for k in range(2):
            gp_over(n, k).wait_send()
            gp_core(n, k).wait_send()
            gp_pass(n, k).wait_send()
            gp_own(n, k).wait()
        for j in range(4):
            pair_copy(n, j).wait_send()
        line_copy(n, 2, weights[n].at[mate], 8, mate).wait_send()

        @pl.when(outer)
        def _():
            for j in range(2):
                line_copy(n, j, weights[n].at[pieces[j]], 4 + j, near).wait_send()

        @pl.when(inside)
        def _():
            for j in range(2):
                line_copy(n, j, weights[n].at[4 + j], 7, (far_out, far_near)[j]).wait_send()

    for k in range(3):
        pack_copy(k, l, shards[k]).wait_send()
    for z in range(LINE):
        pack_over(z).wait_send()


def layer_call(inner, *args):
    vm = pl.BlockSpec(memory_space=pltpu.VMEM)
    hbm = pl.BlockSpec(memory_space=pl.ANY)
    smem = pl.BlockSpec(memory_space=pltpu.SMEM)
    heads = (LOCAL_HEADS, STREAM, 64)
    wide = (LOCAL_HEADS, STREAM, 128)
    _, _, sends, recvs = semaphores()
    scratch = [
        ((4, TOK, D), BF), ((OUTER, PACK, 128), BF), ((OUTER, 576, 128), BF), ((D, D), BF),
        ((OUTER, 96, FF), BF), ((OUTER, 128, D), BF), ((1, 96, FF), BF), ((1, 128, D), BF),
        ((OUTER, 96, FF), BF), ((OUTER, 128, D), BF),
        ((8, CAP, D), BF), ((8, CAP, D), BF), ((2, 4, CAP, D), BF), ((2, 4, CAP, D), BF),
        ((4, ATT, 128), BF), ((3, OUTER, O_ROWS, 128), BF),
        ((LINE, PACKG, 128), BF), ((LINE, PACKG, 128), BF), ((4, CAP, D), BF),
        ((STREAM, D), BF), (wide, BF), (wide, BF), ((STREAM, 64), BF), ((LOCAL_HEADS, 8, STREAM), F32),
        ((TOK, D), BF), ((TOK, D), BF), ((STREAM, 128), F32), ((STREAM, 128), F32), ((TOK, D), BF),
        ((2, 4, CAP, D), BF), ((8, STREAM), jnp.int32), ((TOK, 128), F32), ((16, D), F32),
        ((4, CAP, 128), BF), ((8, CAP, 128), BF),
    ]
    return pl.pallas_call(
        functools.partial(layer_kernel, inner),
        out_shape=[
            jax.ShapeDtypeStruct((TOK, D), BF),
            jax.ShapeDtypeStruct((TOK, D), F32),
            jax.ShapeDtypeStruct((TOK, NEXP), F32),
            jax.ShapeDtypeStruct((4, PACKG, 128), BF),
            jax.ShapeDtypeStruct((8, 96, FF), BF),
            jax.ShapeDtypeStruct((8, 128, D), BF),
        ],
        in_specs=[hbm] * 8 + [vm, smem] + [vm] * 5,
        out_specs=[vm] * 4 + [hbm] * 2,
        scratch_shapes=[pltpu.VMEM(s, t) for s, t in scratch]
        + [
            pltpu.SemaphoreType.DMA((sends,)),
            pltpu.SemaphoreType.DMA((recvs,)),
            pltpu.SemaphoreType.DMA((14,)),
            pltpu.SemaphoreType.REGULAR((4,)),
        ],
        compiler_params=pltpu.CompilerParams(
            collective_id=0, has_side_effects=True, vmem_limit_bytes=VMEM_LIMIT
        ),
        name="layer",
    )(*args)


def adam(weight, grad, first, second, rate, decay):
    first_new = MOMENT_DECAY * first + (1.0 - MOMENT_DECAY) * grad
    second_new = MOMENT_DECAY * second + (1.0 - MOMENT_DECAY) * grad * grad
    correction = 1.0 - MOMENT_DECAY**STEP
    update = first_new / correction / (jnp.sqrt(second_new / correction) + ADAM_EPSILON)
    return weight - rate * (update + decay * weight), first_new, second_new


UP_PARTS = 2


def update_kernel(
    apack, gu, gd,
    in_w, in_m, in_v, out_w, out_m, out_v, rt_w, rt_m, rt_v, vec_w, vec_m, vec_v,
    up_w, up_m, up_v, dn_w, dn_m, dn_v,
    in_w2, in_m2, in_v2, out_w2, out_m2, out_v2, rt_w2, rt_m2, rt_v2, vec_w2, vec_m2, vec_v2,
    up_w2, up_m2, up_v2, dn_w2, dn_m2, dn_v2,
):
    step = pl.program_id(0)

    for j in range(16):
        cols, part = slice(256 * j, 256 * (j + 1)), slice(128 * j, 128 * (j + 1))
        grad = jnp.concatenate([gu[0, :, part], gu[1, :, part]], axis=1).astype(F32)
        new = adam(up_w[0, :, cols], grad, up_m[0, :, cols], up_v[0, :, cols], STEP_RATES[2], STEP_DECAYS[2])
        up_w2[0, :, cols], up_m2[0, :, cols], up_v2[0, :, cols] = new
    for half in range(2):
        rows = slice(128 * half, 128 * (half + 1))
        grad = gd[half].astype(F32)
        new = adam(dn_w[0, rows, :], grad, dn_m[0, rows, :], dn_v[0, rows, :], STEP_RATES[3], STEP_DECAYS[3])
        dn_w2[0, rows, :], dn_m2[0, rows, :], dn_v2[0, rows, :] = new

    @pl.when(step == 0)
    def _():
        tiles = [[apack[p, 96 * t:96 * (t + 1), :].astype(F32) for t in range(5)] for p in range(4)]
        for kind in range(3):
            pieces = []
            for p in range(4):
                if kind < 2:
                    pieces += [tiles[p][h][:, 64 * kind:64 * kind + 64] for h in range(LOCAL_HEADS)]
                else:
                    pieces += [tiles[p][3][:, :64], tiles[p][3][:, 64:], tiles[p][4][:, :64]]
            grad = jnp.concatenate(pieces, axis=1)
            new = adam(in_w[kind], grad, in_m[kind], in_v[kind], STEP_RATES[0], STEP_DECAYS[0])
            in_w2[kind], in_m2[kind], in_v2[kind] = new
        rows = jnp.concatenate([apack[p, A_ROWS:A_ROWS + O_ROWS, :] for p in range(4)], axis=0)
        for t in range(6):
            cols = slice(128 * t, 128 * (t + 1))
            grad = rows[96 * t:96 * (t + 1), :].astype(F32)
            new = adam(out_w[:, cols], grad, out_m[:, cols], out_v[:, cols], STEP_RATES[1], STEP_DECAYS[1])
            out_w2[:, cols], out_m2[:, cols], out_v2[:, cols] = new
        small = jnp.zeros((16, 128), F32)
        for p in range(4):
            small = small + apack[p, A_ROWS + O_ROWS:A_ROWS + O_ROWS + 16, :].astype(F32)
        new = adam(vec_w[...], small[12:, :96], vec_m[...], vec_v[...], STEP_RATES[5], STEP_DECAYS[5])
        vec_w2[...], vec_m2[...], vec_v2[...] = new
        new = adam(rt_w[...], small[:12, :96], rt_m[...], rt_v[...], STEP_RATES[4], STEP_DECAYS[4])
        rt_w2[...], rt_m2[...], rt_v2[...] = new


def update_call(apack, gu, gd, states):
    flat = [a for group in states for a in group]

    def whole(a):
        return pl.BlockSpec(a.shape, lambda e: (0,) * a.ndim)

    def by_expert(a):
        return pl.BlockSpec((1,) + a.shape[1:], lambda e: (e, 0, 0))

    specs = [whole(a) for a in flat[:12]] + [by_expert(a) for a in flat[12:]]
    pairs = [pl.BlockSpec((2,) + a.shape[1:], lambda e: (e, 0, 0)) for a in (gu, gd)]
    return pl.pallas_call(
        update_kernel,
        grid=(NFFN,),
        out_shape=[jax.ShapeDtypeStruct(a.shape, a.dtype) for a in flat],
        in_specs=[whole(apack)] + pairs + specs,
        out_specs=specs,
        compiler_params=pltpu.CompilerParams(vmem_limit_bytes=56 * 2**20),
        name="update",
    )(apack, gu, gd, *flat)


def gather_inner(values, axis, inner):
    if inner == 1:
        return values
    count = lax.axis_size("shard")
    groups = [[o * inner + i for i in range(inner)] for o in range(count // inner)]
    return lax.all_gather(values, "shard", axis=axis, tiled=True, axis_index_groups=groups)


def scatter_inner(values, axis, inner):
    count = lax.axis_size("shard")
    groups = [[o * inner + i for i in range(inner)] for o in range(count // inner)]
    return lax.psum_scatter(
        values, "shard", scatter_dimension=axis, axis_index_groups=groups, tiled=True
    )


def whole_gradients(apack, gup_all, gdn_all):
    tiles = apack[:, :A_ROWS].reshape(4, 5, 96, 128)
    heads = [
        tiles[:, 0:3, :, :64].transpose(2, 0, 1, 3),
        tiles[:, 0:3, :, 64:].transpose(2, 0, 1, 3),
        jnp.stack([tiles[:, 3, :, :64], tiles[:, 3, :, 64:], tiles[:, 4, :, :64]], axis=1).transpose(2, 0, 1, 3),
    ]
    g_in = jnp.stack([head.reshape(96, D) for head in heads])
    g_out = apack[:, A_ROWS:A_ROWS + O_ROWS].reshape(6, 96, 128).transpose(1, 0, 2).reshape(96, D)
    g_small = jnp.sum(apack[:, A_ROWS + O_ROWS:, :96].astype(F32), axis=0)
    g_up = gup_all.reshape(NFFN, 2, 96, 2, 8, 128).transpose(0, 2, 3, 4, 1, 5).reshape(NFFN, 96, 2 * FF)
    g_down = gdn_all.reshape(NFFN, 256, D)
    grads = (g_in, g_out, g_small[:12].T, g_small[12:], g_up, g_down)
    return [grad.astype(F32) for grad in grads]


def local(
    tokens, route_residual, doc_lengths, routes, priority, grad_out,
    attend_in, attend_in_first, attend_in_second,
    attend_out, attend_out_first, attend_out_second,
    expert_up, expert_up_first, expert_up_second,
    expert_down, expert_down_first, expert_down_second,
    router_mix, router_mix_first, router_mix_second,
    vectors, vectors_first, vectors_second,
):
    inner = lax.axis_size("shard") // OUTER
    cosine, sine, turn = rope_constants(STREAM)
    layer_out, grad_tokens, grad_route, apack, gup_all, gdn_all = layer_call(
        inner,
        tokens[0], grad_out[0],
        gather_inner(attend_in, 1, inner), gather_inner(attend_out, 0, inner),
        gather_inner(expert_up, 1, inner), gather_inner(expert_down, 1, inner),
        jnp.asarray(cosine), jnp.asarray(sine), jnp.asarray(turn, BF), doc_lengths,
        routes[0].T, route_residual[0].T, priority,
        gather_inner(router_mix, 0, inner).T, gather_inner(vectors, 1, inner),
    )
    states = (
        (attend_in, attend_in_first, attend_in_second),
        (attend_out, attend_out_first, attend_out_second),
        (router_mix, router_mix_first, router_mix_second),
        (vectors, vectors_first, vectors_second),
        (expert_up, expert_up_first, expert_up_second),
        (expert_down, expert_down_first, expert_down_second),
    )
    if inner == 1:
        turned = [a.T for a in states[2]]
        updated = update_call(apack, gup_all, gdn_all, (states[0], states[1], turned, *states[3:]))
        router = [a.T for a in updated[6:9]]
        results = (*updated[0:6], *updated[12:18], *router, *updated[9:12])
        return (layer_out[None], grad_tokens[None], grad_route[None], *results)

    grads = whole_gradients(apack, gup_all, gdn_all)
    axes = (1, 0, 0, 1, 1, 1)
    rates = [STEP_RATES[k] for k in (0, 1, 4, 5, 2, 3)]
    decays = [STEP_DECAYS[k] for k in (0, 1, 4, 5, 2, 3)]
    updated = [
        adam(weight, scatter_inner(grad, axis, inner), first, second, rate, decay)
        for (weight, first, second), grad, axis, rate, decay in zip(states, grads, axes, rates, decays)
    ]
    results = [a for k in (0, 1, 4, 5, 2, 3) for a in updated[k]]
    return (layer_out[None], grad_tokens[None], grad_route[None], *results)


def solution(mesh):
    token = P("shard", "seq", None)
    middle = P(None, "shard", None)
    front = P("shard", None)
    back = P(None, "shard")
    weights = (middle,) * 3 + (front,) * 3 + (middle,) * 6 + (front,) * 3 + (back,) * 3
    return jax.shard_map(
        local,
        mesh=mesh,
        in_specs=(token, token, front, token, P("shard", "seq"), token) + weights,
        out_specs=(token, token, token) + weights,
        check_vma=False,
    )
```

```python
import functools

import jax
import jax.numpy as jnp
import numpy as np
from jax import lax
from jax.experimental import pallas as pl
from jax.experimental.pallas import tpu as pltpu
from jax.sharding import PartitionSpec as P

D = 768
HEADS = 12
HEAD_DIM = 64
FF = 2048
NFFN = 4
NEXP = 8
TOPK = 2
STEP = 5
CAP = 96
LINE = 4
OUTER = 8
LOCAL_HEADS = 3

NORM_EPSILON = 1e-05
ROPE_BASE = 10000.0
NEGATIVE = -1e30
MOMENT_DECAY = 0.5
ADAM_EPSILON = 1e-08
STEP_RATES = (0.04, 0.1, 0.04, 0.02, 0.02, 0.2)
STEP_DECAYS = (0.1, 0.1, 0.1, 0.1, 0.1, 0.0)
BF = jnp.bfloat16
F32 = jnp.float32
MESH = pl.DeviceIdType.MESH
VMEM_LIMIT = 58 * 2**20


def mm(left, right):
    return jnp.dot(left, right, preferred_element_type=F32)


def mm_nt(left, right):
    return lax.dot_general(left, right, (((1,), (1,)), ((), ())), preferred_element_type=F32)


def mm_tn(left, right):
    return lax.dot_general(left, right, (((0,), (0,)), ((), ())), preferred_element_type=F32)


class Place:
    def __init__(self, inner):
        q = lax.axis_index("seq")
        shard = lax.axis_index("shard")
        self.inner = inner
        self.rest = lax.rem(shard, inner) if inner > 1 else 0
        outer = lax.div(shard, inner) if inner > 1 else shard
        self.q = q
        self.x = lax.div(q, 2)
        self.c = lax.rem(q, 2)
        self.l = lax.div(outer, 2)
        self.y = lax.rem(outer, 2)
        self.own = outer

    def at(self, x=None, c=None, l=None, y=None):
        x = self.x if x is None else x
        c = self.c if c is None else c
        l = self.l if l is None else l
        y = self.y if y is None else y
        return (2 * x + c, (2 * l + y) * self.inner + self.rest)


def greet(devices):
    barrier = pltpu.get_barrier_semaphore()
    for device in devices:
        pl.semaphore_signal(barrier, inc=1, device_id=device, device_id_type=MESH)
    pl.semaphore_wait(barrier, len(devices))


def remote(src, dst, send, recv, device):
    return pltpu.make_async_remote_copy(
        src_ref=src, dst_ref=dst, send_sem=send, recv_sem=recv, device_id=device, device_id_type=MESH
    )


def rope_constants(stream_len):
    frequency = ROPE_BASE ** (-(np.arange(HEAD_DIM // 2, dtype=np.float64) * 2.0 / HEAD_DIM))
    angles = np.arange(stream_len, dtype=np.float64)[:, None] * frequency[None, :]
    cosine = np.tile(np.cos(angles), (1, 4)).astype(np.float32)
    sine = np.tile(np.sin(angles), (1, 4)).astype(np.float32)
    turn = np.zeros((128, 128), np.float32)
    for j in range(128):
        if j % 64 < 32:
            turn[j + 32, j] = -1.0
        else:
            turn[j - 32, j] = 1.0
    return cosine, sine, turn


A_ROWS = 5 * 96
O_ROWS = 144
S_ROWS = 96
PACK = A_ROWS + S_ROWS
PACKG = A_ROWS + O_ROWS + 16
A_PARTS = (slice(0, 192), slice(192, A_ROWS + O_ROWS), slice(A_ROWS + O_ROWS, PACKG))
TOK = 384
STREAM = 1536
ATT = 576
HALF = TOK // 2
BLOCK = 256
KEYS = 512
ROWS = 128


class Counter:
    def __init__(self):
        self.used = 0

    def take(self, count):
        first = self.used
        self.used += count
        return first


def semaphores():
    s, r = Counter(), Counter()
    counts = {
        "tok": (3, 3), "pack": (7, 8), "wo8": (7, 8), "wo": (3, 3), "ex": (8, 18), "over": (8, 0), "last": (2, 0),
        "att": (6, 6), "row": (9, 12), "core": (12, 12), "part": (2, 2), "back": (6, 8), "pair": (8, 8), "line": (8, 10),
        "att2": (3, 3), "wo2": (3, 3), "ay": (12, 12), "al": (9, 12), "gn": (3, 3), "aa": (9, 9), "gp": (12, 16),
    }
    send = {name: s.take(count[0]) for name, count in counts.items()}
    recv = {name: r.take(count[1]) for name, count in counts.items()}
    return send, recv, s.used, r.used


def small_rows(packs):
    tiles = []
    for t in range(6):
        first = A_ROWS + 16 * t
        total = packs[0, first:first + 16, :].astype(F32)
        for s in range(1, OUTER):
            total = total + packs[s, first:first + 16, :].astype(F32)
        tiles.append(total)
    return jnp.concatenate(tiles, axis=1)


def split_low(values):
    high = values.astype(BF)
    return high, (values - high.astype(F32)).astype(BF)


def layer_kernel(
    inner,
    tok, gout_in, w_in, w_out, w_up, w_dn, cos_in, sin_in, turn, lengths, routes, residual, priority, router, vectors,
    layer_out, gtokens, groute, apack, gup_all, gdn_all,
    stream, packs, wo_all, wo, wup, wdn, ringx_up, ringx_dn, gup, gdn, rowh, rowg, part_in, ret, got, wo_in,
    ap_in, ap_line, gn_ret, normed, qk, vo, ks, lse, attended, hidden, cos, sin, gout, bufs, begin,
    cols, facts, gate_out, gate_in, ss, rs, ls, ready,
):
    me = Place(inner)
    x, c, l, y, q, own = me.x, me.c, me.l, me.y, me.q, me.own
    nx, nc, ny = 1 - x, 1 - c, 1 - y
    side = lax.div(l, 2)
    far = 1 - side
    outer = (l == 0) | (l == LINE - 1)
    inside = (l == 1) | (l == 2)
    out, near, far_near, far_out = 3 * side, 1 + side, 2 - side, 3 - 3 * side
    mate = 1 - l + 4 * side
    mine = 2 * side + x
    S, R, _, _ = semaphores()
    chips = [(nx, side), (x, far), (nx, far)]
    others = [(2 * nx + c, me.at(x=nx)), (2 * nx + nc, me.at(x=nx, c=nc)), (2 * x + nc, me.at(c=nc))]

    def load(src, dst, k):
        return pltpu.make_async_copy(src, dst, ls.at[k])

    def tok_copy(k, part, device):
        return remote(stream.at[part], stream.at[part], ss.at[S["tok"] + k], rs.at[R["tok"] + k], device)

    turns = [lax.rem(l + dl, LINE) for dl in range(LINE)]
    shards = [me.at(l=turns[dl]) for dl in (1, 3, 2)] + [me.at(l=turns[dl], y=ny) for dl in (0, 1, 3, 2)]

    def pack_copy(k, z, device):
        slot = 2 * z + y
        return remote(packs.at[slot], packs.at[slot], ss.at[S["pack"] + k], rs.at[R["pack"] + slot], device)

    def pack_wait(slot):
        remote(packs.at[slot], packs.at[slot], ss.at[0], rs.at[R["pack"] + slot], me.at(y=ny)).wait_recv()

    def pack_over(z):
        return pack_copy(3 + z, z, me.at(y=ny))

    def pack_step(step):
        @pl.when(l - step >= 0)
        def _():
            pack_wait(2 * (l - step) + y)
            pack_over(l - step).start()

        @pl.when(l + step < LINE)
        def _():
            pack_wait(2 * (l + step) + y)
            pack_over(l + step).start()

    weights = (wup, wdn)

    def ex_ref(n, z, yy):
        return weights[n].at[2 * z + yy]

    def ex_send(n, k, src, dst, recv, device):
        return remote(src, dst, ss.at[S["ex"] + 2 * k + n], rs.at[R["ex"] + recv], device)

    def ex_recv(n, z, yy):
        ref = ex_ref(n, z, yy)
        remote(ref, ref, ss.at[0], rs.at[R["ex"] + 2 * (2 * z + yy) + n], me.at(y=ny)).wait_recv()

    def ex_line(n, k, z, node, src=None):
        ref = ex_ref(n, z, y)
        return ex_send(n, k, ref if src is None else src, ref, 2 * (2 * z + y) + n, me.at(l=node))

    def ex_through(n, src):
        return ex_send(n, 0, src, ring_extra[n].at[0], 16 + n, me.at(l=near))

    def ex_through_wait(n):
        ref = ring_extra[n].at[0]
        remote(ref, ref, ss.at[0], rs.at[R["ex"] + 16 + n], me.at(l=out)).wait_recv()

    def ex_over(n, z):
        ref = ex_ref(n, z, y)
        return remote(ref, ref, ss.at[S["over"] + 2 * z + n], rs.at[R["ex"] + 2 * (2 * z + y) + n], me.at(y=ny))

    def ex_first(n, other):
        @pl.when(outer)
        def _():
            ex_through(n, other).start()
            ex_line(n, 1, l, near).start()

        @pl.when(inside)
        def _():
            ex_line(n, 0, l, far_near, other).start()
            ex_line(n, 1, l, out).start()

        ex_over(n, l).start()

    def relay(step):
        for n in range(2):
            if step == 1:
                @pl.when(inside)
                def _():
                    ex_through_wait(n)
                    ex_line(n, 2, out, far_near, ring_extra[n].at[0]).start()
                    ex_recv(n, far_near, y)
                    ex_line(n, 3, far_near, out).start()
                    ex_over(n, far_near).start()

                @pl.when(outer)
                def _():
                    ex_recv(n, near, y)
                    ex_over(n, near).start()
            elif step == 2:
                @pl.when(inside)
                def _():
                    ex_recv(n, out, y)
                    ex_over(n, out).start()

                @pl.when(outer)
                def _():
                    ex_recv(n, far_near, y)
                    ex_over(n, far_near).start()
            else:
                @pl.when(inside)
                def _():
                    ex_recv(n, far_out, y)
                    ex_line_last(n).start()
                    ex_over(n, far_out).start()

    def ex_line_last(n):
        ref = ex_ref(n, far_out, y)
        return remote(ref, ref, ss.at[S["last"] + n], rs.at[R["ex"] + 2 * (2 * far_out + y) + n], me.at(l=out))

    def wo_copy(k, part, device):
        rows = pl.ds(pl.multiple_of(part * O_ROWS, O_ROWS), O_ROWS)
        return remote(
            wo_all.at[:, rows, :], wo_all.at[:, rows, :], ss.at[S["wo"] + k], rs.at[R["wo"] + k], device
        )

    row_src = (bufs.at[0], bufs.at[1], gate_out)
    row_dst = (rowh, rowg, gate_in)

    def row_copy(n, k, cx, cy):
        return remote(
            row_src[n].at[2 * cy + cx], row_dst[n].at[4 * c + mine], ss.at[S["row"] + 3 * n + k],
            rs.at[R["row"] + 4 * n + mine], me.at(x=cx, l=l + 2 * (cy - side))
        )

    def row_wait(n, cx, cy):
        row, slot = row_dst[n], 2 * cy + cx
        remote(
            row.at[4 * c + slot], row.at[4 * c + slot], ss.at[0], rs.at[R["row"] + 4 * n + slot],
            me.at(x=cx, l=l + 2 * (cy - side))
        ).wait_recv()

    def core_copy(n, k, first, slot):
        row = row_dst[n]
        return remote(
            row.at[first + slot], row.at[first + slot], ss.at[S["core"] + 4 * n + k], rs.at[R["core"] + 4 * n + slot],
            me.at(c=nc)
        )

    def row_send(n):
        for k, (cx, cy) in enumerate(chips):
            row_copy(n, k, cx, cy).start()
        row_dst[n][4 * c + mine] = row_src[n][mine]
        core_copy(n, 0, 4 * c, mine).start()

    def row_pass(n):
        for k, (cx, cy) in enumerate(chips):
            row_wait(n, cx, cy)
            core_copy(n, 1 + k, 4 * c, 2 * cy + cx).start()

    def row_collect(n):
        for slot in range(4):
            core_copy(n, 0, 4 * nc, slot).wait_recv()

    def back_copy(n, k, cx, cy):
        return remote(
            bufs.at[n, 2 * cy + cx], ret.at[n, mine], ss.at[S["back"] + 3 * n + k], rs.at[R["back"] + 4 * n + mine],
            me.at(x=cx, l=l + 2 * (cy - side))
        )

    def back_wait(n, cx, cy):
        slot = 2 * cy + cx
        remote(
            ret.at[n, slot], ret.at[n, slot], ss.at[0], rs.at[R["back"] + 4 * n + slot], me.at(x=cx, l=l + 2 * (cy - side))
        ).wait_recv()

    loads = [
        load(tok, stream.at[q], 0), load(cos_in, cos, 1), load(sin_in, sin, 2), load(gout_in, gout, 3),
    ]
    for copy in loads:
        copy.start()

    ring_extra = (ringx_up, ringx_dn)

    def forward(st_in, st_out, st_up, st_dn, upx, dnx, wo_tiles, wo_mine, wq, wr, pk, begin_col, maps, slot_lanes):
        from_hbm = [load(w_in, st_in, 4), load(w_out, st_out, 5)]
        experts = [2 * side + x, 2 * far + x]
        from_hbm += [load(w_up.at[e], st_up.at[k], 6 + k) for k, e in enumerate(experts)]
        half_rows = pl.ds(pl.multiple_of(128 * c, 128), 128)
        from_hbm += [load(w_dn.at[e, half_rows, :], st_dn.at[k], 8 + k) for k, e in enumerate(experts)]
        for copy in from_hbm:
            copy.start()
        away = l + 2 * (far - side)
        greet([me.at(c=nc), me.at(x=nx), me.at(x=nx, c=nc), me.at(x=nx, l=away)] + shards)
        loads[0].wait()
        tok_copy(1, q, me.at(x=nx)).start()
        tok_copy(0, q, me.at(c=nc)).start()

        from_hbm[0].wait()
        from_hbm[1].wait()
        for t in range(6):
            wo_tiles[96 * t:96 * (t + 1), :] = st_out[:, 128 * t:128 * (t + 1)].astype(BF)
        for part in range(4):

            @pl.when(q == part)
            def _():
                def head(kind, h):
                    first = 192 * part + 64 * h
                    return st_in[kind, :, first:first + 64]

                tiles = [(head(0, h), head(1, h)) for h in range(LOCAL_HEADS)]
                tiles += [(head(2, 0), head(2, 1)), (head(2, 2), jnp.zeros((96, 64), F32))]
                for t, pair in enumerate(tiles):
                    packs[own, 96 * t:96 * (t + 1), :] = jnp.concatenate(pair, axis=1).astype(BF)

        rows = pl.ds(pl.multiple_of(q * O_ROWS, O_ROWS), O_ROWS)
        wo_mine[...] = wo_tiles[rows, :]
        wo_all[own, rows, :] = wo_tiles[rows, :]
        small = jnp.concatenate([router[...], vectors[...]], axis=0)
        small = jnp.concatenate([small, jnp.zeros((16, 32), F32)], axis=1).astype(BF)
        to_col = lax.broadcasted_iota(jnp.int32, (128, D), 1) - 96 * own
        from_row = lax.broadcasted_iota(jnp.int32, (128, D), 0)
        place = ((to_col == from_row) & (from_row < 96)).astype(F32).astype(BF)
        placed = mm(small, place).astype(BF)
        for t in range(6):
            first = A_ROWS + 16 * t
            packs[own, first:first + 16, :] = placed[:, 128 * t:128 * (t + 1)]
        for k in range(3):
            pack_copy(k, l, shards[k]).start()
        pack_over(l).start()

        for k in range(2):
            from_hbm[4 + k].wait()
        wdn[own] = st_dn[0].astype(BF)
        dnx[...] = st_dn[1].astype(BF)
        for k in range(2):
            from_hbm[2 + k].wait()
        for j in range(16):
            part = pl.ds(pl.multiple_of(256 * j + 128 * c, 128), 128)
            wup[own, :, 128 * j:128 * (j + 1)] = st_up[0, :, part].astype(BF)
            upx[:, 128 * j:128 * (j + 1)] = st_up[1, :, part].astype(BF)

        expert = jnp.concatenate([routes[k:k + 1, :] for k in range(TOPK)], axis=1).astype(F32)
        order = jnp.concatenate([priority[...], priority[...] + STREAM], axis=1).astype(F32)
        base = expert * 4096.0
        rank_key = base + order
        key_rows = jnp.transpose(jnp.broadcast_to(rank_key, (128, 2 * TOK)))[:, 0:1]
        ahead = jnp.where((key_rows < rank_key) & (key_rows >= base), 1.0, 0.0)
        rank = jnp.sum(ahead, axis=0, keepdims=True)
        slot = jnp.where((expert < NFFN) & (rank < CAP), expert * CAP + rank, -1.0)
        slots = [slot[:, :TOK], slot[:, TOK:]]
        slot_row = lax.broadcasted_iota(jnp.int32, (NFFN * CAP, TOK), 0).astype(F32)
        for k in range(TOPK):
            slot_lanes[k:k + 1, :] = slots[k]
            maps[k] = (slot_row == slots[k]).astype(F32).astype(BF)
        loads[3].wait()
        bufs[1] = mm(maps[0] + maps[1], gout[...]).astype(BF).reshape(NFFN, CAP, D)

        pack_step(1)
        pack_step(2)
        tok_copy(1, 2 * nx + c, me.at(x=nx)).wait_recv()
        tok_copy(2, 2 * nx + c, me.at(c=nc)).start()
        pack_step(3)
        def wo_send(k):
            return remote(
                wo_mine, wo_all.at[own, rows, :], ss.at[S["wo8"] + k], rs.at[R["wo8"] + own], shards[k]
            )

        def wo_arrive(k):
            slot = 2 * turns[(1, 3, 2, 0, 1, 3, 2)[k]] + (y if k < 3 else ny)
            remote(
                wo_all.at[slot, rows, :], wo_all.at[slot, rows, :], ss.at[0], rs.at[R["wo8"] + slot], shards[k]
            ).wait_recv()

        for k in range(7):
            wo_send(k).start()
        for n, other in enumerate((upx, dnx)):
            ex_first(n, other)
        row_send(1)

        ids = lax.broadcasted_iota(jnp.int32, (8, STREAM), 1)
        first = lengths[0, 0] * 0
        at = jnp.zeros((8, STREAM), jnp.int32)
        for k in range(8):
            at = jnp.maximum(at, jnp.where(ids >= first, first, 0))
            first = first + lengths[0, k]
        begin[...] = at
        begin_col[...] = jnp.transpose(jnp.broadcast_to(at[0:1].astype(F32), (128, STREAM)))

        for z in range(LINE):
            pack_wait(2 * z + ny)
        for s in range(OUTER):
            for t in range(5):
                wq[t, 96 * s:96 * (s + 1), :] = packs[s, 96 * t:96 * (t + 1), :]
        for t in range(LOCAL_HEADS):
            wr[t] = mm(wq[t], turn[...]).astype(BF)
        gain = small_rows(packs)[12:13]
        tok_copy(0, 2 * x + nc, me.at(c=nc)).wait_recv()
        tok_copy(2, 2 * nx + nc, me.at(c=nc)).wait_recv()
        loads[1].wait()
        loads[2].wait()

        halves = jnp.where(lax.broadcasted_iota(jnp.int32, (1, 128), 1) < 64, 0.125, 1.0)

        @pl.loop(0, 4)
        def _(part):
            values = stream[part].astype(F32)
            scale = lax.rsqrt(jnp.mean(values * values, axis=1, keepdims=True) + NORM_EPSILON)
            rows = pl.ds(pl.multiple_of(part * TOK, TOK), TOK)
            low = (values * scale * gain).astype(BF)
            normed[rows, :] = low
            cosine, sine = cos[rows, :], sin[rows, :]
            for h in range(LOCAL_HEADS):
                turned = mm(low, wq[h]) * cosine + mm(low, wr[h]) * sine
                qk[h, rows, :] = (turned * halves).astype(BF)
            both = mm(low, wq[3]).astype(BF)
            vo[0, rows, 0:64] = both[:, :64]
            vo[1, rows, 0:64] = both[:, 64:]
            vo[2, rows, 0:64] = mm(low, wq[4])[:, :64].astype(BF)

        def one_head(h):
            ks[...] = qk[h, :, 64:128]
            for b in range(STREAM // BLOCK):
                first, last = b * BLOCK, (b + 1) * BLOCK
                scores = mm_nt(qk[h, first:last, 0:64], ks[0:last, :])
                col = lax.broadcasted_iota(jnp.int32, (BLOCK, last), 1)
                row = lax.broadcasted_iota(jnp.int32, (BLOCK, last), 0) + first
                starts = begin_col[first:last, 0:1].astype(jnp.int32)
                scores = jnp.where((col >= starts) & (col <= row), scores, NEGATIVE)
                top = jnp.max(scores, axis=1, keepdims=True)
                weight = jnp.exp(scores - top)
                total = jnp.sum(weight, axis=1, keepdims=True)
                vo[h, first:last, 64:128] = (mm(weight.astype(BF), vo[h, 0:last, 0:64]) / total).astype(BF)
                logs = jnp.broadcast_to(top + jnp.log(total), (BLOCK, 128))
                lse[h, :, first:last] = jnp.transpose(logs)[0:8, :]

        att_rows = (slice(0, TOK), slice(TOK, ATT))

        def att_copy(k, piece, to, frm, device):
            part = att_rows[piece]
            return remote(
                pk.at[to, part, :], got.at[frm, part, :], ss.at[S["att"] + 2 * k + piece],
                rs.at[R["att"] + 2 * k + piece], device
            )

        pl.loop(0, 1)(one_head)
        for k in range(7):
            wo_arrive(k)
        wo_copy(1, q, me.at(x=nx)).start()
        wo_copy(0, q, me.at(c=nc)).start()
        relay(1)
        pl.loop(1, 2)(one_head)
        for part in range(4):
            here = slice(part * TOK, (part + 1) * TOK)
            pk[part, 0:TOK, :] = jnp.concatenate([vo[0, here, 64:128], vo[1, here, 64:128]], axis=1)
        for k, (other, device) in enumerate(others):
            att_copy(k, 0, other, q, device).start()
        pl.loop(2, LOCAL_HEADS)(one_head)
        wo_copy(1, 2 * nx + c, me.at(x=nx)).wait_recv()
        wo_copy(2, 2 * nx + c, me.at(c=nc)).start()
        for part in range(4):
            third = [vo[2, part * TOK + k * HALF:part * TOK + (k + 1) * HALF, 64:128] for k in range(2)]
            pk[part, TOK:ATT, :] = jnp.concatenate(third, axis=1)
        for k, (other, device) in enumerate(others):
            att_copy(k, 1, other, q, device).start()
        got[q] = pk[q]
        relay(2)

        wo_copy(0, 2 * x + nc, me.at(c=nc)).wait_recv()
        wo_copy(2, 2 * nx + nc, me.at(c=nc)).wait_recv()
        for s in range(OUTER):
            for t in range(6):
                wo[96 * s:96 * (s + 1), 128 * t:128 * (t + 1)] = wo_all[s, 96 * t:96 * (t + 1), :]
        row_pass(1)
        for k, (other, device) in enumerate(others):
            for piece in range(2):
                att_copy(k, piece, q, other, device).wait_recv()
        pieces = []
        for part in range(4):
            low = got[part, TOK:ATT, :]
            pieces.append(got[part, 0:TOK, :])
            pieces.append(jnp.concatenate([low[:, :64], low[:, 64:]], axis=0))
        whole = jnp.concatenate(pieces, axis=1)
        attended[...] = whole
        middle = stream[q].astype(F32) + mm(whole, wo[...])
        gtokens[...] = middle

        smalls = small_rows(packs)
        scale = lax.rsqrt(jnp.mean(middle * middle, axis=1, keepdims=True) + NORM_EPSILON)
        low = (middle * scale * smalls[13:14]).astype(BF)
        hidden[...] = low
        logits = mm_nt(smalls.astype(BF), low)
        route_logits = logits[0:8] + residual[...]
        expert_row = lax.broadcasted_iota(jnp.int32, (8, TOK), 0)
        picks = [routes[k:k + 1, :] for k in range(TOPK)]
        picked = [
            jnp.sum(jnp.where(expert_row == pick, route_logits, 0.0), axis=0, keepdims=True) for pick in picks
        ]

        def pair_softmax(first, second):
            top = jnp.maximum(first, second)
            one, two = jnp.exp(first - top), jnp.exp(second - top)
            return [one / (one + two), two / (one + two)]

        gates = pair_softmax(*picked)
        coefs = pair_softmax(logits[8:9], logits[9:10]) + pair_softmax(logits[10:11], logits[11:12])
        slots = [slot_lanes[k:k + 1, :] for k in range(TOPK)]
        lanes = gates + coefs + slots + [pick.astype(F32) for pick in picks]
        lanes = jnp.concatenate(lanes + [jnp.zeros((128 - len(lanes), TOK), F32)], axis=0)
        cols[...] = jnp.transpose(lanes)
        bufs[0] = mm(maps[0] + maps[1], low).astype(BF).reshape(NFFN, CAP, D)
        row_send(0)
        slot_gate = jnp.zeros((NFFN * CAP, 1), F32)
        for k in range(TOPK):
            slot_gate = slot_gate + jnp.sum(maps[k].astype(F32) * gates[k], axis=1, keepdims=True)
        high, rest = split_low(slot_gate)
        lane = lax.broadcasted_iota(jnp.int32, (NFFN * CAP, 128), 1)
        packed = jnp.where(lane == 0, high.astype(F32), jnp.where(lane == 1, rest.astype(F32), 0.0))
        gate_out[...] = packed.astype(BF).reshape(NFFN, CAP, 128)
        row_send(2)

        for n, other in enumerate((upx, dnx)):
            @pl.when(outer)
            def _():
                ex_through(n, other).wait_send()

            @pl.when(inside)
            def _():
                ex_line(n, 0, l, far_near, other).wait_send()

        for k, (other, device) in enumerate(others):
            for piece in range(2):
                att_copy(k, piece, other, q, device).wait_send()
        for k in range(7):
            wo_send(k).wait_send()

    pl.run_scoped(
        forward,
        pltpu.VMEM((3, 96, D), F32),
        pltpu.VMEM((96, D), F32),
        pltpu.VMEM((2, 96, 2 * FF), F32),
        pltpu.VMEM((2, 128, D), F32),
        pltpu.VMEM((96, FF), BF),
        pltpu.VMEM((128, D), BF),
        pltpu.VMEM((576, 128), BF),
        pltpu.VMEM((O_ROWS, 128), BF),
        pltpu.VMEM((5, D, 128), BF),
        pltpu.VMEM((3, D, 128), BF),
        pltpu.VMEM((4, ATT, 128), BF),
        pltpu.VMEM((STREAM, 128), F32),
        pltpu.VMEM((TOPK, NFFN * CAP, TOK), BF),
        pltpu.VMEM((8, TOK), F32),
    )
    relay(3)
    row_pass(0)
    row_pass(2)
    row_collect(1)
    row_collect(0)

    def experts(rowt, total, part_out, act, slope_gate, slope_lin):
        rowt[...] = jnp.transpose(rowh[...].reshape(8 * CAP, D).astype(F32)).astype(BF)
        total[...] = jnp.zeros_like(total)
        for n in range(2):
            @pl.when(outer)
            def _():
                ex_recv(n, far_out, y)
                ex_over(n, far_out).start()

            for z in range(LINE):
                ex_recv(n, z, ny)

        def swap(n):
            return remote(
                part_out.at[n], part_in.at[n], ss.at[S["part"] + n], rs.at[R["part"] + n], me.at(c=nc)
            )

        away = pl.ds(pl.multiple_of(nc * 4 * CAP, 4 * CAP), 4 * CAP)
        here = pl.ds(pl.multiple_of(c * 4 * CAP, 4 * CAP), 4 * CAP)

        def swap_start(n):
            part_out[n] = total[away, :].astype(BF).reshape(4, CAP, D)
            swap(n).start()

        def give_back(n):
            swap(n).wait_recv()
            bufs[n] = (total[here, :].reshape(4, CAP, D) + part_in[n].astype(F32)).astype(BF)
            for k, (cx, cy) in enumerate(chips):
                back_copy(n, k, cx, cy).start()
            ret[n, mine] = bufs[n, mine]

        def columns(j):
            gate_cols = pl.ds(pl.multiple_of(j * 256, 256), 256)
            return gate_cols, pl.ds(pl.multiple_of(1024 + j * 256, 256), 256)

        @pl.loop(0, 4)
        def _(j):
            gate_cols, lin_cols = columns(j)
            rows_h = rowh[...].reshape(8 * CAP, D)
            gate = mm(rows_h, wup[:, :, gate_cols].reshape(D, 256))
            lin = mm(rows_h, wup[:, :, lin_cols].reshape(D, 256))
            sigma = jax.nn.sigmoid(gate)
            silu = gate * sigma
            low = (silu * lin).astype(BF)
            act[:, gate_cols] = low
            slope_gate[:, gate_cols] = (lin * sigma * (1.0 + gate * (1.0 - sigma))).astype(BF)
            slope_lin[:, gate_cols] = silu.astype(BF)
            total[...] += mm(low, wdn[pl.ds(2 * j, 2)].reshape(256, D))

        for n in range(3):
            for k, (cx, cy) in enumerate(chips):
                row_copy(n, k, cx, cy).wait_send()
        swap_start(0)
        row_collect(2)
        for n in range(3):
            core_copy(n, 0, 4 * c, mine).wait_send()
            for k, (cx, cy) in enumerate(chips):
                core_copy(n, 1 + k, 4 * c, 2 * cy + cx).wait_send()
        for slot in range(8):
            gate = gate_in[slot].astype(F32)
            rowg[slot] = ((gate[:, 0:1] + gate[:, 1:2]) * rowg[slot].astype(F32)).astype(BF)
        give_back(0)
        total[...] = jnp.zeros_like(total)

        @pl.loop(0, 4)
        def _(j):
            gate_cols, lin_cols = columns(j)
            rows_g = rowg[...].reshape(8 * CAP, D)
            grad_act = mm_nt(rows_g, wdn[pl.ds(2 * j, 2)].reshape(256, D))
            grad_gate = (grad_act * slope_gate[:, gate_cols].astype(F32)).astype(BF)
            grad_lin = (grad_act * slope_lin[:, gate_cols].astype(F32)).astype(BF)
            total[...] += mm_nt(grad_gate, wup[:, :, gate_cols].reshape(D, 256))
            total[...] += mm_nt(grad_lin, wup[:, :, lin_cols].reshape(D, 256))
            gdn[pl.ds(2 * j, 2)] = mm_tn(act[:, gate_cols], rows_g).astype(BF).reshape(2, 128, D)
            gup[:, :, gate_cols] = mm(rowt[...], grad_gate).astype(BF).reshape(8, 96, 256)
            gup[:, :, lin_cols] = mm(rowt[...], grad_lin).astype(BF).reshape(8, 96, 256)

        swap_start(1)
        for n in range(2):
            @pl.when(outer)
            def _():
                ex_line(n, 1, l, near).wait_send()

            @pl.when(inside)
            def _():
                ex_line(n, 1, l, out).wait_send()
                ex_line(n, 2, out, far_near, ring_extra[n].at[0]).wait_send()
                ex_line(n, 3, far_near, out).wait_send()
                ex_line_last(n).wait_send()

            for z in range(LINE):
                ex_over(n, z).wait_send()

        @pl.when(l < LINE - 1)
        def _():
            pl.semaphore_signal(ready.at[0], inc=1, device_id=me.at(l=l + 1), device_id_type=MESH)

        @pl.when(l > 0)
        def _():
            pl.semaphore_signal(ready.at[1], inc=1, device_id=me.at(l=l - 1), device_id_type=MESH)

        pl.semaphore_signal(ready.at[2], inc=1, device_id=me.at(y=ny), device_id_type=MESH)

        @pl.when(outer)
        def _():
            pl.semaphore_signal(ready.at[3], inc=1, device_id=me.at(l=far_near), device_id_type=MESH)


        give_back(1)
        for n in range(2):
            swap(n).wait_send()

    pl.run_scoped(
        experts,
        pltpu.VMEM((D, 8 * CAP), BF),
        pltpu.VMEM((8 * CAP, D), F32),
        pltpu.VMEM((2, 4, CAP, D), BF),
        pltpu.VMEM((8 * CAP, 1024), BF),
        pltpu.VMEM((8 * CAP, 1024), BF),
        pltpu.VMEM((8 * CAP, 1024), BF),
    )

    grads = (gup, gdn)

    def room(n, i):
        return weights[n].at[i] if isinstance(i, jax.Array) or i < 8 else ring_extra[n].at[0]

    pieces = [far_out, far_near, mate, l]

    def pair_copy(n, j):
        z = pieces[j]
        return remote(
            grads[n].at[2 * z + ny], weights[n].at[z], ss.at[S["pair"] + 2 * j + n], rs.at[R["pair"] + 2 * j + n],
            me.at(y=ny)
        )

    def line_copy(n, k, src, to, node):
        return remote(
            src, room(n, to), ss.at[S["line"] + 2 * k + n], rs.at[R["line"] + 2 * (to - 4) + n], me.at(l=node)
        )

    def line_wait(n, to):
        remote(room(n, to), room(n, to), ss.at[0], rs.at[R["line"] + 2 * (to - 4) + n], me.at(y=ny)).wait_recv()

    def add(n, into, other):
        rows = grads[n].shape[1]

        @pl.loop(0, rows // 16)
        def _(r):
            part = pl.ds(pl.multiple_of(r * 16, 16), 16)
            into[part, :] = (into[part, :].astype(F32) + other[part, :].astype(F32)).astype(BF)

    def pair_end(n, j):
        pair_copy(n, j).wait_recv()
        add(n, weights[n].at[pieces[j]], grads[n].at[2 * pieces[j] + y])

    def line_step(j):
        for n in range(2):
            pair_end(n, j)
            if j == 2:
                line_copy(n, 2, weights[n].at[mate], 8, mate).start()
                continue

            @pl.when(outer)
            def _():
                line_copy(n, j, weights[n].at[pieces[j]], 4 + j, near).start()

    def line_cross(j):
        for n in range(2):
            @pl.when(inside)
            def _():
                if j == 0 and n == 0:
                    pl.semaphore_wait(ready.at[3], 1)
                line_wait(n, 4 + j)
                add(n, weights[n].at[4 + j], weights[n].at[pieces[j]])
                line_copy(n, j, weights[n].at[4 + j], 7, (far_out, far_near)[j]).start()

    @pl.when(l < LINE - 1)
    def _():
        pl.semaphore_wait(ready.at[1], 1)

    @pl.when(l > 0)
    def _():
        pl.semaphore_wait(ready.at[0], 1)

    pl.semaphore_wait(ready.at[2], 1)
    def pair_start(j):
        for n in range(2):
            pair_copy(n, j).start()

    pair_start(0)
    pair_start(1)

    for n in range(2):
        for cx, cy in chips:
            back_wait(n, cx, cy)
    smalls = small_rows(packs)
    down_rows = ret[0].reshape(NFFN * CAP, D)
    back_rows = ret[1].reshape(NFFN * CAP, D)
    vector = [smalls[14 + j:15 + j] for j in range(2)]
    router_row = lax.broadcasted_iota(jnp.int32, (16, 1), 0)
    router_low = jnp.where(router_row < 12, smalls, 0.0)
    router_low = jnp.concatenate([router_low, jnp.zeros((112, D), F32)], axis=0).astype(BF)
    facts[...] = jnp.zeros_like(facts)

    @pl.loop(0, TOK // ROWS)
    def _(i):
        rows = pl.ds(pl.multiple_of(i * ROWS, ROWS), ROWS)
        middle = gtokens[rows, :]
        low = hidden[rows, :]
        grad_low = gout[rows, :]
        info = cols[rows, :]
        token_lane = lax.broadcasted_iota(jnp.int32, (ROWS, NFFN * CAP), 1).astype(F32)
        gates = [info[:, k:k + 1] for k in range(TOPK)]
        coefs = [[info[:, 2 + 2 * j:3 + 2 * j], info[:, 3 + 2 * j:4 + 2 * j]] for j in range(2)]
        spread = [(token_lane == info[:, 6 + k:7 + k]).astype(F32).astype(BF) for k in range(TOPK)]
        picks = [info[:, 8 + k:9 + k] for k in range(TOPK)]
        chosen = [[(pick == e).astype(F32) for e in (5.0, 6.0, 7.0)] for pick in picks]
        grad_top = grad_low.astype(F32)
        value_hidden = low.astype(F32)
        grad_gate, mixture = [], middle
        for k in range(TOPK):
            copy, one, two = chosen[k]
            value = mm(spread[k], down_rows)
            value = value + (copy + one * coefs[0][0] + two * coefs[1][0]) * value_hidden
            value = value + (one * coefs[0][1]) * vector[0] + (two * coefs[1][1]) * vector[1]
            mixture = mixture + gates[k] * value
            grad_gate.append(jnp.sum(grad_top * value, axis=1, keepdims=True))
        layer_out[rows, :] = mixture.astype(BF)
        mean_gate = gates[0] * grad_gate[0] + gates[1] * grad_gate[1]
        grad_pick = [gates[k] * (grad_gate[k] - mean_gate) for k in range(TOPK)]
        lane = lax.broadcasted_iota(jnp.int32, (ROWS, 128), 1).astype(F32)
        grad_logits = sum(jnp.where(lane == picks[k], grad_pick[k], 0.0) for k in range(TOPK))
        groute[rows, :] = grad_logits[:, :NEXP]
        on_hidden = jnp.sum(grad_top * value_hidden, axis=1, keepdims=True)
        direct = gates[0] * chosen[0][0] + gates[1] * chosen[1][0]
        on_vectors = jnp.zeros((ROWS, 128), F32)
        for j in range(2):
            weight = gates[0] * chosen[0][1 + j] + gates[1] * chosen[1][1 + j]
            direct = direct + weight * coefs[j][0]
            grad_coef = [weight * on_hidden, weight * jnp.sum(grad_top * vector[j], axis=1, keepdims=True)]
            mean_coef = coefs[j][0] * grad_coef[0] + coefs[j][1] * grad_coef[1]
            for n in range(2):
                grad_logits = grad_logits + jnp.where(
                    lane == 8.0 + 2 * j + n, coefs[j][n] * (grad_coef[n] - mean_coef), 0.0
                )
            on_vectors = on_vectors + jnp.where(lane == 14.0 + j, weight * coefs[j][1], 0.0)
        logit_parts = split_low(grad_logits)
        vector_parts = split_low(on_vectors)
        grad_hidden = direct * grad_top + mm(spread[0] + spread[1], back_rows)
        grad_hidden = grad_hidden + mm(logit_parts[0], router_low) + mm(logit_parts[1], router_low)
        small_sum = mm_tn(logit_parts[0], low) + mm_tn(logit_parts[1], low)
        small_sum = small_sum + mm_tn(vector_parts[0], grad_low) + mm_tn(vector_parts[1], grad_low)
        scale = lax.rsqrt(jnp.mean(middle * middle, axis=1, keepdims=True) + NORM_EPSILON)
        normal = middle * scale
        gain_sum = jnp.sum(grad_hidden * normal, axis=0, keepdims=True)
        facts[...] += small_sum[0:16] + jnp.where(router_row == 13, gain_sum, 0.0)
        inner_term = grad_hidden * smalls[13:14]
        gtokens[rows, :] = grad_top + scale * (
            inner_term - normal * jnp.mean(inner_term * normal, axis=1, keepdims=True)
        )

    def al_copy(p, k):
        z, rows = turns[(1, 3, 2)[k]], A_PARTS[p]
        return remote(
            ap_in.at[z, rows, :], ap_line.at[l, rows, :], ss.at[S["al"] + 3 * p + k], rs.at[R["al"] + 4 * p + l], shards[k]
        )

    def backward(pk, kt, grad, dq, dv, dk_sum, dv_sum, delta, gr, wall, ap):
        line_step(0)
        pair_start(2)
        grad_att = mm_nt(gtokens[...].astype(BF), wo[...])
        for part in range(4):
            wide = grad_att[:, 192 * part:192 * (part + 1)]
            pk[part, 0:TOK, :] = wide[:, :128].astype(BF)
            third = wide[:, 128:]
            pk[part, TOK:ATT, :] = jnp.concatenate([third[:HALF], third[HALF:]], axis=1).astype(BF)
        got[q] = pk[q]

        def att_copy(k, to, frm, device):
            return remote(pk.at[to], got.at[frm], ss.at[S["att2"] + k], rs.at[R["att2"] + k], device)

        for k, (other, device) in enumerate(others):
            att_copy(k, other, q, device).start()

        wo_copy(1, q, me.at(x=nx)).wait_send()
        wo_copy(0, q, me.at(c=nc)).wait_send()
        wo_copy(2, 2 * nx + c, me.at(c=nc)).wait_send()

        @pl.loop(0, 2)
        def _(i):
            wide = pl.ds(pl.multiple_of(i * 384, 384), 384)
            grad_wo = mm_tn(attended[:, wide], gtokens[...].astype(BF)).astype(BF)
            for s in range(4):
                for t in range(6):
                    tile = grad_wo[96 * s:96 * (s + 1), 128 * t:128 * (t + 1)]
                    wo_all[4 * i + s, 96 * t:96 * (t + 1), :] = tile

        def wo_rows(part):
            return pl.ds(pl.multiple_of(part * O_ROWS, O_ROWS), O_ROWS)

        def wo_share(k, to, device):
            return remote(
                wo_all.at[:, wo_rows(to), :], wo_in.at[k], ss.at[S["wo2"] + k], rs.at[R["wo2"] + k], device
            )

        for s in range(OUTER):
            for t in range(5):
                wall[96 * s:96 * (s + 1), 128 * t:128 * (t + 1)] = packs[s, 96 * t:96 * (t + 1), :]

        for k, (other, device) in enumerate(others):
            att_copy(k, q, other, device).wait_recv()
        for k, (other, device) in enumerate(others):
            wo_share(k, other, device).start()
        for part in range(4):
            rows = slice(part * TOK, (part + 1) * TOK)
            both = got[part, 0:TOK, :]
            third = got[part, TOK:ATT, :]
            grad[0, rows, :] = both[:, :64]
            grad[1, rows, :] = both[:, 64:]
            grad[2, rows, :] = jnp.concatenate([third[:, :64], third[:, 64:]], axis=0)
        for h in range(LOCAL_HEADS):
            dots = jnp.sum(grad[h].astype(F32) * vo[h, :, 64:128].astype(F32), axis=1, keepdims=True)
            delta[h] = jnp.transpose(jnp.broadcast_to(dots, (STREAM, 128)))[0:8, :]

        def one_head(h):
            ks[...] = qk[h, :, 64:128]
            kt[...] = jnp.transpose(ks[...].astype(F32)).astype(BF)
            dk_sum[...] = jnp.zeros((STREAM, 64), F32)
            dv_sum[...] = jnp.zeros((STREAM, 64), F32)
            for b in range(STREAM // BLOCK):
                first, last = b * BLOCK, (b + 1) * BLOCK
                q_rows, g_rows = qk[h, first:last, 0:64], grad[h, first:last, :]
                grad_q = jnp.zeros((64, BLOCK), F32)
                for start in range(0, last, KEYS):
                    keys = slice(start, min(start + KEYS, last))
                    size = keys.stop - start
                    scores = mm_nt(ks[keys, :], q_rows)
                    key = lax.broadcasted_iota(jnp.int32, (size, BLOCK), 0) + start
                    col = lax.broadcasted_iota(jnp.int32, (size, BLOCK), 1) + first
                    seen = (key >= begin[0:1, first:last]) & (key <= col)
                    probs = jnp.exp(jnp.where(seen, scores, NEGATIVE) - lse[h, 0:1, first:last])
                    grad_probs = mm_nt(vo[h, keys, 0:64], g_rows)
                    grad_scores = (probs * (grad_probs - delta[h, 0:1, first:last])).astype(BF)
                    dv_sum[keys, :] += mm(probs.astype(BF), g_rows)
                    dk_sum[keys, :] += mm(grad_scores, q_rows)
                    grad_q = grad_q + mm(kt[:, keys], grad_scores)
                dq[first:last, :] = (jnp.transpose(grad_q) * 0.125).astype(BF)
            dv[h] = dv_sum[...].astype(BF)
            for part in range(4):
                rows = slice(part * TOK, (part + 1) * TOK)
                turned = jnp.concatenate([dq[rows, :], dk_sum[rows, :].astype(BF)], axis=1)
                raw = turned.astype(F32) * cos[rows, :] - mm(turned, turn[...]) * sin[rows, :]
                gr[rows, pl.ds(pl.multiple_of(h * 128, 128), 128)] = raw.astype(BF)

        def grad_tiles(first, last):
            @pl.loop(0, 2)
            def _(i):
                wide = pl.ds(pl.multiple_of(i * 384, 384), 384)
                grad_a = mm_tn(normed[:, wide], gr[:, 128 * first:128 * last]).astype(BF)
                for s in range(4):
                    for t in range(first, last):
                        tile = grad_a[96 * s:96 * (s + 1), 128 * (t - first):128 * (t - first + 1)]
                        ap[4 * i + s, 96 * t:96 * (t + 1), :] = tile

        def ay_copy(p, z):
            rows = A_PARTS[p]
            return remote(
                ap.at[2 * z + ny, rows, :], ap_in.at[z, rows, :], ss.at[S["ay"] + 4 * p + z],
                rs.at[R["ay"] + 4 * p + z], me.at(y=ny)
            )

        def ay_start(p):
            for z in range(LINE):
                ay_copy(p, z).start()

        def ay_end(p):
            rows = A_PARTS[p]
            for z in range(LINE):
                ay_copy(p, z).wait_recv()
                ap_in[z, rows, :] = (ap[2 * z + y, rows, :].astype(F32) + ap_in[z, rows, :].astype(F32)).astype(BF)
            for k in range(3):
                al_copy(p, k).start()

        line_step(1)
        pl.loop(0, 1)(one_head)
        line_cross(0)
        pl.loop(1, 2)(one_head)
        grad_tiles(0, 2)
        ay_start(0)
        pair_start(3)
        line_cross(1)
        pl.loop(2, LOCAL_HEADS)(one_head)
        for part in range(4):
            rows = slice(part * TOK, (part + 1) * TOK)
            gr[rows, 384:512] = jnp.concatenate([dv[0, rows, :], dv[1, rows, :]], axis=1)
            gr[rows, 512:640] = jnp.concatenate([dv[2, rows, :], jnp.zeros((TOK, 64), BF)], axis=1)

        line_step(2)
        grad_tiles(2, 5)
        for k, (other, device) in enumerate(others):
            wo_share(k, q, device).wait_recv()
        wo_total = wo_all[:, wo_rows(q), :].astype(F32)
        for k in range(3):
            wo_total = wo_total + wo_in[k].astype(F32)
        ap[:, A_ROWS:A_ROWS + O_ROWS, :] = wo_total.astype(BF)
        ay_start(1)

        for n in range(2):
            for k, (cx, cy) in enumerate(chips):
                back_copy(n, k, cx, cy).wait_send()
        gain_sum = jnp.zeros((1, D), F32)
        for part in range(4):
            rows = slice(part * TOK, (part + 1) * TOK)
            grad_n = mm_nt(gr[rows, :], wall[...])
            values = stream[part].astype(F32)
            scale = lax.rsqrt(jnp.mean(values * values, axis=1, keepdims=True) + NORM_EPSILON)
            gain_sum = gain_sum + jnp.sum(grad_n * (values * scale), axis=0, keepdims=True)
            first = 4 * (part % 2)
            (rowh, rowg)[part // 2][first:first + 4] = grad_n.astype(BF).reshape(4, CAP, D)

        def gn_swap(a):
            row = (rowh, rowg)[a]
            return remote(
                row.at[pl.ds(4 * nc, 4)], part_in.at[a], ss.at[S["gn"] + a], rs.at[R["gn"] + a], me.at(c=nc)
            )

        for a in range(2):
            gn_swap(a).start()
        small_all = facts[...] + jnp.where(router_row == 12, gain_sum, 0.0)
        for s in range(OUTER):
            piece = jnp.concatenate([small_all[:, 96 * s:96 * (s + 1)], jnp.zeros((16, 32), F32)], axis=1)
            ap[s, A_ROWS + O_ROWS:PACKG, :] = piece.astype(BF)

        ay_start(2)
        ay_end(0)
        for a in range(2):
            gn_swap(a).wait_recv()
            bufs[a] = ((rowh, rowg)[a][pl.ds(4 * c, 4)].astype(F32) + part_in[a].astype(F32)).astype(BF)
        gn_over = remote(bufs.at[nx], gn_ret, ss.at[S["gn"] + 2], rs.at[R["gn"] + 2], me.at(x=nx))
        gn_over.start()
        ay_end(1)
        ay_end(2)
        for k, (other, device) in enumerate(others):
            att_copy(k, other, q, device).wait_send()
            wo_share(k, other, device).wait_send()
        for a in range(2):
            gn_swap(a).wait_send()
        for p in range(3):
            for z in range(LINE):
                ay_copy(p, z).wait_send()

    heads = (LOCAL_HEADS, STREAM, 64)
    pl.run_scoped(
        backward,
        pltpu.VMEM((4, ATT, 128), BF),
        pltpu.VMEM((64, STREAM), BF),
        pltpu.VMEM(heads, BF),
        pltpu.VMEM((STREAM, 64), BF),
        pltpu.VMEM(heads, BF),
        pltpu.VMEM((STREAM, 64), F32),
        pltpu.VMEM((STREAM, 64), F32),
        pltpu.VMEM((LOCAL_HEADS, 8, STREAM), F32),
        pltpu.VMEM((STREAM, 640), BF),
        pltpu.VMEM((D, 640), BF),
        pltpu.VMEM((OUTER, PACKG, 128), BF),
    )

    def aa_copy(p, k, part, device):
        rows = A_PARTS[p]
        return remote(
            apack.at[part, rows, :], apack.at[part, rows, :], ss.at[S["aa"] + 3 * p + k], rs.at[R["aa"] + 3 * p + k], device
        )

    def al_end(p):
        rows = A_PARTS[p]
        total = ap_in[l, rows, :].astype(F32)
        for k in range(3):
            z = turns[(1, 3, 2)[k]]
            ref = ap_line.at[z, rows, :]
            remote(ref, ref, ss.at[0], rs.at[R["al"] + 4 * p + z], shards[k]).wait_recv()
            total = total + ap_line[z, rows, :].astype(F32)
        apack[q, rows, :] = total.astype(BF)
        for k, (other, device) in enumerate(others):
            aa_copy(p, k, q, device).start()

    spread_out = (gup_all, gdn_all)

    def gp_slot(k, cx, cc):
        return 2 * (2 * (side if k == 0 else far) + cx) + cc

    def gp_src(n, k):
        return ring_extra[n].at[0] if k == 0 else weights[n].at[7]

    def gp_over(n, k):
        slot = gp_slot(k, x, c)
        return remote(
            gp_src(n, k), spread_out[n].at[slot], ss.at[S["gp"] + 6 * n + k], rs.at[R["gp"] + 8 * n + slot], me.at(x=nx)
        )

    def gp_wait(n, slot):
        ref = spread_out[n].at[slot]
        remote(ref, ref, ss.at[0], rs.at[R["gp"] + 8 * n + slot], me.at(c=nc)).wait_recv()

    def gp_own(n, k):
        return pltpu.make_async_copy(gp_src(n, k), spread_out[n].at[gp_slot(k, x, c)], ls.at[10 + 2 * n + k])

    def gp_core(n, k):
        slot = gp_slot(k, x, c)
        return remote(
            gp_src(n, k), spread_out[n].at[slot], ss.at[S["gp"] + 6 * n + 2 + k], rs.at[R["gp"] + 8 * n + slot],
            me.at(c=nc)
        )

    def gp_pass(n, k):
        slot = gp_slot(k, nx, c)
        ref = spread_out[n].at[slot]
        return remote(ref, ref, ss.at[S["gp"] + 6 * n + 4 + k], rs.at[R["gp"] + 8 * n + slot], me.at(c=nc))

    def gp_start(n, k):
        gp_over(n, k).start()
        gp_own(n, k).start()
        gp_core(n, k).start()

    def line_other():
        for n in range(2):
            line_wait(n, 7)
            gp_start(n, 1)

    def line_own():
        for n in range(2):
            pair_end(n, 3)
            line_wait(n, 8)
            add(n, ring_extra[n].at[0], weights[n].at[l])
            gp_start(n, 0)

    al_end(0)

    gn_over = remote(bufs.at[nx], gn_ret, ss.at[S["gn"] + 2], rs.at[R["gn"] + 2], me.at(x=nx))
    gn_over.wait_recv()
    values = stream[q].astype(F32)
    scale = lax.rsqrt(jnp.mean(values * values, axis=1, keepdims=True) + NORM_EPSILON)
    normal = values * scale
    grad_n = (bufs[x].astype(F32) + gn_ret[...].astype(F32)).reshape(TOK, D)
    inner_term = grad_n * small_rows(packs)[12:13]
    gtokens[...] = gtokens[...] + scale * (
        inner_term - normal * jnp.mean(inner_term * normal, axis=1, keepdims=True)
    )

    line_other()
    line_own()
    al_end(1)
    al_end(2)

    for k in (1, 0):
        for n in range(2):
            gp_wait(n, gp_slot(k, nx, c))
            gp_pass(n, k).start()
    for k in range(2):
        for n in range(2):
            gp_wait(n, gp_slot(k, x, nc))
            gp_wait(n, gp_slot(k, nx, nc))
    for p in range(3):
        for k, (other, device) in enumerate(others):
            aa_copy(p, k, other, device).wait_recv()

    tok_copy(1, q, me.at(x=nx)).wait_send()
    tok_copy(0, q, me.at(c=nc)).wait_send()
    tok_copy(2, 2 * nx + c, me.at(c=nc)).wait_send()
    gn_over.wait_send()
    for p in range(3):
        for k, (other, device) in enumerate(others):
            aa_copy(p, k, q, device).wait_send()
            al_copy(p, k).wait_send()
    for n in range(2):
        for k in range(2):
            gp_over(n, k).wait_send()
            gp_core(n, k).wait_send()
            gp_pass(n, k).wait_send()
            gp_own(n, k).wait()
        for j in range(4):
            pair_copy(n, j).wait_send()
        line_copy(n, 2, weights[n].at[mate], 8, mate).wait_send()

        @pl.when(outer)
        def _():
            for j in range(2):
                line_copy(n, j, weights[n].at[pieces[j]], 4 + j, near).wait_send()

        @pl.when(inside)
        def _():
            for j in range(2):
                line_copy(n, j, weights[n].at[4 + j], 7, (far_out, far_near)[j]).wait_send()

    for k in range(3):
        pack_copy(k, l, shards[k]).wait_send()
    for z in range(LINE):
        pack_over(z).wait_send()


def layer_call(inner, *args):
    vm = pl.BlockSpec(memory_space=pltpu.VMEM)
    hbm = pl.BlockSpec(memory_space=pl.ANY)
    smem = pl.BlockSpec(memory_space=pltpu.SMEM)
    heads = (LOCAL_HEADS, STREAM, 64)
    wide = (LOCAL_HEADS, STREAM, 128)
    _, _, sends, recvs = semaphores()
    scratch = [
        ((4, TOK, D), BF), ((OUTER, PACK, 128), BF), ((OUTER, 576, 128), BF), ((D, D), BF),
        ((OUTER, 96, FF), BF), ((OUTER, 128, D), BF), ((1, 96, FF), BF), ((1, 128, D), BF),
        ((OUTER, 96, FF), BF), ((OUTER, 128, D), BF),
        ((8, CAP, D), BF), ((8, CAP, D), BF), ((2, 4, CAP, D), BF), ((2, 4, CAP, D), BF),
        ((4, ATT, 128), BF), ((3, OUTER, O_ROWS, 128), BF),
        ((LINE, PACKG, 128), BF), ((LINE, PACKG, 128), BF), ((4, CAP, D), BF),
        ((STREAM, D), BF), (wide, BF), (wide, BF), ((STREAM, 64), BF), ((LOCAL_HEADS, 8, STREAM), F32),
        ((TOK, D), BF), ((TOK, D), BF), ((STREAM, 128), F32), ((STREAM, 128), F32), ((TOK, D), BF),
        ((2, 4, CAP, D), BF), ((8, STREAM), jnp.int32), ((TOK, 128), F32), ((16, D), F32),
        ((4, CAP, 128), BF), ((8, CAP, 128), BF),
    ]
    return pl.pallas_call(
        functools.partial(layer_kernel, inner),
        out_shape=[
            jax.ShapeDtypeStruct((TOK, D), BF),
            jax.ShapeDtypeStruct((TOK, D), F32),
            jax.ShapeDtypeStruct((TOK, NEXP), F32),
            jax.ShapeDtypeStruct((4, PACKG, 128), BF),
            jax.ShapeDtypeStruct((8, 96, FF), BF),
            jax.ShapeDtypeStruct((8, 128, D), BF),
        ],
        in_specs=[hbm] * 8 + [vm, smem] + [vm] * 5,
        out_specs=[vm] * 4 + [hbm] * 2,
        scratch_shapes=[pltpu.VMEM(s, t) for s, t in scratch]
        + [
            pltpu.SemaphoreType.DMA((sends,)),
            pltpu.SemaphoreType.DMA((recvs,)),
            pltpu.SemaphoreType.DMA((14,)),
            pltpu.SemaphoreType.REGULAR((4,)),
        ],
        compiler_params=pltpu.CompilerParams(
            collective_id=0, has_side_effects=True, vmem_limit_bytes=VMEM_LIMIT
        ),
        name="layer",
    )(*args)


def adam(weight, grad, first, second, rate, decay):
    first_new = MOMENT_DECAY * first + (1.0 - MOMENT_DECAY) * grad
    second_new = MOMENT_DECAY * second + (1.0 - MOMENT_DECAY) * grad * grad
    scale = 1.0 / (1.0 - MOMENT_DECAY**STEP)
    update = (first_new * scale) / (jnp.sqrt(second_new * scale) + ADAM_EPSILON)
    return weight - rate * (update + decay * weight), first_new, second_new


UP_PARTS = 2


def update_kernel(
    apack, gu, gd,
    in_w, in_m, in_v, out_w, out_m, out_v, rt_w, rt_m, rt_v, vec_w, vec_m, vec_v,
    up_w, up_m, up_v, dn_w, dn_m, dn_v,
    in_w2, in_m2, in_v2, out_w2, out_m2, out_v2, rt_w2, rt_m2, rt_v2, vec_w2, vec_m2, vec_v2,
    up_w2, up_m2, up_v2, dn_w2, dn_m2, dn_v2,
):
    step = pl.program_id(0)

    for j in range(16):
        cols, part = slice(256 * j, 256 * (j + 1)), slice(128 * j, 128 * (j + 1))
        grad = jnp.concatenate([gu[0, :, part], gu[1, :, part]], axis=1).astype(F32)
        new = adam(up_w[0, :, cols], grad, up_m[0, :, cols], up_v[0, :, cols], STEP_RATES[2], STEP_DECAYS[2])
        up_w2[0, :, cols], up_m2[0, :, cols], up_v2[0, :, cols] = new
    for half in range(2):
        rows = slice(128 * half, 128 * (half + 1))
        grad = gd[half].astype(F32)
        new = adam(dn_w[0, rows, :], grad, dn_m[0, rows, :], dn_v[0, rows, :], STEP_RATES[3], STEP_DECAYS[3])
        dn_w2[0, rows, :], dn_m2[0, rows, :], dn_v2[0, rows, :] = new

    @pl.when(step == 0)
    def _():
        tiles = [[apack[p, 96 * t:96 * (t + 1), :].astype(F32) for t in range(5)] for p in range(4)]
        for kind in range(3):
            pieces = []
            for p in range(4):
                if kind < 2:
                    pieces += [tiles[p][h][:, 64 * kind:64 * kind + 64] for h in range(LOCAL_HEADS)]
                else:
                    pieces += [tiles[p][3][:, :64], tiles[p][3][:, 64:], tiles[p][4][:, :64]]
            grad = jnp.concatenate(pieces, axis=1)
            new = adam(in_w[kind], grad, in_m[kind], in_v[kind], STEP_RATES[0], STEP_DECAYS[0])
            in_w2[kind], in_m2[kind], in_v2[kind] = new
        rows = jnp.concatenate([apack[p, A_ROWS:A_ROWS + O_ROWS, :] for p in range(4)], axis=0)
        for t in range(6):
            cols = slice(128 * t, 128 * (t + 1))
            grad = rows[96 * t:96 * (t + 1), :].astype(F32)
            new = adam(out_w[:, cols], grad, out_m[:, cols], out_v[:, cols], STEP_RATES[1], STEP_DECAYS[1])
            out_w2[:, cols], out_m2[:, cols], out_v2[:, cols] = new
        small = jnp.zeros((16, 128), F32)
        for p in range(4):
            small = small + apack[p, A_ROWS + O_ROWS:A_ROWS + O_ROWS + 16, :].astype(F32)
        new = adam(vec_w[...], small[12:, :96], vec_m[...], vec_v[...], STEP_RATES[5], STEP_DECAYS[5])
        vec_w2[...], vec_m2[...], vec_v2[...] = new
        new = adam(rt_w[...], small[:12, :96], rt_m[...], rt_v[...], STEP_RATES[4], STEP_DECAYS[4])
        rt_w2[...], rt_m2[...], rt_v2[...] = new


def update_call(apack, gu, gd, states):
    flat = [a for group in states for a in group]

    def whole(a):
        return pl.BlockSpec(a.shape, lambda e: (0,) * a.ndim)

    def by_expert(a):
        return pl.BlockSpec((1,) + a.shape[1:], lambda e: (e, 0, 0))

    specs = [whole(a) for a in flat[:12]] + [by_expert(a) for a in flat[12:]]
    pairs = [pl.BlockSpec((2,) + a.shape[1:], lambda e: (e, 0, 0)) for a in (gu, gd)]
    return pl.pallas_call(
        update_kernel,
        grid=(NFFN,),
        out_shape=[jax.ShapeDtypeStruct(a.shape, a.dtype) for a in flat],
        in_specs=[whole(apack)] + pairs + specs,
        out_specs=specs,
        compiler_params=pltpu.CompilerParams(vmem_limit_bytes=56 * 2**20),
        name="update",
    )(apack, gu, gd, *flat)


def gather_inner(values, axis, inner):
    if inner == 1:
        return values
    count = lax.axis_size("shard")
    groups = [[o * inner + i for i in range(inner)] for o in range(count // inner)]
    return lax.all_gather(values, "shard", axis=axis, tiled=True, axis_index_groups=groups)


def scatter_inner(values, axis, inner):
    count = lax.axis_size("shard")
    groups = [[o * inner + i for i in range(inner)] for o in range(count // inner)]
    return lax.psum_scatter(
        values, "shard", scatter_dimension=axis, axis_index_groups=groups, tiled=True
    )


def whole_gradients(apack, gup_all, gdn_all):
    tiles = apack[:, :A_ROWS].reshape(4, 5, 96, 128)
    heads = [
        tiles[:, 0:3, :, :64].transpose(2, 0, 1, 3),
        tiles[:, 0:3, :, 64:].transpose(2, 0, 1, 3),
        jnp.stack([tiles[:, 3, :, :64], tiles[:, 3, :, 64:], tiles[:, 4, :, :64]], axis=1).transpose(2, 0, 1, 3),
    ]
    g_in = jnp.stack([head.reshape(96, D) for head in heads])
    g_out = apack[:, A_ROWS:A_ROWS + O_ROWS].reshape(6, 96, 128).transpose(1, 0, 2).reshape(96, D)
    g_small = jnp.sum(apack[:, A_ROWS + O_ROWS:, :96].astype(F32), axis=0)
    g_up = gup_all.reshape(NFFN, 2, 96, 2, 8, 128).transpose(0, 2, 3, 4, 1, 5).reshape(NFFN, 96, 2 * FF)
    g_down = gdn_all.reshape(NFFN, 256, D)
    grads = (g_in, g_out, g_small[:12].T, g_small[12:], g_up, g_down)
    return [grad.astype(F32) for grad in grads]


def local(
    tokens, route_residual, doc_lengths, routes, priority, grad_out,
    attend_in, attend_in_first, attend_in_second,
    attend_out, attend_out_first, attend_out_second,
    expert_up, expert_up_first, expert_up_second,
    expert_down, expert_down_first, expert_down_second,
    router_mix, router_mix_first, router_mix_second,
    vectors, vectors_first, vectors_second,
):
    inner = lax.axis_size("shard") // OUTER
    cosine, sine, turn = rope_constants(STREAM)
    layer_out, grad_tokens, grad_route, apack, gup_all, gdn_all = layer_call(
        inner,
        tokens[0], grad_out[0],
        gather_inner(attend_in, 1, inner), gather_inner(attend_out, 0, inner),
        gather_inner(expert_up, 1, inner), gather_inner(expert_down, 1, inner),
        jnp.asarray(cosine), jnp.asarray(sine), jnp.asarray(turn, BF), doc_lengths,
        routes[0].T, route_residual[0].T, priority,
        gather_inner(router_mix, 0, inner).T, gather_inner(vectors, 1, inner),
    )
    states = (
        (attend_in, attend_in_first, attend_in_second),
        (attend_out, attend_out_first, attend_out_second),
        (router_mix, router_mix_first, router_mix_second),
        (vectors, vectors_first, vectors_second),
        (expert_up, expert_up_first, expert_up_second),
        (expert_down, expert_down_first, expert_down_second),
    )
    if inner == 1:
        turned = [a.T for a in states[2]]
        updated = update_call(apack, gup_all, gdn_all, (states[0], states[1], turned, *states[3:]))
        router = [a.T for a in updated[6:9]]
        results = (*updated[0:6], *updated[12:18], *router, *updated[9:12])
        return (layer_out[None], grad_tokens[None], grad_route[None], *results)

    grads = whole_gradients(apack, gup_all, gdn_all)
    axes = (1, 0, 0, 1, 1, 1)
    rates = [STEP_RATES[k] for k in (0, 1, 4, 5, 2, 3)]
    decays = [STEP_DECAYS[k] for k in (0, 1, 4, 5, 2, 3)]
    updated = [
        adam(weight, scatter_inner(grad, axis, inner), first, second, rate, decay)
        for (weight, first, second), grad, axis, rate, decay in zip(states, grads, axes, rates, decays)
    ]
    results = [a for k in (0, 1, 4, 5, 2, 3) for a in updated[k]]
    return (layer_out[None], grad_tokens[None], grad_route[None], *results)


def solution(mesh):
    token = P("shard", "seq", None)
    middle = P(None, "shard", None)
    front = P("shard", None)
    back = P(None, "shard")
    weights = (middle,) * 3 + (front,) * 3 + (middle,) * 6 + (front,) * 3 + (back,) * 3
    return jax.shard_map(
        local,
        mesh=mesh,
        in_specs=(token, token, front, token, P("shard", "seq"), token) + weights,
        out_specs=(token, token, token) + weights,
        check_vma=False,
    )
```
